32 devices in a mesh: grp: 8 (over z, core), ep: 4 (over y, x).
Axes of the slice: x: 2, y: 2, z: 4, core: 2. Of those that a mesh axis runs over, the one named last changes fastest.
Arguments:
- queries: bfloat16 [128, 64, 576], P(('grp', 'ep')), may hold values from -75 to 75
- cache: bfloat16 [128, 256, 576], P(('grp', 'ep')), may hold values from -6 to 6
- lengths: int32 [128], P(('grp', 'ep')), may hold values from 2 to 256, as said below
- live_rows: int32 [32], P(('grp', 'ep')), may hold values from 1 to 4, as said below
- tokens: bfloat16 [512, 3584], P(('grp', 'ep')), may hold values from -6 to 6
- ids: int32 [512, 8], P(('grp', 'ep')), may hold values from 0 to 15, all different within a row; in each aligned block of 16 rows (0 to 15, 16 to 31, ...) at most 16 rows name the same one
- gates: float32 [512, 8], P(('grp', 'ep')), may hold values from 0.1 to 1
- w_gate: bfloat16 [32, 3584, 512], P(('grp', 'ep')), may hold values from -0.09375 to 0.09375
- w_up: bfloat16 [32, 3584, 512], P(('grp', 'ep')), may hold values from -0.09375 to 0.09375
- w_down: bfloat16 [32, 512, 3584], P(('grp', 'ep')), may hold values from -0.1875 to 0.1875
Outputs:
- context: bfloat16 [128, 64, 512], P(('grp', 'ep'))
- mixed: bfloat16 [512, 3584], P(('grp', 'ep'))
The draws below stay inside these ranges and needn't reach their ends.
Inputs may be any that keep to these rules, and one draw needn't show every extreme that they name: `ids`: each row names 8 different experts; among the rows of one device no expert is named more than 16 times. `lengths`: the first request slot of every device holds 256 positions. `live_rows`: a device's live request slots are its first ones; on a quarter of the grp indices every device holds 2 or fewer, elsewhere exactly 4.
All inputs are finite; a program needn't handle non-finite values.
Results may differ from the reference program's by a relative error of at most 0.012.
Values may be sent and summed in bfloat16 or wider, within the bound.
No kernel may reach another device: no remote copies, remote signals or barrier semaphores. Data moves between devices by JAX's collectives and lax.ppermute only.
A program may use at most 128 MiB of HBM per device.

```python
import math
import jax
import jax.numpy as jnp
import numpy as np
from jax import lax

D = 3584
HID = 1024
HALF = 512
TOPK = 8
EXPERTS = 16
H = 64
LAT = 512
ROPE = 64
CACHE = 256
RA = 4
ROWS = 16
CAP = 16
REQS = 128
TOKENS = 512
N_GRP = 8
N_EP = 4


def draw_queries(key, part):
    base = jnp.clip(jax.random.normal(jax.random.fold_in(key, 1), (REQS, H, LAT + ROPE), jnp.float32), -6.0, 6.0)
    return base.astype(jnp.bfloat16)


def draw_cache(key, part):
    base = jnp.clip(jax.random.normal(jax.random.fold_in(key, 2), (REQS, CACHE, LAT + ROPE), jnp.float32), -6.0, 6.0)
    return base.astype(jnp.bfloat16)


def draw_lengths(key, part):
    drawn = jax.random.randint(jax.random.fold_in(key, 3), (REQS,), 2, CACHE + 1)
    request = jnp.arange(REQS)
    return jnp.where(request % RA == 0, CACHE, drawn).astype(jnp.int32)


def draw_live_rows(key, part):
    device_count = N_GRP * N_EP
    group = jnp.arange(device_count) // N_EP
    order = jax.random.permutation(jax.random.fold_in(key, 4), N_GRP)
    capped = order[group] < N_GRP // 4
    lowered = jax.random.randint(jax.random.fold_in(key, 5), (device_count,), 1, RA // 2 + 1)
    return jnp.where(capped, lowered, RA).astype(jnp.int32)


def level_of(rng, dims, cuts, smallest, largest):
    gain = 1.0
    for axis_at, blocks in cuts:
        steps = jax.random.uniform(jax.random.fold_in(jax.random.fold_in(rng, 6), axis_at), (blocks,), jnp.float32, smallest / len(cuts), largest / len(cuts))
        gain = gain * jnp.repeat(jnp.exp(steps), dims[axis_at] // blocks).reshape((-1,) + (1,) * (len(dims) - 1 - axis_at))
    return gain


def deal_out(rng, own, number, rows, count, top, bound, skew):
    sequence = jax.random.permutation(rng, count)
    crowded, common = shares(count, rows * top, bound, skew, True), shares(count, rows * top, bound, skew, False)
    places = jnp.arange(count)

    def named(sizes, turn):
        used = int((sizes > 0).sum())
        fixed = max(1, used // 4)
        passed = fixed + (places - fixed + turn * (used - fixed)) % max(1, count - fixed)
        return jnp.zeros((count,), jnp.int32).at[sequence[jnp.where(places < fixed, places, passed)]].set(jnp.asarray(sizes, jnp.int32))

    sizes = jnp.where(number % 4 == 0, named(crowded, number // 4), named(common, number - number // 4 - 1))
    mixed = jax.random.permutation(jax.random.fold_in(own, 3), count)
    donor, sink = mixed[0:count // 2 * 2:2], mixed[1:count // 2 * 2:2]
    slack = jnp.minimum(sizes[donor] - 1, bound - sizes[sink]) // 2
    slack = jnp.where((donor == sequence[0]) | (sink == sequence[0]) | (sizes[sink] == 0), 0, jnp.maximum(slack, 0))
    passed = jax.random.randint(jax.random.fold_in(own, 4), (count // 2,), 0, 1 << 20) % (slack + 1)
    sizes = sizes.at[donor].add(-passed).at[sink].add(passed)
    items = jnp.searchsorted(jnp.cumsum(sizes), jnp.arange(rows * top), side="right").astype(jnp.int32)
    grid = items.reshape(top, rows).T
    grid = grid[jax.random.permutation(jax.random.fold_in(own, 1), rows)]
    turn = jax.random.randint(jax.random.fold_in(own, 2), (rows, 1), 0, top)
    return jnp.take_along_axis(grid, (jnp.arange(top)[None, :] + turn) % top, axis=1)


def shares(amount, total, most, lean, full):
    portions = [(1 << 20) // math.isqrt(rank ** lean) + 1 for rank in range(1, amount + 1)]
    largest = most if full else min(most, max(-(-total // amount), total * portions[0] // sum(portions)))
    least = 1 if total - largest >= amount - 1 else 0
    counts, surplus = [largest] + [least] * (amount - 1), total - largest - least * (amount - 1)
    while surplus > 0:
        candidates = [i for i in range(1, amount) if counts[i] < largest] or [i for i in range(1, amount) if counts[i] < most]
        whole, budget = sum([portions[i] for i in candidates]), surplus
        for i in candidates:
            extra = min(most - counts[i], max(1, budget * portions[i] // whole), surplus)
            counts[i] = counts[i] + extra
            surplus = surplus - extra
    return np.array(counts)


def bell_draw(key, dims, scale, reach, shards=(), kind=jnp.bfloat16):
    level = level_of(key, dims, shards, -0.22, 0.18) if shards else 1.0
    result = jax.random.normal(key, dims, jnp.float32) * scale * level
    return jnp.minimum(jnp.maximum(result, -reach), reach).astype(kind)


def setup_inputs(seed: int = 0) -> dict:
    keys = jax.random.split(jax.random.key(seed), 11)
    queries = draw_queries(jax.random.fold_in(keys[10], 71), 0)
    cache = draw_cache(jax.random.fold_in(keys[10], 71), 0)
    lengths = draw_lengths(jax.random.fold_in(keys[10], 71), 0)
    live_rows = draw_live_rows(jax.random.fold_in(keys[10], 71), 0)
    tokens = bell_draw(keys[4], (TOKENS, D), 1.0, 6.0, ((0, 32),))
    ids_keys = jax.random.split(jax.random.fold_in(keys[5], 1), TOKENS // ROWS)
    ids_turns = jax.random.permutation(jax.random.fold_in(keys[5], 3), TOKENS // ROWS)
    ids = jax.vmap(lambda own, number: deal_out(jax.random.fold_in(keys[5], 2), own, number, ROWS, EXPERTS, TOPK, CAP, 2))(ids_keys, ids_turns).reshape((TOKENS, TOPK))
    gates = jnp.clip(0.1 + 0.9 * jax.random.uniform(keys[6], (TOKENS, TOPK), jnp.float32) ** level_of(keys[6], (TOKENS, TOPK), ((0, 32),), -0.2, 0.2), 0.1, 1.0)
    w_gate = bell_draw(keys[7], (2 * EXPERTS, D, HALF), D ** -0.5, 0.09375, ((0, 32),))
    w_up = bell_draw(keys[8], (2 * EXPERTS, D, HALF), D ** -0.5, 0.09375, ((0, 32),))
    w_down = bell_draw(keys[9], (2 * EXPERTS, HALF, D), HID ** -0.5, 0.1875, ((0, 32),))
    return {"queries": queries, "cache": cache, "lengths": lengths, "live_rows": live_rows, "tokens": tokens, "ids": ids, "gates": gates, "w_gate": w_gate, "w_up": w_up, "w_down": w_down}


score_scale = 192.0 ** -0.5
neg_large = -1.0e30


def attend(queries, cache, lengths, live_mask):
    scores = jnp.einsum('rhc,rlc->rhl', queries.astype(jnp.float32), cache.astype(jnp.float32)) * score_scale
    positions = lax.broadcasted_iota(jnp.int32, scores.shape, 2)
    inside = positions < lengths[:, None, None]
    masked = jnp.where(inside, scores, neg_large)
    highest = jnp.max(masked, axis=2, keepdims=True)
    powers = jnp.where(inside, jnp.exp(masked - highest), 0.0)
    totals = jnp.sum(powers, axis=2, keepdims=True)
    weights = (powers / totals).astype(jnp.bfloat16)
    context = jnp.einsum('rhl,rlc->rhc', weights.astype(jnp.float32), cache[:, :, :LAT].astype(jnp.float32)).astype(jnp.bfloat16)
    return jnp.where(live_mask[:, None, None], context, jnp.zeros_like(context))


def reference(queries, cache, lengths, live_rows, tokens, ids, gates, w_gate, w_up, w_down):
    request_index = jnp.arange(REQS, dtype=jnp.int32)
    live_mask = (request_index % RA) < live_rows[request_index // RA]
    context = attend(queries, cache, lengths, live_mask)

    device_count = N_GRP * N_EP
    expert_count = EXPERTS
    chosen_ids = ids.reshape(device_count, ROWS * TOPK)
    onehot = (chosen_ids[:, :, None] == jnp.arange(expert_count, dtype=jnp.int32)[None, None, :]).astype(jnp.int32)
    earlier = jnp.cumsum(onehot, axis=1) - onehot
    slot_only = jnp.sum(earlier * onehot, axis=2)
    device_index = jnp.arange(device_count, dtype=jnp.int32)[:, None]
    slot_index = device_index * CAP + slot_only
    source_row = device_index * ROWS + (jnp.arange(ROWS * TOPK, dtype=jnp.int32) // TOPK)[None, :]
    table = jnp.full((expert_count, device_count * CAP), TOKENS, jnp.int32)
    table = table.at[chosen_ids, slot_index].set(source_row)
    padded = jnp.concatenate([tokens, jnp.zeros((1, D), tokens.dtype)], axis=0)
    gate_pairs = w_gate.reshape(expert_count, 2, D, HALF)
    up_pairs = w_up.reshape(expert_count, 2, D, HALF)
    down_pairs = w_down.reshape(expert_count, 2, HALF, D)

    def serve(item):
        table_row, gate_half, up_half, down_half = item
        gathered = padded[table_row]
        summed = jnp.zeros((gathered.shape[0], D), jnp.float32)
        for which_half in range(2):
            gate_part = jnp.dot(gathered, gate_half[which_half], preferred_element_type=jnp.float32)
            up_part = jnp.dot(gathered, up_half[which_half], preferred_element_type=jnp.float32)
            hidden = (jax.nn.silu(gate_part) * up_part).astype(jnp.bfloat16)
            summed = summed + jnp.dot(hidden, down_half[which_half], preferred_element_type=jnp.float32)
        return summed.astype(jnp.bfloat16)

    answers = lax.map(serve, (table, gate_pairs, up_pairs, down_pairs))
    picked = answers[chosen_ids, slot_index].reshape(TOKENS, TOPK, D)
    summed = jnp.zeros((TOKENS, D), jnp.float32)
    for which_pick in range(TOPK):
        summed = summed + gates[:, which_pick:which_pick + 1] * picked[:, which_pick, :].astype(jnp.float32)
    mixed = summed.astype(jnp.bfloat16)
    return (context, mixed)
```

```python
import jax
import jax.numpy as jnp
from jax import lax
from jax.sharding import PartitionSpec as P

LAT = 512
AXES = ("grp", "ep")

score_scale = 192.0 ** (-0.5)
neg_large = -1e30


def attend(queries, cache, lengths, live_count):
    scores = (
        jnp.einsum("rhc,rlc->rhl", queries, cache, preferred_element_type=jnp.float32) * score_scale
    )
    positions = lax.broadcasted_iota(jnp.int32, scores.shape, 2)
    inside = positions < lengths[:, None, None]
    masked = jnp.where(inside, scores, neg_large)
    highest = jnp.max(masked, axis=2, keepdims=True)
    powers = jnp.where(inside, jnp.exp(masked - highest), 0.0)
    totals = jnp.sum(powers, axis=2, keepdims=True)
    weights = (powers / totals).astype(jnp.bfloat16)
    context = jnp.einsum(
        "rhl,rlc->rhc", weights, cache[:, :, :LAT], preferred_element_type=jnp.float32
    ).astype(jnp.bfloat16)
    request_slot = lax.broadcasted_iota(jnp.int32, context.shape, 0)
    return jnp.where(request_slot < live_count, context, jnp.zeros_like(context))


def per_device(queries, cache, lengths, live_rows, tokens, ids, gates, w_gate, w_up, w_down):
    me = lax.axis_index("grp") * lax.axis_size("ep") + lax.axis_index("ep")
    expert = me // 2
    all_tokens = lax.all_gather(tokens, AXES, axis=0, tiled=True)
    all_ids = lax.all_gather(ids, AXES, axis=0, tiled=True)
    all_gates = lax.all_gather(gates, AXES, axis=0, tiled=True)
    context = attend(queries, cache, lengths, live_rows[0])
    share = jnp.sum(jnp.where(all_ids == expert, all_gates, 0.0), axis=1, keepdims=True)
    gate_part = jnp.dot(all_tokens, w_gate[0], preferred_element_type=jnp.float32)
    up_part = jnp.dot(all_tokens, w_up[0], preferred_element_type=jnp.float32)
    hidden = (jax.nn.silu(gate_part) * up_part).astype(jnp.bfloat16)
    partial_out = jnp.dot(hidden, w_down[0], preferred_element_type=jnp.float32)
    weighted = (partial_out * share).astype(jnp.bfloat16)
    mixed = lax.psum_scatter(weighted, AXES, scatter_dimension=0, tiled=True)
    return (context, mixed)


def solution(mesh):
    rows3 = P(AXES, None, None)
    rows2 = P(AXES, None)
    rows1 = P(AXES)
    return jax.shard_map(
        per_device,
        mesh=mesh,
        in_specs=(rows3, rows3, rows1, rows1, rows2, rows2, rows2, rows3, rows3, rows3),
        out_specs=(rows3, rows2),
        check_vma=False,
    )
```

```python
import jax
import jax.numpy as jnp
from jax import lax
from jax.sharding import PartitionSpec as P

LAT = 512
AXES = ("grp", "ep")

score_scale = 192.0 ** (-0.5)
neg_large = -1e30


def attend(queries, cache, lengths, live_count):
    scores = (
        jnp.einsum("rhc,rlc->rhl", queries, cache, preferred_element_type=jnp.float32) * score_scale
    )
    positions = lax.broadcasted_iota(jnp.int32, scores.shape, 2)
    inside = positions < lengths[:, None, None]
    masked = jnp.where(inside, scores, neg_large)
    highest = jnp.max(masked, axis=2, keepdims=True)
    powers = jnp.where(inside, jnp.exp(masked - highest), 0.0)
    totals = jnp.sum(powers, axis=2, keepdims=True)
    weights = (powers / totals).astype(jnp.bfloat16)
    context = jnp.einsum(
        "rhl,rlc->rhc", weights, cache[:, :, :LAT], preferred_element_type=jnp.float32
    ).astype(jnp.bfloat16)
    request_slot = lax.broadcasted_iota(jnp.int32, context.shape, 0)
    return jnp.where(request_slot < live_count, context, jnp.zeros_like(context))


def bits_of(count):
    return [1 << i for i in range(count.bit_length() - 1)]


def swap(value, step):
    axis, bit = step
    size = lax.axis_size(axis)
    return lax.ppermute(value, axis, [(i, i ^ bit) for i in range(size)])


def spread(value, steps):
    for step in steps:
        value = jnp.concatenate([value, swap(value, step)], axis=0)
    return value


def fold(value, steps):
    for step in reversed(steps):
        half = value.shape[0] // 2
        arrived = swap(value[half:], step)
        value = (value[:half].astype(jnp.float32) + arrived.astype(jnp.float32)).astype(
            jnp.bfloat16
        )
    return value


def pack(tokens, ids, gates):
    high = lax.reduce_precision(gates, 8, 7)
    low = gates - high
    extra = jnp.concatenate([ids.astype(jnp.float32), high, low], axis=1)
    extra = jnp.pad(extra, ((0, 0), (0, 128 - extra.shape[1]))).astype(jnp.bfloat16)
    return jnp.concatenate([tokens, extra], axis=1)


def per_device(queries, cache, lengths, live_rows, tokens, ids, gates, w_gate, w_up, w_down):
    feature = tokens.shape[1]
    picks = ids.shape[1]
    grp_bits = bits_of(lax.axis_size("grp"))
    ep_bits = bits_of(lax.axis_size("ep"))
    core = ("grp", 1)
    z_steps = [("grp", bit) for bit in reversed(grp_bits[1:])]
    x_steps = [("ep", bit) for bit in ep_bits[: len(ep_bits) // 2]]
    y_steps = [("ep", bit) for bit in ep_bits[len(ep_bits) // 2 :]]
    expert = (lax.axis_index("grp") * lax.axis_size("ep") + lax.axis_index("ep")) // 2

    def share_of(extra):
        extra = extra.astype(jnp.float32)
        named = extra[:, :picks] == expert.astype(jnp.float32)
        value = extra[:, picks : 2 * picks] + extra[:, 2 * picks : 3 * picks]
        return jnp.sum(jnp.where(named, value, 0.0), axis=1, keepdims=True)

    def order_rows(value, steps, wanted):
        row_count = value.shape[0] >> len(steps)
        cube = value.reshape((2,) * len(steps) + (row_count, value.shape[1]))
        axes = [len(steps) - 1 - steps.index(step) for step in reversed(wanted)]
        cube = cube.transpose(axes + [len(steps), len(steps) + 1])
        return cube.reshape(value.shape)

    packed = pack(tokens, ids, gates)
    near = spread(packed, z_steps)
    half_width = feature // 2
    first = spread(near[:, :half_width], x_steps + y_steps)
    second = spread(near[:, half_width:], y_steps + x_steps)
    second = order_rows(second, z_steps + y_steps + x_steps, z_steps + x_steps + y_steps)
    own = jnp.concatenate([first, second], axis=1)
    other = swap(own, core)

    context = attend(queries, cache, lengths, live_rows[0])

    def hidden_of(rows):
        gate_part = jnp.dot(rows[:, :feature], w_gate[0], preferred_element_type=jnp.float32)
        up_part = jnp.dot(rows[:, :feature], w_up[0], preferred_element_type=jnp.float32)
        return (jax.nn.silu(gate_part) * up_part).astype(jnp.bfloat16)

    def partial_of(rows, hidden):
        product = jnp.dot(hidden, w_down[0], preferred_element_type=jnp.float32)
        return product * share_of(rows[:, feature:])

    own_hidden = hidden_of(own)
    other_hidden = hidden_of(other)
    arrived = swap(partial_of(other, other_hidden).astype(jnp.bfloat16), core)
    summed = (partial_of(own, own_hidden) + arrived.astype(jnp.float32)).astype(jnp.bfloat16)
    first = fold(summed[:, :half_width], x_steps + y_steps)
    second = order_rows(
        summed[:, half_width:], z_steps + x_steps + y_steps, z_steps + y_steps + x_steps
    )
    second = fold(second, y_steps + x_steps)
    mixed = fold(jnp.concatenate([first, second], axis=1), z_steps)
    return (context, mixed)


def solution(mesh):
    rows3 = P(AXES, None, None)
    rows2 = P(AXES, None)
    rows1 = P(AXES)
    return jax.shard_map(
        per_device,
        mesh=mesh,
        in_specs=(rows3, rows3, rows1, rows1, rows2, rows2, rows2, rows3, rows3, rows3),
        out_specs=(rows3, rows2),
        check_vma=False,
    )
```

```python
import functools

import jax
import jax.numpy as jnp
from jax import lax
from jax.experimental import pallas as pl
from jax.experimental.pallas import tpu as pltpu
from jax.sharding import PartitionSpec as P

LAT = 512
AXES = ("grp", "ep")
EXTRA = 128
BLOCKS = 4
VMEM_BYTES = 48 * 1024 * 1024

score_scale = 192.0 ** (-0.5)
neg_large = -1e30


def attend(queries, cache, lengths, live_count):
    scores = (
        jnp.einsum("rhc,rlc->rhl", queries, cache, preferred_element_type=jnp.float32) * score_scale
    )
    positions = lax.broadcasted_iota(jnp.int32, scores.shape, 2)
    inside = positions < lengths[:, None, None]
    masked = jnp.where(inside, scores, neg_large)
    highest = jnp.max(masked, axis=2, keepdims=True)
    powers = jnp.where(inside, jnp.exp(masked - highest), 0.0)
    totals = jnp.sum(powers, axis=2, keepdims=True)
    weights = (powers / totals).astype(jnp.bfloat16)
    context = jnp.einsum(
        "rhl,rlc->rhc", weights, cache[:, :, :LAT], preferred_element_type=jnp.float32
    ).astype(jnp.bfloat16)
    request_slot = lax.broadcasted_iota(jnp.int32, context.shape, 0)
    return jnp.where(request_slot < live_count, context, jnp.zeros_like(context))


def bits_of(count):
    return [1 << i for i in range(count.bit_length() - 1)]


def swap(value, step):
    axis, bit = step
    size = lax.axis_size(axis)
    return lax.ppermute(value, axis, [(i, i ^ bit) for i in range(size)])


def spread(value, steps):
    for step in steps:
        value = jnp.concatenate([value, swap(value, step)], axis=0)
    return value


def others(value, steps):
    if len(steps) == 1:
        return swap(value, steps[0])
    return spread(value, steps)[value.shape[0] :]


def give_back(rest, steps, rows):
    terms = []
    for step in reversed(steps):
        keep = (rest.shape[0] + rows) // 2 - rows
        arrived = swap(rest[keep:], step)
        terms.append(arrived[:rows])
        if keep:
            rest = add_up(rest[:keep], [arrived[rows:]])
    return terms


def add_up(own, terms):
    total = own.astype(jnp.float32)
    for term in terms:
        total = total + term.astype(jnp.float32)
    return total.astype(jnp.bfloat16)


def pack_kernel(tokens, ids, gates, out):
    feature = tokens.shape[1]
    high = gates[...].astype(jnp.bfloat16)
    low = (gates[...] - high.astype(jnp.float32)).astype(jnp.bfloat16)
    named = ids[...].astype(jnp.float32).astype(jnp.bfloat16)
    stacked = jnp.concatenate(
        [named.astype(jnp.float32), high.astype(jnp.float32), low.astype(jnp.float32)], axis=0
    ).astype(jnp.bfloat16)
    row = lax.broadcasted_iota(jnp.int32, (stacked.shape[0], EXTRA), 0)
    column = lax.broadcasted_iota(jnp.int32, (stacked.shape[0], EXTRA), 1)
    place = jnp.where(row == column, 1.0, 0.0).astype(jnp.bfloat16)
    extra = lax.dot_general(
        stacked, place, (((0,), (0,)), ((), ())), preferred_element_type=jnp.float32
    )
    out[:, :feature] = tokens[...]
    out[:, feature:] = extra.astype(jnp.bfloat16)


def pack(tokens, ids, gates):
    return pl.pallas_call(
        pack_kernel,
        out_shape=jax.ShapeDtypeStruct((tokens.shape[0], tokens.shape[1] + EXTRA), jnp.bfloat16),
        in_specs=[pl.BlockSpec(memory_space=pltpu.VMEM)] * 3,
        out_specs=pl.BlockSpec(memory_space=pltpu.VMEM),
        name="pack",
    )(tokens, ids.T, gates.T)


def hidden_kernel(picks, expert, own, other, extra_own, extra_other, w_gate, w_up, h_own, h_other, gate_sum, up_sum):
    step = pl.program_id(0)
    rows = jnp.concatenate([own[...], other[...]], axis=0)
    gate_part = jnp.dot(rows, w_gate[0], preferred_element_type=jnp.float32)
    up_part = jnp.dot(rows, w_up[0], preferred_element_type=jnp.float32)

    @pl.when(step == 0)
    def _():
        gate_sum[...] = gate_part
        up_sum[...] = up_part

    @pl.when(step > 0)
    def _():
        gate_sum[...] += gate_part
        up_sum[...] += up_part

    @pl.when(step == pl.num_programs(0) - 1)
    def _():
        count = own.shape[0]
        wanted = expert[0].astype(jnp.float32)
        for extra, out, at in ((extra_own, h_own, 0), (extra_other, h_other, count)):
            columns = extra[...].astype(jnp.float32)
            value = columns[:, picks : 2 * picks] + columns[:, 2 * picks : 3 * picks]
            share = jnp.sum(
                jnp.where(columns[:, :picks] == wanted, value, 0.0), axis=1, keepdims=True
            )
            gate_all = gate_sum[at : at + count, :]
            up_all = up_sum[at : at + count, :]
            hidden = gate_all / (1.0 + jnp.exp(-gate_all)) * up_all
            out[...] = (hidden * share).astype(jnp.bfloat16)


def hidden_of(expert, own, other, w_gate, w_up, picks):
    count, width = own.shape
    _, feature, half = w_gate.shape
    depth = feature // BLOCKS
    rows_spec = pl.BlockSpec((count, depth), lambda k: (0, k))
    extra_spec = pl.BlockSpec((count, EXTRA), lambda k: (0, feature // EXTRA))
    weight_spec = pl.BlockSpec((1, depth, half), lambda k: (0, k, 0))
    out_spec = pl.BlockSpec((count, half), lambda k: (0, 0))
    return pl.pallas_call(
        functools.partial(hidden_kernel, picks),
        grid=(BLOCKS,),
        out_shape=[jax.ShapeDtypeStruct((count, half), jnp.bfloat16)] * 2,
        in_specs=[pl.BlockSpec(memory_space=pltpu.SMEM), rows_spec, rows_spec, extra_spec, extra_spec]
        + [weight_spec] * 2,
        out_specs=[out_spec] * 2,
        scratch_shapes=[pltpu.VMEM((2 * count, half), jnp.float32)] * 2,
        compiler_params=pltpu.CompilerParams(vmem_limit_bytes=VMEM_BYTES),
        cost_estimate=pl.CostEstimate(
            flops=8 * count * feature * half,
            bytes_accessed=4 * feature * half + 4 * count * width,
            transcendentals=2 * count * half,
        ),
        name="hidden",
    )(expert, own, other, own, other, w_gate, w_up)


def down_kernel(cuts, hidden, w_down, *refs):
    part = jnp.dot(hidden[...], w_down[0], preferred_element_type=jnp.float32)
    if len(refs) > len(cuts):
        part = part + refs[0][...].astype(jnp.float32)
        refs = refs[1:]
    at = 0
    for cut, out in zip(cuts, refs):
        out[...] = part[at : at + cut, :].astype(jnp.bfloat16)
        at += cut


def down_of(hidden, w_down, cuts, arrived=None):
    count, half = hidden.shape
    feature = w_down.shape[2]
    wide = feature // BLOCKS
    operands = [hidden, w_down]
    in_specs = [
        pl.BlockSpec((count, half), lambda n: (0, 0)),
        pl.BlockSpec((1, half, wide), lambda n: (0, 0, n)),
    ]
    if arrived is not None:
        operands.append(arrived)
        in_specs.append(pl.BlockSpec((count, wide), lambda n: (0, n)))
    return pl.pallas_call(
        functools.partial(down_kernel, cuts),
        grid=(BLOCKS,),
        out_shape=[jax.ShapeDtypeStruct((cut, feature), jnp.bfloat16) for cut in cuts],
        in_specs=in_specs,
        out_specs=[pl.BlockSpec((cut, wide), lambda n: (0, n)) for cut in cuts],
        compiler_params=pltpu.CompilerParams(vmem_limit_bytes=VMEM_BYTES),
        cost_estimate=pl.CostEstimate(
            flops=2 * count * feature * half,
            bytes_accessed=2 * feature * half + 4 * count * feature,
            transcendentals=0,
        ),
        name="down",
    )(*operands)


def per_device(queries, cache, lengths, live_rows, tokens, ids, gates, w_gate, w_up, w_down):
    picks = ids.shape[1]
    grp_bits = bits_of(lax.axis_size("grp"))
    ep_bits = bits_of(lax.axis_size("ep"))
    core = ("grp", 1)
    z_near = [("grp", bit) for bit in reversed(grp_bits[1:-1])]
    z_far = ("grp", grp_bits[-1])
    x_steps = [("ep", bit) for bit in ep_bits[: len(ep_bits) // 2]]
    y_steps = [("ep", bit) for bit in ep_bits[len(ep_bits) // 2 :]]
    expert = ((lax.axis_index("grp") * lax.axis_size("ep") + lax.axis_index("ep")) >> 1).reshape(1)

    packed = pack(tokens, ids, gates)
    near = spread(packed, z_near)
    far = spread(swap(packed, z_far), z_near)
    near_x, near_y = others(near, x_steps), others(near, y_steps)
    far_x, far_y = others(far, x_steps), others(far, y_steps)
    near_xy, far_xy = others(near_x, y_steps), others(far_y, x_steps)
    early = [near, near_x, near_y, far, far_x, far_y]
    late = [near_xy, far_xy]
    early_cuts = [group.shape[0] for group in early]
    late_cuts = [group.shape[0] for group in late]
    early_own = jnp.concatenate(early, axis=0)
    late_own = jnp.concatenate(late, axis=0)
    early_other = swap(early_own, core)
    late_other = swap(late_own, core)

    context = attend(queries, cache, lengths, live_rows[0])

    early_h, early_h_other = hidden_of(expert, early_own, early_other, w_gate, w_up, picks)
    late_h, late_h_other = hidden_of(expert, late_own, late_other, w_gate, w_up, picks)

    (late_out,) = down_of(late_h_other, w_down, [late_h_other.shape[0]])
    late_in = swap(late_out, core)
    (early_out,) = down_of(early_h_other, w_down, [early_h_other.shape[0]])
    early_in = swap(early_out, core)
    near_xy, far_xy = down_of(late_h, w_down, late_cuts, late_in)
    near, near_x, near_y, far, far_x, far_y = down_of(early_h, w_down, early_cuts, early_in)
    rows, count = near.shape[0], tokens.shape[0]
    near_x = add_up(near_x, give_back(near_xy, y_steps, near_x.shape[0]))
    far_y = add_up(far_y, give_back(far_xy, x_steps, far_y.shape[0]))
    far = add_up(far, give_back(far_x, x_steps, rows) + give_back(far_y, y_steps, rows))
    near = add_up(near, give_back(near_y, y_steps, rows) + give_back(near_x, x_steps, rows))
    far = add_up(far[:count], give_back(far[count:], z_near, count))
    mixed = add_up(near[:count], give_back(near[count:], z_near, count) + [swap(far, z_far)])
    return (context, mixed)


def solution(mesh):
    rows3 = P(AXES, None, None)
    rows2 = P(AXES, None)
    rows1 = P(AXES)
    return jax.shard_map(
        per_device,
        mesh=mesh,
        in_specs=(rows3, rows3, rows1, rows1, rows2, rows2, rows2, rows3, rows3, rows3),
        out_specs=(rows3, rows2),
        check_vma=False,
    )
```

```python
import functools

import jax
import jax.numpy as jnp
from jax import lax
from jax.experimental import pallas as pl
from jax.experimental.pallas import tpu as pltpu
from jax.sharding import PartitionSpec as P

LAT = 512
AXES = ("grp", "ep")
EXTRA = 128
BLOCKS = 4
TILE = 256
RESIDENT_ROWS = 256
VMEM_BYTES = 48 * 1024 * 1024
LARGE_BYTES = 16 * 1024 * 1024
SMALL_BYTES = 8 * 1024 * 1024
whole = pl.BlockSpec(memory_space=pltpu.VMEM)

score_scale = 192.0 ** (-0.5)
neg_large = -1e30


def attend(queries, cache, lengths, live_count):
    scores = (
        jnp.einsum("rhc,rlc->rhl", queries, cache, preferred_element_type=jnp.float32) * score_scale
    )
    positions = lax.broadcasted_iota(jnp.int32, scores.shape, 2)
    inside = positions < lengths[:, None, None]
    masked = jnp.where(inside, scores, neg_large)
    highest = jnp.max(masked, axis=2, keepdims=True)
    powers = jnp.where(inside, jnp.exp(masked - highest), 0.0)
    totals = jnp.sum(powers, axis=2, keepdims=True)
    weights = (powers / totals).astype(jnp.bfloat16)
    context = jnp.einsum(
        "rhl,rlc->rhc", weights, cache[:, :, :LAT], preferred_element_type=jnp.float32
    ).astype(jnp.bfloat16)
    request_slot = lax.broadcasted_iota(jnp.int32, context.shape, 0)
    return jnp.where(request_slot < live_count, context, jnp.zeros_like(context))


def bits_of(count):
    return [1 << i for i in range(count.bit_length() - 1)]


def swap(value, step):
    axis, bit = step
    size = lax.axis_size(axis)
    return lax.ppermute(value, axis, [(i, i ^ bit) for i in range(size)])


def spread(value, steps):
    for step in steps:
        value = jnp.concatenate([value, swap(value, step)], axis=0)
    return value


def others(value, steps):
    if len(steps) == 1:
        return swap(value, steps[0])
    return spread(value, steps)[value.shape[0] :]


def give_back(rest, steps, rows):
    terms = []
    for step in reversed(steps):
        keep = (rest.shape[0] + rows) // 2 - rows
        arrived = swap(rest[keep:], step)
        terms.append(arrived[:rows])
        if keep:
            rest = add_up(rest[:keep], [arrived[rows:]])
    return terms


def add_up(own, terms):
    total = own.astype(jnp.float32)
    for term in terms:
        total = total + term.astype(jnp.float32)
    return total.astype(jnp.bfloat16)


def pack_kernel(tokens, ids, gates, out):
    feature = tokens.shape[1]
    high = gates[...].astype(jnp.bfloat16)
    low = (gates[...] - high.astype(jnp.float32)).astype(jnp.bfloat16)
    named = ids[...].astype(jnp.float32).astype(jnp.bfloat16)
    stacked = jnp.concatenate(
        [named.astype(jnp.float32), high.astype(jnp.float32), low.astype(jnp.float32)], axis=0
    ).astype(jnp.bfloat16)
    row = lax.broadcasted_iota(jnp.int32, (stacked.shape[0], EXTRA), 0)
    column = lax.broadcasted_iota(jnp.int32, (stacked.shape[0], EXTRA), 1)
    place = jnp.where(row == column, 1.0, 0.0).astype(jnp.bfloat16)
    extra = lax.dot_general(
        stacked, place, (((0,), (0,)), ((), ())), preferred_element_type=jnp.float32
    )
    out[:, :feature] = tokens[...]
    out[:, feature:] = extra.astype(jnp.bfloat16)


def pack(tokens, ids, gates):
    return pl.pallas_call(
        pack_kernel,
        out_shape=jax.ShapeDtypeStruct((tokens.shape[0], tokens.shape[1] + EXTRA), jnp.bfloat16),
        in_specs=[pl.BlockSpec(memory_space=pltpu.VMEM)] * 3,
        out_specs=pl.BlockSpec(memory_space=pltpu.VMEM),
        name="pack",
    )(tokens, ids.T, gates.T)


def hidden_kernel(picks, expert, own, other, extra_own, extra_other, w_gate, w_up, h_own, h_other, gate_sum, up_sum):
    step = pl.program_id(0)
    rows = jnp.concatenate([own[...], other[...]], axis=0)
    gate_part = jnp.dot(rows, w_gate[0], preferred_element_type=jnp.float32)
    up_part = jnp.dot(rows, w_up[0], preferred_element_type=jnp.float32)

    @pl.when(step == 0)
    def _():
        gate_sum[...] = gate_part
        up_sum[...] = up_part

    @pl.when(step > 0)
    def _():
        gate_sum[...] += gate_part
        up_sum[...] += up_part

    @pl.when(step == pl.num_programs(0) - 1)
    def _():
        count = own.shape[0]
        wanted = expert[0].astype(jnp.float32)
        for extra, out, at in ((extra_own, h_own, 0), (extra_other, h_other, count)):
            columns = extra[...].astype(jnp.float32)
            value = columns[:, picks : 2 * picks] + columns[:, 2 * picks : 3 * picks]
            share = jnp.sum(
                jnp.where(columns[:, :picks] == wanted, value, 0.0), axis=1, keepdims=True
            )
            gate_all = gate_sum[at : at + count, :]
            up_all = up_sum[at : at + count, :]
            hidden = gate_all / (1.0 + jnp.exp(-gate_all)) * up_all
            out[...] = (hidden * share).astype(jnp.bfloat16)


def hidden_of(expert, own, other, w_gate, w_up, picks):
    count, width = own.shape
    _, feature, half = w_gate.shape
    depth = feature // BLOCKS
    rows_spec = pl.BlockSpec((count, depth), lambda k: (0, k))
    extra_spec = pl.BlockSpec((count, EXTRA), lambda k: (0, feature // EXTRA))
    weight_spec = pl.BlockSpec((1, depth, half), lambda k: (0, k, 0))
    out_spec = pl.BlockSpec((count, half), lambda k: (0, 0))
    return pl.pallas_call(
        functools.partial(hidden_kernel, picks),
        grid=(BLOCKS,),
        out_shape=[jax.ShapeDtypeStruct((count, half), jnp.bfloat16)] * 2,
        in_specs=[pl.BlockSpec(memory_space=pltpu.SMEM), rows_spec, rows_spec, extra_spec, extra_spec]
        + [weight_spec] * 2,
        out_specs=[out_spec] * 2,
        scratch_shapes=[pltpu.VMEM((2 * count, half), jnp.float32)] * 2,
        compiler_params=pltpu.CompilerParams(vmem_limit_bytes=VMEM_BYTES),
        cost_estimate=pl.CostEstimate(
            flops=8 * count * feature * half,
            bytes_accessed=4 * feature * half + 4 * count * width,
            transcendentals=2 * count * half,
        ),
        name="hidden",
    )(expert, own, other, own, other, w_gate, w_up)


def down_kernel(cuts, hidden, w_down, *refs):
    part = jnp.dot(hidden[...], w_down[0], preferred_element_type=jnp.float32)
    if len(refs) > len(cuts):
        part = part + refs[0][...].astype(jnp.float32)
        refs = refs[1:]
    at = 0
    for cut, out in zip(cuts, refs):
        out[...] = part[at : at + cut, :].astype(jnp.bfloat16)
        at += cut


def down_of(hidden, w_down, cuts, arrived=None):
    count, half = hidden.shape
    feature = w_down.shape[2]
    wide = feature // BLOCKS
    operands = [hidden, w_down]
    in_specs = [
        pl.BlockSpec((count, half), lambda n: (0, 0)),
        pl.BlockSpec((1, half, wide), lambda n: (0, 0, n)),
    ]
    if arrived is not None:
        operands.append(arrived)
        in_specs.append(pl.BlockSpec((count, wide), lambda n: (0, n)))
    return pl.pallas_call(
        functools.partial(down_kernel, cuts),
        grid=(BLOCKS,),
        out_shape=[jax.ShapeDtypeStruct((cut, feature), jnp.bfloat16) for cut in cuts],
        in_specs=in_specs,
        out_specs=[pl.BlockSpec((cut, wide), lambda n: (0, n)) for cut in cuts],
        compiler_params=pltpu.CompilerParams(vmem_limit_bytes=VMEM_BYTES),
        cost_estimate=pl.CostEstimate(
            flops=2 * count * feature * half,
            bytes_accessed=2 * feature * half + 4 * count * feature,
            transcendentals=0,
        ),
        name="down",
    )(*operands)


def join_kernel(count, *refs):
    out, at = refs[-1], 0
    for group in refs[:count]:
        out[at : at + group.shape[0], :] = group[...]
        at += group.shape[0]


def join(groups, after=()):
    rows = sum(group.shape[0] for group in groups)
    return pl.pallas_call(
        functools.partial(join_kernel, len(groups)),
        out_shape=jax.ShapeDtypeStruct((rows, groups[0].shape[1]), groups[0].dtype),
        in_specs=[whole] * len(groups) + [pl.BlockSpec(memory_space=pl.ANY)] * len(after),
        out_specs=whole,
        compiler_params=pltpu.CompilerParams(vmem_limit_bytes=SMALL_BYTES),
        name="join",
    )(*groups, *after)


def expert_kernel(picks, own, other, w_gate, w_up, w_down, expert, *refs):
    h_own, out, rows, hidden = refs[-4:]
    count, feature, half = own.shape[0], w_gate.shape[1], w_gate.shape[2]
    wanted = expert[0].astype(jnp.float32)
    shares = []
    for ref, at in ((own, 0), (other, count)):
        rows[at : at + count, :] = ref[:, :feature]
        columns = ref[:, feature:].astype(jnp.float32)
        value = columns[:, picks : 2 * picks] + columns[:, 2 * picks : 3 * picks]
        named = columns[:, :picks] == wanted
        shares.append(jnp.sum(jnp.where(named, value, 0.0), axis=1, keepdims=True))
    share = jnp.concatenate(shares, axis=0)
    for at in range(0, half, TILE):
        gate_part = jnp.dot(
            rows[...], w_gate[0, :, at : at + TILE], preferred_element_type=jnp.float32
        )
        up_part = jnp.dot(
            rows[...], w_up[0, :, at : at + TILE], preferred_element_type=jnp.float32
        )
        product = gate_part / (1.0 + jnp.exp(-gate_part)) * up_part * share
        hidden[:, at : at + TILE] = product.astype(jnp.bfloat16)
    h_own[...] = hidden[:count, :]
    for at in range(0, feature, 2 * TILE):
        out[:, at : at + 2 * TILE] = jnp.dot(
            hidden[count:, :],
            w_down[0, :, at : at + 2 * TILE],
            preferred_element_type=jnp.float32,
        ).astype(jnp.bfloat16)


def expert_of(expert, own, other, w_gate, w_up, w_down, picks, after=()):
    count = own.shape[0]
    _, feature, half = w_gate.shape
    return pl.pallas_call(
        functools.partial(expert_kernel, picks),
        out_shape=[
            jax.ShapeDtypeStruct((count, half), jnp.bfloat16),
            jax.ShapeDtypeStruct((count, feature), jnp.bfloat16),
        ],
        in_specs=[whole] * 5
        + [pl.BlockSpec(memory_space=pltpu.SMEM)]
        + [pl.BlockSpec(memory_space=pl.ANY)] * len(after),
        out_specs=[whole] * 2,
        scratch_shapes=[
            pltpu.VMEM((2 * count, feature), jnp.bfloat16),
            pltpu.VMEM((2 * count, half), jnp.bfloat16),
        ],
        compiler_params=pltpu.CompilerParams(vmem_limit_bytes=LARGE_BYTES),
        cost_estimate=pl.CostEstimate(
            flops=10 * count * feature * half,
            bytes_accessed=2 * count * feature,
            transcendentals=2 * count * half,
        ),
        name="expert",
    )(own, other, w_gate, w_up, w_down, expert, *after)


def sums_kernel(cuts, hidden, w_down, arrived, *outs):
    feature = w_down.shape[2]
    for column in range(0, feature, 2 * TILE):
        span = slice(column, column + 2 * TILE)
        part = jnp.dot(hidden[...], w_down[0, :, span], preferred_element_type=jnp.float32)
        part = part + arrived[:, span].astype(jnp.float32)
        at = 0
        for cut, out in zip(cuts, outs):
            out[:, span] = part[at : at + cut, :].astype(jnp.bfloat16)
            at += cut


def sums_of(hidden, w_down, cuts, arrived):
    count, half = hidden.shape
    feature = w_down.shape[2]
    return pl.pallas_call(
        functools.partial(sums_kernel, cuts),
        out_shape=[jax.ShapeDtypeStruct((cut, feature), jnp.bfloat16) for cut in cuts],
        in_specs=[whole] * 3,
        out_specs=[whole] * len(cuts),
        compiler_params=pltpu.CompilerParams(vmem_limit_bytes=SMALL_BYTES),
        cost_estimate=pl.CostEstimate(
            flops=2 * count * feature * half,
            bytes_accessed=2 * count * feature,
            transcendentals=0,
        ),
        name="sums",
    )(hidden, w_down, arrived)


def per_device(queries, cache, lengths, live_rows, tokens, ids, gates, w_gate, w_up, w_down):
    picks = ids.shape[1]
    grp_bits = bits_of(lax.axis_size("grp"))
    ep_bits = bits_of(lax.axis_size("ep"))
    core = ("grp", 1)
    z_near = [("grp", bit) for bit in reversed(grp_bits[1:-1])]
    z_far = ("grp", grp_bits[-1])
    x_steps = [("ep", bit) for bit in ep_bits[: len(ep_bits) // 2]]
    y_steps = [("ep", bit) for bit in ep_bits[len(ep_bits) // 2 :]]
    expert = ((lax.axis_index("grp") * lax.axis_size("ep") + lax.axis_index("ep")) >> 1).reshape(1)

    packed = pack(tokens, ids, gates)
    near = spread(packed, z_near)
    far = spread(swap(packed, z_far), z_near)
    near_x, near_y = others(near, x_steps), others(near, y_steps)
    far_x, far_y = others(far, x_steps), others(far, y_steps)
    near_xy, far_xy = others(near_x, y_steps), others(far_y, x_steps)
    early = [near, near_x, near_y, far, far_x, far_y]
    late = [near_xy, far_xy]
    early_cuts = [group.shape[0] for group in early]
    late_cuts = [group.shape[0] for group in late]
    context = attend(queries, cache, lengths, live_rows[0])

    if sum(early_cuts) <= RESIDENT_ROWS:
        early_own = join(early)
        early_other = swap(early_own, core)
        early_h, early_out = expert_of(expert, early_own, early_other, w_gate, w_up, w_down, picks)
        early_in = swap(early_out, core)
        late_own = join(late, [early_out])
        late_other = swap(late_own, core)
        near, near_x, near_y, far, far_x, far_y = sums_of(early_h, w_down, early_cuts, early_in)
        late_h, late_out = expert_of(
            expert, late_own, late_other, w_gate, w_up, w_down, picks, [near]
        )
        near_xy, far_xy = sums_of(late_h, w_down, late_cuts, swap(late_out, core))
    else:
        early_own, late_own = jnp.concatenate(early, axis=0), jnp.concatenate(late, axis=0)
        early_other, late_other = swap(early_own, core), swap(late_own, core)
        early_h, early_h_other = hidden_of(expert, early_own, early_other, w_gate, w_up, picks)
        late_h, late_h_other = hidden_of(expert, late_own, late_other, w_gate, w_up, picks)
        (late_out,) = down_of(late_h_other, w_down, [late_h_other.shape[0]])
        late_in = swap(late_out, core)
        (early_out,) = down_of(early_h_other, w_down, [early_h_other.shape[0]])
        early_in = swap(early_out, core)
        near_xy, far_xy = down_of(late_h, w_down, late_cuts, late_in)
        near, near_x, near_y, far, far_x, far_y = down_of(early_h, w_down, early_cuts, early_in)

    rows, count = near.shape[0], tokens.shape[0]
    near_x = add_up(near_x, give_back(near_xy, y_steps, near_x.shape[0]))
    far_y = add_up(far_y, give_back(far_xy, x_steps, far_y.shape[0]))
    far = add_up(far, give_back(far_x, x_steps, rows) + give_back(far_y, y_steps, rows))
    near = add_up(near, give_back(near_y, y_steps, rows) + give_back(near_x, x_steps, rows))
    far = add_up(far[:count], give_back(far[count:], z_near, count))
    mixed = add_up(near[:count], give_back(near[count:], z_near, count) + [swap(far, z_far)])
    return (context, mixed)


def solution(mesh):
    rows3 = P(AXES, None, None)
    rows2 = P(AXES, None)
    rows1 = P(AXES)
    return jax.shard_map(
        per_device,
        mesh=mesh,
        in_specs=(rows3, rows3, rows1, rows1, rows2, rows2, rows2, rows3, rows3, rows3),
        out_specs=(rows3, rows2),
        check_vma=False,
    )
```

```python
import functools

import jax
import jax.numpy as jnp
from jax import lax
from jax.experimental import pallas as pl
from jax.experimental.pallas import tpu as pltpu
from jax.sharding import PartitionSpec as P

LAT = 512
AXES = ("grp", "ep")
EXTRA = 128
BLOCKS = 4
TILE = 256
WIDE = 512
VMEM_BYTES = 48 * 1024 * 1024
LARGE_BYTES = 16 * 1024 * 1024
SMALL_BYTES = 8 * 1024 * 1024
whole = pl.BlockSpec(memory_space=pltpu.VMEM)

score_scale = 192.0 ** (-0.5)
neg_large = -1e30


def attend(queries, cache, lengths, live_count):
    scores = (
        jnp.einsum("rhc,rlc->rhl", queries, cache, preferred_element_type=jnp.float32) * score_scale
    )
    positions = lax.broadcasted_iota(jnp.int32, scores.shape, 2)
    inside = positions < lengths[:, None, None]
    masked = jnp.where(inside, scores, neg_large)
    highest = jnp.max(masked, axis=2, keepdims=True)
    powers = jnp.where(inside, jnp.exp(masked - highest), 0.0)
    totals = jnp.sum(powers, axis=2, keepdims=True)
    weights = (powers / totals).astype(jnp.bfloat16)
    context = jnp.einsum(
        "rhl,rlc->rhc", weights, cache[:, :, :LAT], preferred_element_type=jnp.float32
    ).astype(jnp.bfloat16)
    request_slot = lax.broadcasted_iota(jnp.int32, context.shape, 0)
    return jnp.where(request_slot < live_count, context, jnp.zeros_like(context))


def bits_of(count):
    return [1 << i for i in range(count.bit_length() - 1)]


def swap(value, step):
    axis, bit = step
    size = lax.axis_size(axis)
    return lax.ppermute(value, axis, [(i, i ^ bit) for i in range(size)])


def spread(value, steps):
    for step in steps:
        value = jnp.concatenate([value, swap(value, step)], axis=0)
    return value


def others(value, steps):
    if len(steps) == 1:
        return swap(value, steps[0])
    return spread(value, steps)[value.shape[0] :]


def give_back(rest, steps, rows):
    terms = []
    for step in reversed(steps):
        keep = (rest.shape[0] + rows) // 2 - rows
        arrived = swap(rest[keep:], step)
        terms.append(arrived[:rows])
        if keep:
            rest = add_up(rest[:keep], [arrived[rows:]])
    return terms


def add_up(own, terms):
    total = own.astype(jnp.float32)
    for term in terms:
        total = total + term.astype(jnp.float32)
    return total.astype(jnp.bfloat16)


def pack_kernel(tokens, ids, gates, out):
    feature = tokens.shape[1]
    high = gates[...].astype(jnp.bfloat16)
    low = (gates[...] - high.astype(jnp.float32)).astype(jnp.bfloat16)
    named = ids[...].astype(jnp.float32).astype(jnp.bfloat16)
    stacked = jnp.concatenate(
        [named.astype(jnp.float32), high.astype(jnp.float32), low.astype(jnp.float32)], axis=0
    ).astype(jnp.bfloat16)
    row = lax.broadcasted_iota(jnp.int32, (stacked.shape[0], EXTRA), 0)
    column = lax.broadcasted_iota(jnp.int32, (stacked.shape[0], EXTRA), 1)
    place = jnp.where(row == column, 1.0, 0.0).astype(jnp.bfloat16)
    extra = lax.dot_general(
        stacked, place, (((0,), (0,)), ((), ())), preferred_element_type=jnp.float32
    )
    out[:, :feature] = tokens[...]
    out[:, feature:] = extra.astype(jnp.bfloat16)


def pack(tokens, ids, gates):
    return pl.pallas_call(
        pack_kernel,
        out_shape=jax.ShapeDtypeStruct((tokens.shape[0], tokens.shape[1] + EXTRA), jnp.bfloat16),
        in_specs=[pl.BlockSpec(memory_space=pltpu.VMEM)] * 3,
        out_specs=pl.BlockSpec(memory_space=pltpu.VMEM),
        name="pack",
    )(tokens, ids.T, gates.T)


def hidden_kernel(picks, expert, own, other, extra_own, extra_other, w_gate, w_up, h_own, h_other, gate_sum, up_sum):
    step = pl.program_id(0)
    rows = jnp.concatenate([own[...], other[...]], axis=0)
    gate_part = jnp.dot(rows, w_gate[0], preferred_element_type=jnp.float32)
    up_part = jnp.dot(rows, w_up[0], preferred_element_type=jnp.float32)

    @pl.when(step == 0)
    def _():
        gate_sum[...] = gate_part
        up_sum[...] = up_part

    @pl.when(step > 0)
    def _():
        gate_sum[...] += gate_part
        up_sum[...] += up_part

    @pl.when(step == pl.num_programs(0) - 1)
    def _():
        count = own.shape[0]
        wanted = expert[0].astype(jnp.float32)
        for extra, out, at in ((extra_own, h_own, 0), (extra_other, h_other, count)):
            columns = extra[...].astype(jnp.float32)
            value = columns[:, picks : 2 * picks] + columns[:, 2 * picks : 3 * picks]
            share = jnp.sum(
                jnp.where(columns[:, :picks] == wanted, value, 0.0), axis=1, keepdims=True
            )
            gate_all = gate_sum[at : at + count, :]
            up_all = up_sum[at : at + count, :]
            hidden = gate_all / (1.0 + jnp.exp(-gate_all)) * up_all
            out[...] = (hidden * share).astype(jnp.bfloat16)


def hidden_of(expert, own, other, w_gate, w_up, picks):
    count, width = own.shape
    _, feature, half = w_gate.shape
    depth = feature // BLOCKS
    rows_spec = pl.BlockSpec((count, depth), lambda k: (0, k))
    extra_spec = pl.BlockSpec((count, EXTRA), lambda k: (0, feature // EXTRA))
    weight_spec = pl.BlockSpec((1, depth, half), lambda k: (0, k, 0))
    out_spec = pl.BlockSpec((count, half), lambda k: (0, 0))
    return pl.pallas_call(
        functools.partial(hidden_kernel, picks),
        grid=(BLOCKS,),
        out_shape=[jax.ShapeDtypeStruct((count, half), jnp.bfloat16)] * 2,
        in_specs=[pl.BlockSpec(memory_space=pltpu.SMEM), rows_spec, rows_spec, extra_spec, extra_spec]
        + [weight_spec] * 2,
        out_specs=[out_spec] * 2,
        scratch_shapes=[pltpu.VMEM((2 * count, half), jnp.float32)] * 2,
        compiler_params=pltpu.CompilerParams(vmem_limit_bytes=VMEM_BYTES),
        cost_estimate=pl.CostEstimate(
            flops=8 * count * feature * half,
            bytes_accessed=4 * feature * half + 4 * count * width,
            transcendentals=2 * count * half,
        ),
        name="hidden",
    )(expert, own, other, own, other, w_gate, w_up)


def down_kernel(cuts, hidden, w_down, *refs):
    part = jnp.dot(hidden[...], w_down[0], preferred_element_type=jnp.float32)
    if len(refs) > len(cuts):
        part = part + refs[0][...].astype(jnp.float32)
        refs = refs[1:]
    at = 0
    for cut, out in zip(cuts, refs):
        out[...] = part[at : at + cut, :].astype(jnp.bfloat16)
        at += cut


def down_of(hidden, w_down, cuts, arrived=None):
    count, half = hidden.shape
    feature = w_down.shape[2]
    wide = feature // BLOCKS
    operands = [hidden, w_down]
    in_specs = [
        pl.BlockSpec((count, half), lambda n: (0, 0)),
        pl.BlockSpec((1, half, wide), lambda n: (0, 0, n)),
    ]
    if arrived is not None:
        operands.append(arrived)
        in_specs.append(pl.BlockSpec((count, wide), lambda n: (0, n)))
    return pl.pallas_call(
        functools.partial(down_kernel, cuts),
        grid=(BLOCKS,),
        out_shape=[jax.ShapeDtypeStruct((cut, feature), jnp.bfloat16) for cut in cuts],
        in_specs=in_specs,
        out_specs=[pl.BlockSpec((cut, wide), lambda n: (0, n)) for cut in cuts],
        compiler_params=pltpu.CompilerParams(vmem_limit_bytes=VMEM_BYTES),
        cost_estimate=pl.CostEstimate(
            flops=2 * count * feature * half,
            bytes_accessed=2 * feature * half + 4 * count * feature,
            transcendentals=0,
        ),
        name="down",
    )(*operands)


def combine_kernel(count, plans, *refs):
    outs = refs[len(refs) - len(plans) :]
    width = outs[0].shape[1]
    for plan, out in zip(plans, outs):
        at = 0
        for rows, terms in plan:
            if len(terms) == 1:
                index, start = terms[0]
                out[at : at + rows, :] = refs[index][start : start + rows, :]
            else:
                for left in range(0, width, WIDE):
                    span = slice(left, left + WIDE)
                    total = sum(
                        refs[index][start : start + rows, span].astype(jnp.float32)
                        for index, start in terms
                    )
                    out[at : at + rows, span] = total.astype(out.dtype)
            at += rows


def combine(inputs, plans, after=()):
    width = inputs[0].shape[1]
    return pl.pallas_call(
        functools.partial(combine_kernel, len(inputs), plans),
        out_shape=[
            jax.ShapeDtypeStruct((sum(rows for rows, _ in plan), width), jnp.bfloat16)
            for plan in plans
        ],
        in_specs=[whole] * len(inputs) + [pl.BlockSpec(memory_space=pl.ANY)] * len(after),
        out_specs=[whole] * len(plans),
        compiler_params=pltpu.CompilerParams(vmem_limit_bytes=SMALL_BYTES),
        name="combine",
    )(*inputs, *after)


def hold_kernel(parts, *refs):
    weight, out, sems = refs[0], refs[-2], refs[-1]
    depth = weight.shape[1] // parts
    copies = [
        pltpu.make_async_copy(
            weight.at[:, pl.ds(part * depth, depth), :],
            out.at[:, pl.ds(part * depth, depth), :],
            sems.at[part],
        )
        for part in range(parts)
    ]
    for copy in copies:
        copy.start()
    for copy in copies:
        copy.wait()


def hold(weight, after):
    parts = 8
    return pl.pallas_call(
        functools.partial(hold_kernel, parts),
        out_shape=jax.ShapeDtypeStruct(weight.shape, weight.dtype),
        in_specs=[pl.BlockSpec(memory_space=pltpu.HBM)]
        + [pl.BlockSpec(memory_space=pl.ANY)] * len(after),
        out_specs=whole,
        scratch_shapes=[pltpu.SemaphoreType.DMA((parts,))],
        compiler_params=pltpu.CompilerParams(vmem_limit_bytes=SMALL_BYTES),
        name="hold",
    )(weight, *after)


def expert_kernel(picks, own, other, w_gate, w_up, w_down, expert, *refs):
    h_own, out, rows, hidden = refs[-4:]
    count, feature, half = own.shape[0], w_gate.shape[1], w_gate.shape[2]
    wanted = expert[0].astype(jnp.float32)
    shares = []
    for ref, at in ((own, 0), (other, count)):
        rows[at : at + count, :] = ref[:, :feature]
        columns = ref[:, feature:].astype(jnp.float32)
        value = columns[:, picks : 2 * picks] + columns[:, 2 * picks : 3 * picks]
        named = columns[:, :picks] == wanted
        shares.append(jnp.sum(jnp.where(named, value, 0.0), axis=1, keepdims=True))
    share = jnp.concatenate(shares, axis=0)
    for at in range(0, half, TILE):
        gate_part = jnp.dot(
            rows[...], w_gate[0, :, at : at + TILE], preferred_element_type=jnp.float32
        )
        up_part = jnp.dot(
            rows[...], w_up[0, :, at : at + TILE], preferred_element_type=jnp.float32
        )
        product = gate_part / (1.0 + jnp.exp(-gate_part)) * up_part * share
        hidden[:, at : at + TILE] = product.astype(jnp.bfloat16)
    h_own[...] = hidden[:count, :]
    for at in range(0, feature, 2 * TILE):
        out[:, at : at + 2 * TILE] = jnp.dot(
            hidden[count:, :],
            w_down[0, :, at : at + 2 * TILE],
            preferred_element_type=jnp.float32,
        ).astype(jnp.bfloat16)


def expert_of(expert, own, other, w_gate, w_up, w_down, picks, after=()):
    count = own.shape[0]
    _, feature, half = w_gate.shape
    return pl.pallas_call(
        functools.partial(expert_kernel, picks),
        out_shape=[
            jax.ShapeDtypeStruct((count, half), jnp.bfloat16),
            jax.ShapeDtypeStruct((count, feature), jnp.bfloat16),
        ],
        in_specs=[whole] * 5
        + [pl.BlockSpec(memory_space=pltpu.SMEM)]
        + [pl.BlockSpec(memory_space=pl.ANY)] * len(after),
        out_specs=[whole] * 2,
        scratch_shapes=[
            pltpu.VMEM((2 * count, feature), jnp.bfloat16),
            pltpu.VMEM((2 * count, half), jnp.bfloat16),
        ],
        compiler_params=pltpu.CompilerParams(vmem_limit_bytes=LARGE_BYTES),
        cost_estimate=pl.CostEstimate(
            flops=10 * count * feature * half,
            bytes_accessed=2 * count * feature,
            transcendentals=2 * count * half,
        ),
        name="expert",
    )(own, other, w_gate, w_up, w_down, expert, *after)


def sums_kernel(cuts, hidden, w_down, arrived, *refs):
    outs = refs[len(refs) - len(cuts) :]
    feature = w_down.shape[2]
    for column in range(0, feature, 2 * TILE):
        span = slice(column, column + 2 * TILE)
        part = jnp.dot(hidden[...], w_down[0, :, span], preferred_element_type=jnp.float32)
        part = part + arrived[:, span].astype(jnp.float32)
        at = 0
        for cut, out in zip(cuts, outs):
            out[:, span] = part[at : at + cut, :].astype(jnp.bfloat16)
            at += cut


def sums_of(hidden, w_down, cuts, arrived, after=()):
    count, half = hidden.shape
    feature = w_down.shape[2]
    return pl.pallas_call(
        functools.partial(sums_kernel, cuts),
        out_shape=[jax.ShapeDtypeStruct((cut, feature), jnp.bfloat16) for cut in cuts],
        in_specs=[whole] * 3 + [pl.BlockSpec(memory_space=pl.ANY)] * len(after),
        out_specs=[whole] * len(cuts),
        compiler_params=pltpu.CompilerParams(vmem_limit_bytes=SMALL_BYTES),
        cost_estimate=pl.CostEstimate(
            flops=2 * count * feature * half,
            bytes_accessed=2 * count * feature,
            transcendentals=0,
        ),
        name="sums",
    )(hidden, w_down, arrived, *after)


def mix_large(packed, weights, expert, picks, steps):
    w_gate, w_up, w_down = weights
    z_near, z_far, x_steps, y_steps, core = steps
    near = spread(packed, z_near)
    far = spread(swap(packed, z_far), z_near)
    near_x, near_y = others(near, x_steps), others(near, y_steps)
    far_x, far_y = others(far, x_steps), others(far, y_steps)
    near_xy, far_xy = others(near_x, y_steps), others(far_y, x_steps)
    early = [near, near_x, near_y, far, far_x, far_y]
    late = [near_xy, far_xy]
    early_cuts = [group.shape[0] for group in early]
    late_cuts = [group.shape[0] for group in late]
    early_own, late_own = jnp.concatenate(early, axis=0), jnp.concatenate(late, axis=0)
    early_other, late_other = swap(early_own, core), swap(late_own, core)
    early_h, early_h_other = hidden_of(expert, early_own, early_other, w_gate, w_up, picks)
    late_h, late_h_other = hidden_of(expert, late_own, late_other, w_gate, w_up, picks)
    (late_out,) = down_of(late_h_other, w_down, [late_h_other.shape[0]])
    late_in = swap(late_out, core)
    (early_out,) = down_of(early_h_other, w_down, [early_h_other.shape[0]])
    early_in = swap(early_out, core)
    near_xy, far_xy = down_of(late_h, w_down, late_cuts, late_in)
    near, near_x, near_y, far, far_x, far_y = down_of(early_h, w_down, early_cuts, early_in)
    rows, count = near.shape[0], packed.shape[0]
    near_x = add_up(near_x, give_back(near_xy, y_steps, near_x.shape[0]))
    far_y = add_up(far_y, give_back(far_xy, x_steps, far_y.shape[0]))
    far = add_up(far, give_back(far_x, x_steps, rows) + give_back(far_y, y_steps, rows))
    near = add_up(near, give_back(near_y, y_steps, rows) + give_back(near_x, x_steps, rows))
    far = add_up(far[:count], give_back(far[count:], z_near, count))
    return add_up(near[:count], give_back(near[count:], z_near, count) + [swap(far, z_far)])


def mix_small(packed, weights, expert, picks, steps):
    w_gate, w_up, w_down = weights
    z_near, z_far, x, y, core = steps
    n = packed.shape[0]

    def rows_of(*segments):
        return [(count, [(index, start)]) for index, start, count in segments]

    from_near = swap(packed, z_near)
    from_far = swap(packed, z_far)
    w_down = hold(w_down, [packed])
    (near,) = combine([packed, from_near], [rows_of((0, 0, n), (1, 0, n))], [w_down])
    near_x, near_y = swap(near, x), swap(near, y)
    from_both = swap(from_far, z_near)
    w_gate = hold(w_gate, [near])
    first_own, far, half_x, half_y = combine(
        [near, near_x, near_y, from_far, from_both],
        [
            rows_of((0, 0, 2 * n), (1, 0, 2 * n), (2, 0, 2 * n)),
            rows_of((3, 0, n), (4, 0, n)),
            rows_of((1, 0, n)),
            rows_of((2, n, n)),
        ],
        [w_gate],
    )
    first_other = swap(first_own, core)
    far_x, far_y = swap(far, x), swap(far, y)
    near_xy_top, near_xy_low = swap(half_x, y), swap(half_y, x)
    w_up = hold(w_up, [far])
    held = (w_gate, w_up, w_down)
    first_h, first_out = expert_of(expert, first_own, first_other, *held, picks)
    second_own, half_x, half_y = combine(
        [near_xy_top, near_xy_low, far, far_x, far_y],
        [
            rows_of((0, 0, n), (1, 0, n), (2, 0, 2 * n), (3, 0, 2 * n), (4, 0, 2 * n)),
            rows_of((3, 0, n)),
            rows_of((4, n, n)),
        ],
        [first_out],
    )
    far_xy_top, far_xy_low = swap(half_x, y), swap(half_y, x)
    second_other = swap(second_own, core)
    first_in = swap(first_out, core)
    near, near_x, near_y = sums_of(first_h, w_down, [2 * n] * 3, first_in)
    (third_own,) = combine([far_xy_top, far_xy_low], [rows_of((0, 0, n), (1, 0, n))], [near])
    third_other = swap(third_own, core)
    second_h, second_out = expert_of(
        expert, second_own, second_other, *held, picks, [third_own]
    )
    second_in = swap(second_out, core)
    third_h, third_out = expert_of(expert, third_own, third_other, *held, picks, [second_out])
    near_xy_top, near_xy_low, far, far_x, far_y = sums_of(
        second_h, w_down, [n, n, 2 * n, 2 * n, 2 * n], second_in, [third_out]
    )
    third_in = swap(third_out, core)
    far_xy_top, far_xy_low = sums_of(third_h, w_down, [n, n], third_in)

    to_near_x, to_near_y = swap(near_xy_top, y), swap(near_xy_low, x)
    to_far_x, to_far_y = swap(far_xy_top, y), swap(far_xy_low, x)
    far_x, far_y, near_x, near_y = combine(
        [far_x, far_y, near_x, near_y, to_far_x, to_far_y, to_near_x, to_near_y],
        [
            [(n, [(0, 0), (4, 0)]), (n, [(0, n)])],
            [(n, [(1, 0)]), (n, [(1, n), (5, 0)])],
            [(n, [(2, 0), (6, 0)]), (n, [(2, n)])],
            [(n, [(3, 0)]), (n, [(3, n), (7, 0)])],
        ],
    )
    to_far = [swap(far_x, x), swap(far_y, y)]
    to_near = [swap(near_x, x), swap(near_y, y)]
    both = lambda start: [(n, [(0, start), (1, start), (2, start)])]
    far_sum, both_sum = combine([far, *to_far], [both(0), both(n)])
    own_sum, near_sum = combine([near, *to_near], [both(0), both(n)], [far_sum])
    size = lax.axis_size(z_far[0])
    direct = [(i, i ^ z_far[1] ^ z_near[1]) for i in range(size)]
    terms = [swap(far_sum, z_far), lax.ppermute(both_sum, z_far[0], direct), swap(near_sum, z_near)]
    (mixed,) = combine([own_sum, *terms], [[(n, [(0, 0), (1, 0), (2, 0), (3, 0)])]])
    return mixed


def per_device(queries, cache, lengths, live_rows, tokens, ids, gates, w_gate, w_up, w_down):
    picks = ids.shape[1]
    grp_bits = bits_of(lax.axis_size("grp"))
    ep_bits = bits_of(lax.axis_size("ep"))
    core = ("grp", 1)
    z_near = [("grp", bit) for bit in reversed(grp_bits[1:-1])]
    z_far = ("grp", grp_bits[-1])
    x_steps = [("ep", bit) for bit in ep_bits[: len(ep_bits) // 2]]
    y_steps = [("ep", bit) for bit in ep_bits[len(ep_bits) // 2 :]]
    expert = ((lax.axis_index("grp") * lax.axis_size("ep") + lax.axis_index("ep")) >> 1).reshape(1)

    context = attend(queries, cache, lengths, live_rows[0])
    packed = pack(tokens, ids, gates)
    weights = (w_gate, w_up, w_down)
    if len(z_near) == len(x_steps) == len(y_steps) == 1:
        steps = (z_near[0], z_far, x_steps[0], y_steps[0], core)
        mixed = mix_small(packed, weights, expert, picks, steps)
    else:
        steps = (z_near, z_far, x_steps, y_steps, core)
        mixed = mix_large(packed, weights, expert, picks, steps)
    return (context, mixed)


def solution(mesh):
    rows3 = P(AXES, None, None)
    rows2 = P(AXES, None)
    rows1 = P(AXES)
    return jax.shard_map(
        per_device,
        mesh=mesh,
        in_specs=(rows3, rows3, rows1, rows1, rows2, rows2, rows2, rows3, rows3, rows3),
        out_specs=(rows3, rows2),
        check_vma=False,
    )
```

```python
import functools

import jax
import jax.numpy as jnp
from jax import lax
from jax.experimental import pallas as pl
from jax.experimental.pallas import tpu as pltpu
from jax.sharding import PartitionSpec as P

LAT = 512
AXES = ("grp", "ep")
EXTRA = 128
BLOCKS = 4
TILE = 256
WIDE = 512
VMEM_BYTES = 48 * 1024 * 1024
LARGE_BYTES = 16 * 1024 * 1024
SMALL_BYTES = 8 * 1024 * 1024
FIRST_BYTES = 39 * 1024 * 1024
whole = pl.BlockSpec(memory_space=pltpu.VMEM)

score_scale = 192.0 ** (-0.5)
neg_large = -1e30


def attend_kernel(lengths, live_rows, queries, channels, out):
    request = pl.program_id(0)
    scores = jnp.dot(queries[0], channels[0], preferred_element_type=jnp.float32) * score_scale
    positions = lax.broadcasted_iota(jnp.int32, scores.shape, 1)
    inside = positions < lengths[request]
    masked = jnp.where(inside, scores, neg_large)
    highest = jnp.max(masked, axis=1, keepdims=True)
    powers = jnp.where(inside, jnp.exp(masked - highest), 0.0)
    totals = jnp.sum(powers, axis=1, keepdims=True)
    weights = (powers / totals).astype(jnp.bfloat16)
    context = lax.dot_general(
        weights,
        channels[0, :LAT, :],
        (((1,), (1,)), ((), ())),
        preferred_element_type=jnp.float32,
    )
    out[0] = jnp.where(request < live_rows[0], context, 0.0).astype(jnp.bfloat16)


def attend(queries, cache, lengths, live_rows, after=()):
    count, heads, width = queries.shape
    positions = cache.shape[1]
    scalars = pl.BlockSpec(memory_space=pltpu.SMEM)

    def kernel(*refs):
        attend_kernel(*refs[:4], refs[-2])
        refs[-1][...] = jnp.zeros_like(refs[-1])

    return pl.pallas_call(
        kernel,
        grid=(count,),
        out_shape=[
            jax.ShapeDtypeStruct((count, heads, LAT), jnp.bfloat16),
            jax.ShapeDtypeStruct((8, 128), jnp.float32),
        ],
        in_specs=[
            scalars,
            scalars,
            pl.BlockSpec((1, heads, width), lambda r: (r, 0, 0)),
            pl.BlockSpec((1, width, positions), lambda r: (r, 0, 0)),
        ]
        + [pl.BlockSpec(memory_space=pl.ANY)] * len(after),
        out_specs=[
            pl.BlockSpec((1, heads, LAT), lambda r: (r, 0, 0)),
            pl.BlockSpec((8, 128), lambda r: (0, 0)),
        ],
        compiler_params=pltpu.CompilerParams(vmem_limit_bytes=SMALL_BYTES),
        cost_estimate=pl.CostEstimate(
            flops=4 * count * heads * width * positions,
            bytes_accessed=2 * count * positions * width,
            transcendentals=count * heads * positions,
        ),
        name="attend",
    )(lengths, live_rows, queries, jnp.swapaxes(cache, 1, 2), *after)


def bits_of(count):
    return [1 << i for i in range(count.bit_length() - 1)]


def swap(value, step):
    axis, bit = step
    size = lax.axis_size(axis)
    return lax.ppermute(value, axis, [(i, i ^ bit) for i in range(size)])


def spread(value, steps):
    for step in steps:
        value = jnp.concatenate([value, swap(value, step)], axis=0)
    return value


def others(value, steps):
    if len(steps) == 1:
        return swap(value, steps[0])
    return spread(value, steps)[value.shape[0] :]


def give_back(rest, steps, rows):
    terms = []
    for step in reversed(steps):
        keep = (rest.shape[0] + rows) // 2 - rows
        arrived = swap(rest[keep:], step)
        terms.append(arrived[:rows])
        if keep:
            rest = add_up(rest[:keep], [arrived[rows:]])
    return terms


def add_up(own, terms):
    total = own.astype(jnp.float32)
    for term in terms:
        total = total + term.astype(jnp.float32)
    return total.astype(jnp.bfloat16)


def pack_kernel(tokens, ids, gates, out):
    feature = tokens.shape[1]
    high = gates[...].astype(jnp.bfloat16)
    low = (gates[...] - high.astype(jnp.float32)).astype(jnp.bfloat16)
    named = ids[...].astype(jnp.float32).astype(jnp.bfloat16)
    stacked = jnp.concatenate(
        [named.astype(jnp.float32), high.astype(jnp.float32), low.astype(jnp.float32)], axis=0
    ).astype(jnp.bfloat16)
    row = lax.broadcasted_iota(jnp.int32, (stacked.shape[0], EXTRA), 0)
    column = lax.broadcasted_iota(jnp.int32, (stacked.shape[0], EXTRA), 1)
    place = jnp.where(row == column, 1.0, 0.0).astype(jnp.bfloat16)
    extra = lax.dot_general(
        stacked, place, (((0,), (0,)), ((), ())), preferred_element_type=jnp.float32
    )
    out[:, :feature] = tokens[...]
    out[:, feature:] = extra.astype(jnp.bfloat16)


def pack(tokens, ids, gates):
    return pl.pallas_call(
        pack_kernel,
        out_shape=jax.ShapeDtypeStruct((tokens.shape[0], tokens.shape[1] + EXTRA), jnp.bfloat16),
        in_specs=[pl.BlockSpec(memory_space=pltpu.VMEM)] * 3,
        out_specs=pl.BlockSpec(memory_space=pltpu.VMEM),
        compiler_params=pltpu.CompilerParams(vmem_limit_bytes=SMALL_BYTES),
        name="pack",
    )(tokens, ids.T, gates.T)


def expert_index():
    return (lax.axis_index("grp") * lax.axis_size("ep") + lax.axis_index("ep")) // 2


def hidden_kernel(picks, own, other, extra_own, extra_other, w_gate, w_up, h_own, h_other, gate_sum, up_sum):
    step = pl.program_id(0)
    rows = jnp.concatenate([own[...], other[...]], axis=0)
    gate_part = jnp.dot(rows, w_gate[0], preferred_element_type=jnp.float32)
    up_part = jnp.dot(rows, w_up[0], preferred_element_type=jnp.float32)

    @pl.when(step == 0)
    def _():
        gate_sum[...] = gate_part
        up_sum[...] = up_part

    @pl.when(step > 0)
    def _():
        gate_sum[...] += gate_part
        up_sum[...] += up_part

    @pl.when(step == pl.num_programs(0) - 1)
    def _():
        count = own.shape[0]
        wanted = expert_index().astype(jnp.float32)
        for extra, out, at in ((extra_own, h_own, 0), (extra_other, h_other, count)):
            columns = extra[...].astype(jnp.float32)
            value = columns[:, picks : 2 * picks] + columns[:, 2 * picks : 3 * picks]
            share = jnp.sum(
                jnp.where(columns[:, :picks] == wanted, value, 0.0), axis=1, keepdims=True
            )
            gate_all = gate_sum[at : at + count, :]
            up_all = up_sum[at : at + count, :]
            hidden = gate_all / (1.0 + jnp.exp(-gate_all)) * up_all
            out[...] = (hidden * share).astype(jnp.bfloat16)


def hidden_of(own, other, w_gate, w_up, picks):
    count, width = own.shape
    _, feature, half = w_gate.shape
    depth = feature // BLOCKS
    rows_spec = pl.BlockSpec((count, depth), lambda k: (0, k))
    extra_spec = pl.BlockSpec((count, EXTRA), lambda k: (0, feature // EXTRA))
    weight_spec = pl.BlockSpec((1, depth, half), lambda k: (0, k, 0))
    out_spec = pl.BlockSpec((count, half), lambda k: (0, 0))
    return pl.pallas_call(
        functools.partial(hidden_kernel, picks),
        grid=(BLOCKS,),
        out_shape=[jax.ShapeDtypeStruct((count, half), jnp.bfloat16)] * 2,
        in_specs=[rows_spec] * 2 + [extra_spec] * 2 + [weight_spec] * 2,
        out_specs=[out_spec] * 2,
        scratch_shapes=[pltpu.VMEM((2 * count, half), jnp.float32)] * 2,
        compiler_params=pltpu.CompilerParams(vmem_limit_bytes=VMEM_BYTES),
        cost_estimate=pl.CostEstimate(
            flops=8 * count * feature * half,
            bytes_accessed=4 * feature * half + 4 * count * width,
            transcendentals=2 * count * half,
        ),
        name="hidden",
    )(own, other, own, other, w_gate, w_up)


def down_kernel(cuts, hidden, w_down, *refs):
    part = jnp.dot(hidden[...], w_down[0], preferred_element_type=jnp.float32)
    if len(refs) > len(cuts):
        part = part + refs[0][...].astype(jnp.float32)
        refs = refs[1:]
    at = 0
    for cut, out in zip(cuts, refs):
        out[...] = part[at : at + cut, :].astype(jnp.bfloat16)
        at += cut


def down_of(hidden, w_down, cuts, arrived=None):
    count, half = hidden.shape
    feature = w_down.shape[2]
    wide = feature // BLOCKS
    operands = [hidden, w_down]
    in_specs = [
        pl.BlockSpec((count, half), lambda n: (0, 0)),
        pl.BlockSpec((1, half, wide), lambda n: (0, 0, n)),
    ]
    if arrived is not None:
        operands.append(arrived)
        in_specs.append(pl.BlockSpec((count, wide), lambda n: (0, n)))
    return pl.pallas_call(
        functools.partial(down_kernel, cuts),
        grid=(BLOCKS,),
        out_shape=[jax.ShapeDtypeStruct((cut, feature), jnp.bfloat16) for cut in cuts],
        in_specs=in_specs,
        out_specs=[pl.BlockSpec((cut, wide), lambda n: (0, n)) for cut in cuts],
        compiler_params=pltpu.CompilerParams(vmem_limit_bytes=VMEM_BYTES),
        cost_estimate=pl.CostEstimate(
            flops=2 * count * feature * half,
            bytes_accessed=2 * feature * half + 4 * count * feature,
            transcendentals=0,
        ),
        name="down",
    )(*operands)


def combine_kernel(count, plans, *refs):
    outs = refs[len(refs) - len(plans) :]
    width = outs[0].shape[1]
    for plan, out in zip(plans, outs):
        at = 0
        for rows, terms in plan:
            if len(terms) == 1:
                index, start = terms[0]
                out[at : at + rows, :] = refs[index][start : start + rows, :]
            else:
                for left in range(0, width, WIDE):
                    span = slice(left, left + WIDE)
                    total = sum(
                        refs[index][start : start + rows, span].astype(jnp.float32)
                        for index, start in terms
                    )
                    out[at : at + rows, span] = total.astype(out.dtype)
            at += rows


def combine(inputs, plans, after=()):
    width = inputs[0].shape[1]
    return pl.pallas_call(
        functools.partial(combine_kernel, len(inputs), plans),
        out_shape=[
            jax.ShapeDtypeStruct((sum(rows for rows, _ in plan), width), jnp.bfloat16)
            for plan in plans
        ],
        in_specs=[whole] * len(inputs) + [pl.BlockSpec(memory_space=pl.ANY)] * len(after),
        out_specs=[whole] * len(plans),
        compiler_params=pltpu.CompilerParams(vmem_limit_bytes=SMALL_BYTES),
        name="combine",
    )(*inputs, *after)


def expert_kernel(picks, own, other, w_gate, w_up, w_down, *refs):
    expert_body(picks, own, other, w_gate, w_up, w_down, *refs[-4:])


def expert_body(
    picks, own, other, w_gate, w_up, w_down, h_own, out, rows, hidden, ready=lambda number: None
):
    count, feature, half = own.shape[0], w_gate.shape[1], w_gate.shape[2]
    wanted = expert_index().astype(jnp.float32)
    shares = []
    for ref, at in ((own, 0), (other, count)):
        rows[at : at + count, :] = ref[:, :feature]
        columns = ref[:, feature:].astype(jnp.float32)
        value = columns[:, picks : 2 * picks] + columns[:, 2 * picks : 3 * picks]
        named = columns[:, :picks] == wanted
        shares.append(jnp.sum(jnp.where(named, value, 0.0), axis=1, keepdims=True))
    share = jnp.concatenate(shares, axis=0)
    for at in range(0, half, TILE):
        ready(at // TILE * 2)
        gate_part = jnp.dot(
            rows[...], w_gate[0, :, at : at + TILE], preferred_element_type=jnp.float32
        )
        ready(at // TILE * 2 + 1)
        up_part = jnp.dot(
            rows[...], w_up[0, :, at : at + TILE], preferred_element_type=jnp.float32
        )
        product = gate_part / (1.0 + jnp.exp(-gate_part)) * up_part * share
        hidden[:, at : at + TILE] = product.astype(jnp.bfloat16)
    h_own[...] = hidden[:count, :]
    wide = feature // BLOCKS
    for at in range(0, feature, wide):
        ready(half // TILE * 2 + at // wide)
        out[:, at : at + wide] = jnp.dot(
            hidden[count:, :], w_down[0, :, at : at + wide], preferred_element_type=jnp.float32
        ).astype(jnp.bfloat16)


def first_kernel(picks, own, other, gate_far, up_far, down_far, *refs):
    h_own, out, w_gate, w_up, w_down, rows, hidden, sems = refs
    feature, half = w_gate.shape[1], w_gate.shape[2]
    depth = feature // BLOCKS
    groups = []

    def begin(pairs):
        copies = []
        for source, target, index in pairs:
            at = len(copies) + sum(len(group) for group in groups)
            copies.append(pltpu.make_async_copy(source.at[index], target.at[index], sems.at[at]))
        for copy in copies:
            copy.start()
        groups.append(copies)

    for left in range(0, half, TILE):
        for source, target in ((gate_far, w_gate), (up_far, w_up)):
            begin(
                (source, target, (0, pl.ds(top, depth), pl.ds(left, TILE)))
                for top in range(0, feature, depth)
            )
    for left in range(0, feature, feature // BLOCKS):
        begin([(down_far, w_down, (0, slice(None), pl.ds(left, feature // BLOCKS)))])

    def ready(number):
        for copy in groups[number]:
            copy.wait()

    expert_body(picks, own, other, w_gate, w_up, w_down, h_own, out, rows, hidden, ready)


def first_of(own, other, w_gate, w_up, w_down, picks, after=()):
    count = own.shape[0]
    _, feature, half = w_gate.shape
    copies = 2 * (half // TILE) * BLOCKS + BLOCKS
    return pl.pallas_call(
        functools.partial(first_kernel, picks),
        out_shape=[
            jax.ShapeDtypeStruct((count, half), jnp.bfloat16),
            jax.ShapeDtypeStruct((count, feature), jnp.bfloat16),
        ]
        + [jax.ShapeDtypeStruct(w.shape, w.dtype) for w in (w_gate, w_up, w_down)],
        in_specs=[whole] * 2 + [pl.BlockSpec(memory_space=pl.ANY)] * 3,
        out_specs=[whole] * 5,
        scratch_shapes=[
            pltpu.VMEM((2 * count, feature), jnp.bfloat16),
            pltpu.VMEM((2 * count, half), jnp.bfloat16),
            pltpu.SemaphoreType.DMA((copies,)),
        ],
        compiler_params=pltpu.CompilerParams(vmem_limit_bytes=FIRST_BYTES),
        cost_estimate=pl.CostEstimate(
            flops=10 * count * feature * half,
            bytes_accessed=6 * feature * half,
            transcendentals=2 * count * half,
        ),
        name="first",
    )(own, other, w_gate, w_up, w_down)


def expert_of(own, other, w_gate, w_up, w_down, picks, after=()):
    count = own.shape[0]
    _, feature, half = w_gate.shape
    return pl.pallas_call(
        functools.partial(expert_kernel, picks),
        out_shape=[
            jax.ShapeDtypeStruct((count, half), jnp.bfloat16),
            jax.ShapeDtypeStruct((count, feature), jnp.bfloat16),
        ],
        in_specs=[whole] * 5 + [pl.BlockSpec(memory_space=pl.ANY)] * len(after),
        out_specs=[whole] * 2,
        scratch_shapes=[
            pltpu.VMEM((2 * count, feature), jnp.bfloat16),
            pltpu.VMEM((2 * count, half), jnp.bfloat16),
        ],
        compiler_params=pltpu.CompilerParams(vmem_limit_bytes=LARGE_BYTES),
        cost_estimate=pl.CostEstimate(
            flops=10 * count * feature * half,
            bytes_accessed=2 * count * feature,
            transcendentals=2 * count * half,
        ),
        name="expert",
    )(own, other, w_gate, w_up, w_down, *after)


def sums_kernel(cuts, hidden, w_down, arrived, *refs):
    outs = refs[len(refs) - len(cuts) :]
    feature = w_down.shape[2]
    for column in range(0, feature, 2 * TILE):
        span = slice(column, column + 2 * TILE)
        part = jnp.dot(hidden[...], w_down[0, :, span], preferred_element_type=jnp.float32)
        part = part + arrived[:, span].astype(jnp.float32)
        at = 0
        for cut, out in zip(cuts, outs):
            out[:, span] = part[at : at + cut, :].astype(jnp.bfloat16)
            at += cut


def sums_of(hidden, w_down, cuts, arrived, after=()):
    count, half = hidden.shape
    feature = w_down.shape[2]
    return pl.pallas_call(
        functools.partial(sums_kernel, cuts),
        out_shape=[jax.ShapeDtypeStruct((cut, feature), jnp.bfloat16) for cut in cuts],
        in_specs=[whole] * 3 + [pl.BlockSpec(memory_space=pl.ANY)] * len(after),
        out_specs=[whole] * len(cuts),
        compiler_params=pltpu.CompilerParams(vmem_limit_bytes=SMALL_BYTES),
        cost_estimate=pl.CostEstimate(
            flops=2 * count * feature * half,
            bytes_accessed=2 * count * feature,
            transcendentals=0,
        ),
        name="sums",
    )(hidden, w_down, arrived, *after)


def mix_large(packed, weights, picks, steps):
    w_gate, w_up, w_down = weights
    z_near, z_far, x_steps, y_steps, core = steps
    near = spread(packed, z_near)
    far = spread(swap(packed, z_far), z_near)
    near_x, near_y = others(near, x_steps), others(near, y_steps)
    far_x, far_y = others(far, x_steps), others(far, y_steps)
    near_xy, far_xy = others(near_x, y_steps), others(far_y, x_steps)
    early = [near, near_x, near_y, far, far_x, far_y]
    late = [near_xy, far_xy]
    early_cuts = [group.shape[0] for group in early]
    late_cuts = [group.shape[0] for group in late]
    early_own, late_own = jnp.concatenate(early, axis=0), jnp.concatenate(late, axis=0)
    early_other, late_other = swap(early_own, core), swap(late_own, core)
    early_h, early_h_other = hidden_of(early_own, early_other, w_gate, w_up, picks)
    late_h, late_h_other = hidden_of(late_own, late_other, w_gate, w_up, picks)
    (late_out,) = down_of(late_h_other, w_down, [late_h_other.shape[0]])
    late_in = swap(late_out, core)
    (early_out,) = down_of(early_h_other, w_down, [early_h_other.shape[0]])
    early_in = swap(early_out, core)
    near_xy, far_xy = down_of(late_h, w_down, late_cuts, late_in)
    near, near_x, near_y, far, far_x, far_y = down_of(early_h, w_down, early_cuts, early_in)
    rows, count = near.shape[0], packed.shape[0]
    near_x = add_up(near_x, give_back(near_xy, y_steps, near_x.shape[0]))
    far_y = add_up(far_y, give_back(far_xy, x_steps, far_y.shape[0]))
    far = add_up(far, give_back(far_x, x_steps, rows) + give_back(far_y, y_steps, rows))
    near = add_up(near, give_back(near_y, y_steps, rows) + give_back(near_x, x_steps, rows))
    far = add_up(far[:count], give_back(far[count:], z_near, count))
    return add_up(near[:count], give_back(near[count:], z_near, count) + [swap(far, z_far)])


def mix_small(packed, weights, picks, steps, attention):
    z_near, z_far, x, y, core = steps
    n = packed.shape[0]

    def rows_of(*segments):
        return [(count, [(index, start)]) for index, start, count in segments]

    from_near = swap(packed, z_near)
    from_far = swap(packed, z_far)
    (near,) = combine([packed, from_near], [rows_of((0, 0, n), (1, 0, n))])
    near_x, near_y = swap(near, x), swap(near, y)
    from_both = swap(from_far, z_near)
    context, done = attention([near])
    first_own, far, half_x, half_y = combine(
        [near, near_x, near_y, from_far, from_both],
        [
            rows_of((0, 0, 2 * n), (1, 0, 2 * n), (2, 0, 2 * n)),
            rows_of((3, 0, n), (4, 0, n)),
            rows_of((1, 0, n)),
            rows_of((2, n, n)),
        ],
        [done],
    )
    first_other = swap(first_own, core)
    far_x, far_y = swap(far, x), swap(far, y)
    near_xy_top, near_xy_low = swap(half_x, y), swap(half_y, x)
    first_h, first_out, *weights = first_of(first_own, first_other, *weights, picks)
    w_down = weights[2]
    second_own, half_x, half_y = combine(
        [near_xy_top, near_xy_low, far, far_x, far_y],
        [
            rows_of((0, 0, n), (1, 0, n), (2, 0, 2 * n), (3, 0, 2 * n), (4, 0, 2 * n)),
            rows_of((3, 0, n)),
            rows_of((4, n, n)),
        ],
        [first_out],
    )
    far_xy_top, far_xy_low = swap(half_x, y), swap(half_y, x)
    second_other = swap(second_own, core)
    first_in = swap(first_out, core)
    near, near_x, near_y = sums_of(first_h, w_down, [2 * n] * 3, first_in)
    (third_own,) = combine([far_xy_top, far_xy_low], [rows_of((0, 0, n), (1, 0, n))], [near])
    third_other = swap(third_own, core)
    second_h, second_out = expert_of(
        second_own, second_other, *weights, picks, [third_own]
    )
    second_in = swap(second_out, core)
    third_h, third_out = expert_of(third_own, third_other, *weights, picks, [second_out])
    near_xy_top, near_xy_low, far, far_x, far_y = sums_of(
        second_h, w_down, [n, n, 2 * n, 2 * n, 2 * n], second_in, [third_out]
    )
    third_in = swap(third_out, core)
    far_xy_top, far_xy_low = sums_of(third_h, w_down, [n, n], third_in)

    to_near_x, to_near_y = swap(near_xy_top, y), swap(near_xy_low, x)
    to_far_x, to_far_y = swap(far_xy_top, y), swap(far_xy_low, x)
    far_x, far_y, near_x, near_y = combine(
        [far_x, far_y, near_x, near_y, to_far_x, to_far_y, to_near_x, to_near_y],
        [
            [(n, [(0, 0), (4, 0)]), (n, [(0, n)])],
            [(n, [(1, 0)]), (n, [(1, n), (5, 0)])],
            [(n, [(2, 0), (6, 0)]), (n, [(2, n)])],
            [(n, [(3, 0)]), (n, [(3, n), (7, 0)])],
        ],
    )
    to_far = [swap(far_x, x), swap(far_y, y)]
    to_near = [swap(near_x, x), swap(near_y, y)]
    both = lambda start: [(n, [(0, start), (1, start), (2, start)])]
    far_sum, both_sum = combine([far, *to_far], [both(0), both(n)])
    own_sum, near_sum = combine([near, *to_near], [both(0), both(n)], [far_sum])
    size = lax.axis_size(z_far[0])
    direct = [(i, i ^ z_far[1] ^ z_near[1]) for i in range(size)]
    terms = [swap(far_sum, z_far), lax.ppermute(both_sum, z_far[0], direct), swap(near_sum, z_near)]
    (mixed,) = combine([own_sum, *terms], [[(n, [(0, 0), (1, 0), (2, 0), (3, 0)])]])
    return mixed, context


def per_device(queries, cache, lengths, live_rows, tokens, ids, gates, w_gate, w_up, w_down):
    picks = ids.shape[1]
    grp_bits = bits_of(lax.axis_size("grp"))
    ep_bits = bits_of(lax.axis_size("ep"))
    core = ("grp", 1)
    z_near = [("grp", bit) for bit in reversed(grp_bits[1:-1])]
    z_far = ("grp", grp_bits[-1])
    x_steps = [("ep", bit) for bit in ep_bits[: len(ep_bits) // 2]]
    y_steps = [("ep", bit) for bit in ep_bits[len(ep_bits) // 2 :]]

    packed = pack(tokens, ids, gates)
    weights = (w_gate, w_up, w_down)
    if len(z_near) == len(x_steps) == len(y_steps) == 1:
        steps = (z_near[0], z_far, x_steps[0], y_steps[0], core)
        attention = functools.partial(attend, queries, cache, lengths, live_rows)
        mixed, context = mix_small(packed, weights, picks, steps, attention)
    else:
        steps = (z_near, z_far, x_steps, y_steps, core)
        mixed = mix_large(packed, weights, picks, steps)
        context, _ = attend(queries, cache, lengths, live_rows)
    return (context, mixed)


def solution(mesh):
    rows3 = P(AXES, None, None)
    rows2 = P(AXES, None)
    rows1 = P(AXES)
    return jax.shard_map(
        per_device,
        mesh=mesh,
        in_specs=(rows3, rows3, rows1, rows1, rows2, rows2, rows2, rows3, rows3, rows3),
        out_specs=(rows3, rows2),
        check_vma=False,
    )
```

```python
import functools

import jax
import jax.numpy as jnp
from jax import lax
from jax.experimental import pallas as pl
from jax.experimental.pallas import tpu as pltpu
from jax.sharding import PartitionSpec as P

LAT = 512
AXES = ("grp", "ep")
EXTRA = 128
BLOCKS = 4
TILE = 256
WIDE = 512
VMEM_BYTES = 48 * 1024 * 1024
LARGE_BYTES = 16 * 1024 * 1024
SMALL_BYTES = 8 * 1024 * 1024
FIRST_BYTES = 39 * 1024 * 1024
whole = pl.BlockSpec(memory_space=pltpu.VMEM)

score_scale = 192.0 ** (-0.5)
neg_large = -1e30


def attend_kernel(lengths, live_rows, queries, channels, *refs):
    out, done = refs[-2:]
    count, heads, _ = queries.shape
    positions = lax.broadcasted_iota(jnp.int32, (heads, channels.shape[2]), 1)
    for request in range(count):
        scores = jnp.dot(
            queries[request], channels[request], preferred_element_type=jnp.float32
        )
        inside = positions < lengths[request]
        masked = jnp.where(inside, scores * score_scale, neg_large)
        highest = jnp.max(masked, axis=1, keepdims=True)
        powers = jnp.where(inside, jnp.exp(masked - highest), 0.0)
        totals = jnp.sum(powers, axis=1, keepdims=True)
        weights = (powers / totals).astype(jnp.bfloat16)
        context = lax.dot_general(
            weights,
            channels[request, :LAT, :],
            (((1,), (1,)), ((), ())),
            preferred_element_type=jnp.float32,
        )
        out[request] = jnp.where(request < live_rows[0], context, 0.0).astype(jnp.bfloat16)
    done[...] = jnp.zeros_like(done)


def attend(queries, cache, lengths, live_rows, after=()):
    count, heads, width = queries.shape
    positions = cache.shape[1]
    return pl.pallas_call(
        attend_kernel,
        out_shape=[
            jax.ShapeDtypeStruct((count, heads, LAT), jnp.bfloat16),
            jax.ShapeDtypeStruct((8, 128), jnp.float32),
        ],
        in_specs=[pl.BlockSpec(memory_space=pltpu.SMEM)] * 2
        + [whole] * 2
        + [pl.BlockSpec(memory_space=pl.ANY)] * len(after),
        out_specs=[whole] * 2,
        compiler_params=pltpu.CompilerParams(vmem_limit_bytes=SMALL_BYTES),
        cost_estimate=pl.CostEstimate(
            flops=4 * count * heads * width * positions,
            bytes_accessed=2 * count * positions * width,
            transcendentals=count * heads * positions,
        ),
        name="attend",
    )(lengths, live_rows, queries, jnp.swapaxes(cache, 1, 2), *after)


def bits_of(count):
    return [1 << i for i in range(count.bit_length() - 1)]


def swap(value, step):
    axis, bit = step
    size = lax.axis_size(axis)
    return lax.ppermute(value, axis, [(i, i ^ bit) for i in range(size)])


def across(value, first, second):
    axis = first[0]
    size = lax.axis_size(axis)
    return lax.ppermute(value, axis, [(i, i ^ first[1] ^ second[1]) for i in range(size)])


def spread(value, steps):
    for step in steps:
        value = jnp.concatenate([value, swap(value, step)], axis=0)
    return value


def others(value, steps):
    if len(steps) == 1:
        return swap(value, steps[0])
    return spread(value, steps)[value.shape[0] :]


def give_back(rest, steps, rows):
    terms = []
    for step in reversed(steps):
        keep = (rest.shape[0] + rows) // 2 - rows
        arrived = swap(rest[keep:], step)
        terms.append(arrived[:rows])
        if keep:
            rest = add_up(rest[:keep], [arrived[rows:]])
    return terms


def add_up(own, terms):
    total = own.astype(jnp.float32)
    for term in terms:
        total = total + term.astype(jnp.float32)
    return total.astype(jnp.bfloat16)


def pack_kernel(tokens, ids, gates, out, ids_here, gates_here, extra, sems):
    feature = tokens.shape[1]
    copies = [
        pltpu.make_async_copy(ids, ids_here, sems.at[0]),
        pltpu.make_async_copy(gates, gates_here, sems.at[1]),
        pltpu.make_async_copy(tokens, out.at[:, pl.ds(0, feature)], sems.at[2]),
    ]
    for copy in copies:
        copy.start()
    copies[0].wait()
    copies[1].wait()
    high = gates_here[...].astype(jnp.bfloat16).astype(jnp.float32)
    low = gates_here[...] - high
    stacked = jnp.concatenate([ids_here[...].astype(jnp.float32), high, low], axis=0)
    stacked = stacked.astype(jnp.bfloat16)
    row = lax.broadcasted_iota(jnp.int32, (stacked.shape[0], EXTRA), 0)
    column = lax.broadcasted_iota(jnp.int32, (stacked.shape[0], EXTRA), 1)
    place = jnp.where(row == column, 1.0, 0.0).astype(jnp.bfloat16)
    extra[...] = lax.dot_general(
        stacked, place, (((0,), (0,)), ((), ())), preferred_element_type=jnp.float32
    ).astype(jnp.bfloat16)
    last = pltpu.make_async_copy(extra, out.at[:, pl.ds(feature, EXTRA)], sems.at[3])
    last.start()
    copies[2].wait()
    last.wait()


def pack(tokens, ids, gates):
    rows, feature = tokens.shape
    picks = ids.shape[1]
    return pl.pallas_call(
        pack_kernel,
        out_shape=jax.ShapeDtypeStruct((rows, feature + EXTRA), jnp.bfloat16),
        in_specs=[pl.BlockSpec(memory_space=pl.ANY)] * 3,
        out_specs=pl.BlockSpec(memory_space=pl.ANY),
        scratch_shapes=[
            pltpu.VMEM((picks, rows), jnp.int32),
            pltpu.VMEM((picks, rows), jnp.float32),
            pltpu.VMEM((rows, EXTRA), jnp.bfloat16),
            pltpu.SemaphoreType.DMA((4,)),
        ],
        name="pack",
    )(tokens, ids.T, gates.T)


def expert_index():
    return (lax.axis_index("grp") * lax.axis_size("ep") + lax.axis_index("ep")) // 2


def hidden_kernel(picks, own, other, extra_own, extra_other, w_gate, w_up, h_own, h_other, gate_sum, up_sum):
    step = pl.program_id(0)
    rows = jnp.concatenate([own[...], other[...]], axis=0)
    gate_part = jnp.dot(rows, w_gate[0], preferred_element_type=jnp.float32)
    up_part = jnp.dot(rows, w_up[0], preferred_element_type=jnp.float32)

    @pl.when(step == 0)
    def _():
        gate_sum[...] = gate_part
        up_sum[...] = up_part

    @pl.when(step > 0)
    def _():
        gate_sum[...] += gate_part
        up_sum[...] += up_part

    @pl.when(step == pl.num_programs(0) - 1)
    def _():
        count = own.shape[0]
        wanted = expert_index().astype(jnp.float32)
        for extra, out, at in ((extra_own, h_own, 0), (extra_other, h_other, count)):
            columns = extra[...].astype(jnp.float32)
            value = columns[:, picks : 2 * picks] + columns[:, 2 * picks : 3 * picks]
            share = jnp.sum(
                jnp.where(columns[:, :picks] == wanted, value, 0.0), axis=1, keepdims=True
            )
            gate_all = gate_sum[at : at + count, :]
            up_all = up_sum[at : at + count, :]
            hidden = gate_all / (1.0 + jnp.exp(-gate_all)) * up_all
            out[...] = (hidden * share).astype(jnp.bfloat16)


def hidden_of(own, other, w_gate, w_up, picks):
    count, width = own.shape
    _, feature, half = w_gate.shape
    depth = feature // BLOCKS
    rows_spec = pl.BlockSpec((count, depth), lambda k: (0, k))
    extra_spec = pl.BlockSpec((count, EXTRA), lambda k: (0, feature // EXTRA))
    weight_spec = pl.BlockSpec((1, depth, half), lambda k: (0, k, 0))
    out_spec = pl.BlockSpec((count, half), lambda k: (0, 0))
    return pl.pallas_call(
        functools.partial(hidden_kernel, picks),
        grid=(BLOCKS,),
        out_shape=[jax.ShapeDtypeStruct((count, half), jnp.bfloat16)] * 2,
        in_specs=[rows_spec] * 2 + [extra_spec] * 2 + [weight_spec] * 2,
        out_specs=[out_spec] * 2,
        scratch_shapes=[pltpu.VMEM((2 * count, half), jnp.float32)] * 2,
        compiler_params=pltpu.CompilerParams(vmem_limit_bytes=VMEM_BYTES),
        cost_estimate=pl.CostEstimate(
            flops=8 * count * feature * half,
            bytes_accessed=4 * feature * half + 4 * count * width,
            transcendentals=2 * count * half,
        ),
        name="hidden",
    )(own, other, own, other, w_gate, w_up)


def down_kernel(cuts, hidden, w_down, *refs):
    part = jnp.dot(hidden[...], w_down[0], preferred_element_type=jnp.float32)
    if len(refs) > len(cuts):
        part = part + refs[0][...].astype(jnp.float32)
        refs = refs[1:]
    at = 0
    for cut, out in zip(cuts, refs):
        out[...] = part[at : at + cut, :].astype(jnp.bfloat16)
        at += cut


def down_of(hidden, w_down, cuts, arrived=None):
    count, half = hidden.shape
    feature = w_down.shape[2]
    wide = feature // BLOCKS
    operands = [hidden, w_down]
    in_specs = [
        pl.BlockSpec((count, half), lambda n: (0, 0)),
        pl.BlockSpec((1, half, wide), lambda n: (0, 0, n)),
    ]
    if arrived is not None:
        operands.append(arrived)
        in_specs.append(pl.BlockSpec((count, wide), lambda n: (0, n)))
    return pl.pallas_call(
        functools.partial(down_kernel, cuts),
        grid=(BLOCKS,),
        out_shape=[jax.ShapeDtypeStruct((cut, feature), jnp.bfloat16) for cut in cuts],
        in_specs=in_specs,
        out_specs=[pl.BlockSpec((cut, wide), lambda n: (0, n)) for cut in cuts],
        compiler_params=pltpu.CompilerParams(vmem_limit_bytes=VMEM_BYTES),
        cost_estimate=pl.CostEstimate(
            flops=2 * count * feature * half,
            bytes_accessed=2 * feature * half + 4 * count * feature,
            transcendentals=0,
        ),
        name="down",
    )(*operands)


def combine_kernel(count, plans, *refs):
    outs = refs[len(refs) - len(plans) :]
    width = outs[0].shape[1]
    for plan, out in zip(plans, outs):
        at = 0
        for rows, terms in plan:
            if len(terms) == 1:
                index, start = terms[0]
                out[at : at + rows, :] = refs[index][start : start + rows, :]
            else:
                for left in range(0, width, WIDE):
                    span = slice(left, left + WIDE)
                    total = sum(
                        refs[index][start : start + rows, span].astype(jnp.float32)
                        for index, start in terms
                    )
                    out[at : at + rows, span] = total.astype(out.dtype)
            at += rows


def combine(inputs, plans, after=()):
    width = inputs[0].shape[1]
    return pl.pallas_call(
        functools.partial(combine_kernel, len(inputs), plans),
        out_shape=[
            jax.ShapeDtypeStruct((sum(rows for rows, _ in plan), width), jnp.bfloat16)
            for plan in plans
        ],
        in_specs=[whole] * len(inputs) + [pl.BlockSpec(memory_space=pl.ANY)] * len(after),
        out_specs=[whole] * len(plans),
        compiler_params=pltpu.CompilerParams(vmem_limit_bytes=SMALL_BYTES),
        name="combine",
    )(*inputs, *after)


def expert_kernel(picks, own, other, w_gate, w_up, w_down, *refs):
    expert_body(picks, own, other, w_gate, w_up, w_down, *refs[-4:])


def expert_body(
    picks, own, other, w_gate, w_up, w_down, h_own, out, rows, hidden, ready=lambda number: None
):
    count, feature, half = own.shape[0], w_gate.shape[1], w_gate.shape[2]
    wanted = expert_index().astype(jnp.float32)
    shares = []
    for ref, at in ((own, 0), (other, count)):
        rows[at : at + count, :] = ref[:, :feature]
        columns = ref[:, feature:].astype(jnp.float32)
        value = columns[:, picks : 2 * picks] + columns[:, 2 * picks : 3 * picks]
        named = columns[:, :picks] == wanted
        shares.append(jnp.sum(jnp.where(named, value, 0.0), axis=1, keepdims=True))
    share = jnp.concatenate(shares, axis=0)
    for at in range(0, half, TILE):
        ready(at // TILE * 2)
        gate_part = jnp.dot(
            rows[...], w_gate[0, :, at : at + TILE], preferred_element_type=jnp.float32
        )
        ready(at // TILE * 2 + 1)
        up_part = jnp.dot(
            rows[...], w_up[0, :, at : at + TILE], preferred_element_type=jnp.float32
        )
        product = gate_part / (1.0 + jnp.exp(-gate_part)) * up_part * share
        hidden[:, at : at + TILE] = product.astype(jnp.bfloat16)
    h_own[...] = hidden[:count, :]
    wide = feature // BLOCKS
    for at in range(0, feature, wide):
        ready(half // TILE * 2 + at // wide)
        out[:, at : at + wide] = jnp.dot(
            hidden[count:, :], w_down[0, :, at : at + wide], preferred_element_type=jnp.float32
        ).astype(jnp.bfloat16)


def first_kernel(picks, own, other, gate_far, up_far, down_far, *refs):
    h_own, out, w_gate, w_up, w_down, rows, hidden, sems = refs
    feature, half = w_gate.shape[1], w_gate.shape[2]
    depth = feature // BLOCKS
    groups = []

    def begin(pairs):
        copies = []
        for source, target, index in pairs:
            at = len(copies) + sum(len(group) for group in groups)
            copies.append(pltpu.make_async_copy(source.at[index], target.at[index], sems.at[at]))
        for copy in copies:
            copy.start()
        groups.append(copies)

    for left in range(0, half, TILE):
        for source, target in ((gate_far, w_gate), (up_far, w_up)):
            begin(
                (source, target, (0, pl.ds(top, depth), pl.ds(left, TILE)))
                for top in range(0, feature, depth)
            )
    for left in range(0, feature, feature // BLOCKS):
        begin([(down_far, w_down, (0, slice(None), pl.ds(left, feature // BLOCKS)))])

    def ready(number):
        for copy in groups[number]:
            copy.wait()

    expert_body(picks, own, other, w_gate, w_up, w_down, h_own, out, rows, hidden, ready)


def first_of(own, other, w_gate, w_up, w_down, picks, after=()):
    count = own.shape[0]
    _, feature, half = w_gate.shape
    copies = 2 * (half // TILE) * BLOCKS + BLOCKS
    return pl.pallas_call(
        functools.partial(first_kernel, picks),
        out_shape=[
            jax.ShapeDtypeStruct((count, half), jnp.bfloat16),
            jax.ShapeDtypeStruct((count, feature), jnp.bfloat16),
        ]
        + [jax.ShapeDtypeStruct(w.shape, w.dtype) for w in (w_gate, w_up, w_down)],
        in_specs=[whole] * 2 + [pl.BlockSpec(memory_space=pl.ANY)] * 3,
        out_specs=[whole] * 5,
        scratch_shapes=[
            pltpu.VMEM((2 * count, feature), jnp.bfloat16),
            pltpu.VMEM((2 * count, half), jnp.bfloat16),
            pltpu.SemaphoreType.DMA((copies,)),
        ],
        compiler_params=pltpu.CompilerParams(vmem_limit_bytes=FIRST_BYTES),
        cost_estimate=pl.CostEstimate(
            flops=10 * count * feature * half,
            bytes_accessed=6 * feature * half,
            transcendentals=2 * count * half,
        ),
        name="first",
    )(own, other, w_gate, w_up, w_down)


def expert_of(own, other, w_gate, w_up, w_down, picks, after=()):
    count = own.shape[0]
    _, feature, half = w_gate.shape
    return pl.pallas_call(
        functools.partial(expert_kernel, picks),
        out_shape=[
            jax.ShapeDtypeStruct((count, half), jnp.bfloat16),
            jax.ShapeDtypeStruct((count, feature), jnp.bfloat16),
        ],
        in_specs=[whole] * 5 + [pl.BlockSpec(memory_space=pl.ANY)] * len(after),
        out_specs=[whole] * 2,
        scratch_shapes=[
            pltpu.VMEM((2 * count, feature), jnp.bfloat16),
            pltpu.VMEM((2 * count, half), jnp.bfloat16),
        ],
        compiler_params=pltpu.CompilerParams(vmem_limit_bytes=LARGE_BYTES),
        cost_estimate=pl.CostEstimate(
            flops=10 * count * feature * half,
            bytes_accessed=2 * count * feature,
            transcendentals=2 * count * half,
        ),
        name="expert",
    )(own, other, w_gate, w_up, w_down, *after)


def sums_kernel(cuts, hidden, w_down, arrived, *refs):
    outs = refs[len(refs) - len(cuts) :]
    feature = w_down.shape[2]
    for column in range(0, feature, 2 * TILE):
        span = slice(column, column + 2 * TILE)
        part = jnp.dot(hidden[...], w_down[0, :, span], preferred_element_type=jnp.float32)
        part = part + arrived[:, span].astype(jnp.float32)
        at = 0
        for cut, out in zip(cuts, outs):
            out[:, span] = part[at : at + cut, :].astype(jnp.bfloat16)
            at += cut


def sums_of(hidden, w_down, cuts, arrived, after=()):
    count, half = hidden.shape
    feature = w_down.shape[2]
    return pl.pallas_call(
        functools.partial(sums_kernel, cuts),
        out_shape=[jax.ShapeDtypeStruct((cut, feature), jnp.bfloat16) for cut in cuts],
        in_specs=[whole] * 3 + [pl.BlockSpec(memory_space=pl.ANY)] * len(after),
        out_specs=[whole] * len(cuts),
        compiler_params=pltpu.CompilerParams(vmem_limit_bytes=SMALL_BYTES),
        cost_estimate=pl.CostEstimate(
            flops=2 * count * feature * half,
            bytes_accessed=2 * count * feature,
            transcendentals=0,
        ),
        name="sums",
    )(hidden, w_down, arrived, *after)


def mix_large(packed, weights, picks, steps):
    w_gate, w_up, w_down = weights
    z_near, z_far, x_steps, y_steps, core = steps
    near = spread(packed, z_near)
    far = spread(swap(packed, z_far), z_near)
    near_x, near_y = others(near, x_steps), others(near, y_steps)
    far_x, far_y = others(far, x_steps), others(far, y_steps)
    near_xy, far_xy = others(near_x, y_steps), others(far_y, x_steps)
    early = [near, near_x, near_y, far, far_x, far_y]
    late = [near_xy, far_xy]
    early_cuts = [group.shape[0] for group in early]
    late_cuts = [group.shape[0] for group in late]
    early_own, late_own = jnp.concatenate(early, axis=0), jnp.concatenate(late, axis=0)
    early_other, late_other = swap(early_own, core), swap(late_own, core)
    early_h, early_h_other = hidden_of(early_own, early_other, w_gate, w_up, picks)
    late_h, late_h_other = hidden_of(late_own, late_other, w_gate, w_up, picks)
    (late_out,) = down_of(late_h_other, w_down, [late_h_other.shape[0]])
    late_in = swap(late_out, core)
    (early_out,) = down_of(early_h_other, w_down, [early_h_other.shape[0]])
    early_in = swap(early_out, core)
    near_xy, far_xy = down_of(late_h, w_down, late_cuts, late_in)
    near, near_x, near_y, far, far_x, far_y = down_of(early_h, w_down, early_cuts, early_in)
    rows, count = near.shape[0], packed.shape[0]
    near_x = add_up(near_x, give_back(near_xy, y_steps, near_x.shape[0]))
    far_y = add_up(far_y, give_back(far_xy, x_steps, far_y.shape[0]))
    far = add_up(far, give_back(far_x, x_steps, rows) + give_back(far_y, y_steps, rows))
    near = add_up(near, give_back(near_y, y_steps, rows) + give_back(near_x, x_steps, rows))
    far = add_up(far[:count], give_back(far[count:], z_near, count))
    return add_up(near[:count], give_back(near[count:], z_near, count) + [swap(far, z_far)])


def mix_small(packed, weights, picks, steps, attention):
    z_near, z_far, x, y, core = steps
    n = packed.shape[0]

    def rows_of(*segments):
        return [(count, [(index, start)]) for index, start, count in segments]

    from_near = swap(packed, z_near)
    from_far = swap(packed, z_far)
    (near,) = combine([packed, from_near], [rows_of((0, 0, n), (1, 0, n))])
    near_x, near_y = swap(near, x), swap(near, y)
    from_both = swap(from_far, z_near)
    first_own, far, half_x, half_y = combine(
        [near, near_x, near_y, from_far, from_both],
        [
            rows_of((0, 0, 2 * n), (1, 0, 2 * n), (2, 0, 2 * n), (3, 0, n), (4, 0, n)),
            rows_of((3, 0, n), (4, 0, n)),
            rows_of((1, 0, n)),
            rows_of((2, n, n)),
        ],
    )
    far_x, far_y, far_xy = swap(far, x), swap(far, y), across(far, x, y)
    near_xy_top, near_xy_low = swap(half_x, y), swap(half_y, x)
    first_other = swap(first_own, core)
    first_h, first_out, *weights = first_of(first_own, first_other, *weights, picks)
    w_down = weights[2]
    (second_own,) = combine(
        [far_x, far_y, far_xy, near_xy_top, near_xy_low],
        [
            rows_of(
                (0, 0, 2 * n), (1, 0, 2 * n), (2, 0, 2 * n), (3, 0, n), (4, 0, n)
            )
        ],
        [first_out],
    )
    second_other = swap(second_own, core)
    first_in = swap(first_out, core)
    near, near_x, near_y, far = sums_of(first_h, w_down, [2 * n] * 4, first_in)
    second_h, second_out = expert_of(second_own, second_other, *weights, picks, [near])
    second_in = swap(second_out, core)
    far_x, far_y, far_xy, near_xy_top, near_xy_low = sums_of(
        second_h, w_down, [2 * n] * 3 + [n] * 2, second_in
    )

    to_far = [swap(far_x, x), swap(far_y, y), across(far_xy, x, y)]
    to_near_x, to_near_y = swap(near_xy_top, y), swap(near_xy_low, x)
    context, done = attention([far_x])
    near_x, near_y = combine(
        [near_x, near_y, to_near_x, to_near_y],
        [
            [(n, [(0, 0), (2, 0)]), (n, [(0, n)])],
            [(n, [(1, 0)]), (n, [(1, n), (3, 0)])],
        ],
        [done],
    )
    to_near = [swap(near_x, x), swap(near_y, y)]

    def all_of(terms, start):
        return [(n, [(index, start) for index in range(terms)])]

    far_sum, both_sum = combine([far, *to_far], [all_of(4, 0), all_of(4, n)], [near_x])
    own_sum, near_sum = combine([near, *to_near], [all_of(3, 0), all_of(3, n)], [far_sum])
    terms = [swap(far_sum, z_far), across(both_sum, z_far, z_near), swap(near_sum, z_near)]
    (mixed,) = combine([own_sum, *terms], [all_of(4, 0)])
    return mixed, context


def per_device(queries, cache, lengths, live_rows, tokens, ids, gates, w_gate, w_up, w_down):
    picks = ids.shape[1]
    grp_bits = bits_of(lax.axis_size("grp"))
    ep_bits = bits_of(lax.axis_size("ep"))
    core = ("grp", 1)
    z_near = [("grp", bit) for bit in reversed(grp_bits[1:-1])]
    z_far = ("grp", grp_bits[-1])
    x_steps = [("ep", bit) for bit in ep_bits[: len(ep_bits) // 2]]
    y_steps = [("ep", bit) for bit in ep_bits[len(ep_bits) // 2 :]]

    packed = pack(tokens, ids, gates)
    weights = (w_gate, w_up, w_down)
    if len(z_near) == len(x_steps) == len(y_steps) == 1:
        steps = (z_near[0], z_far, x_steps[0], y_steps[0], core)
        attention = functools.partial(attend, queries, cache, lengths, live_rows)
        mixed, context = mix_small(packed, weights, picks, steps, attention)
    else:
        steps = (z_near, z_far, x_steps, y_steps, core)
        mixed = mix_large(packed, weights, picks, steps)
        context, _ = attend(queries, cache, lengths, live_rows)
    return (context, mixed)


def solution(mesh):
    rows3 = P(AXES, None, None)
    rows2 = P(AXES, None)
    rows1 = P(AXES)
    return jax.shard_map(
        per_device,
        mesh=mesh,
        in_specs=(rows3, rows3, rows1, rows1, rows2, rows2, rows2, rows3, rows3, rows3),
        out_specs=(rows3, rows2),
        check_vma=False,
    )
```

```python
import functools

import jax
import jax.numpy as jnp
from jax import lax
from jax.experimental import pallas as pl
from jax.experimental.pallas import tpu as pltpu
from jax.sharding import PartitionSpec as P

LAT = 512
AXES = ("grp", "ep")
EXTRA = 128
BLOCKS = 4
TILE = 256
WIDE = 512
GROUPS = 4
NEAR_FLOPS = 4 * 10**9
VMEM_BYTES = 48 * 1024 * 1024
LARGE_BYTES = 16 * 1024 * 1024
SMALL_BYTES = 8 * 1024 * 1024
FIRST_BYTES = 39 * 1024 * 1024
whole = pl.BlockSpec(memory_space=pltpu.VMEM)

score_scale = 192.0 ** (-0.5)
neg_large = -1e30


def attend_kernel(lengths, live_rows, queries, channels, *refs):
    out, done = refs[-2:]
    count, heads, _ = queries.shape
    positions = lax.broadcasted_iota(jnp.int32, (heads, channels.shape[2]), 1)
    for request in range(count):
        scores = jnp.dot(
            queries[request], channels[request], preferred_element_type=jnp.float32
        )
        inside = positions < lengths[request]
        masked = jnp.where(inside, scores * score_scale, neg_large)
        highest = jnp.max(masked, axis=1, keepdims=True)
        powers = jnp.where(inside, jnp.exp(masked - highest), 0.0)
        totals = jnp.sum(powers, axis=1, keepdims=True)
        weights = (powers / totals).astype(jnp.bfloat16)
        context = lax.dot_general(
            weights,
            channels[request, :LAT, :],
            (((1,), (1,)), ((), ())),
            preferred_element_type=jnp.float32,
        )
        out[request] = jnp.where(request < live_rows[0], context, 0.0).astype(jnp.bfloat16)
    done[...] = jnp.zeros_like(done)


def attend(queries, cache, lengths, live_rows, after=()):
    count, heads, width = queries.shape
    positions = cache.shape[1]
    return pl.pallas_call(
        attend_kernel,
        out_shape=[
            jax.ShapeDtypeStruct((count, heads, LAT), jnp.bfloat16),
            jax.ShapeDtypeStruct((8, 128), jnp.float32),
        ],
        in_specs=[pl.BlockSpec(memory_space=pltpu.SMEM)] * 2
        + [whole] * 2
        + [pl.BlockSpec(memory_space=pl.ANY)] * len(after),
        out_specs=[whole] * 2,
        compiler_params=pltpu.CompilerParams(vmem_limit_bytes=SMALL_BYTES),
        cost_estimate=pl.CostEstimate(
            flops=4 * count * heads * width * positions,
            bytes_accessed=2 * count * positions * width,
            transcendentals=count * heads * positions,
        ),
        name="attend",
    )(lengths, live_rows, queries, jnp.swapaxes(cache, 1, 2), *after)


def bits_of(count):
    return [1 << i for i in range(count.bit_length() - 1)]


def swap(value, step):
    axis, bit = step
    size = lax.axis_size(axis)
    return lax.ppermute(value, axis, [(i, i ^ bit) for i in range(size)])


def across(value, first, second):
    axis = first[0]
    size = lax.axis_size(axis)
    return lax.ppermute(value, axis, [(i, i ^ first[1] ^ second[1]) for i in range(size)])


def spread(value, steps):
    for step in steps:
        value = jnp.concatenate([value, swap(value, step)], axis=0)
    return value


def others(value, steps):
    if len(steps) == 1:
        return swap(value, steps[0])
    return spread(value, steps)[value.shape[0] :]


def give_back(rest, steps, rows):
    terms = []
    for step in reversed(steps):
        keep = (rest.shape[0] + rows) // 2 - rows
        arrived = swap(rest[keep:], step)
        terms.append(arrived[:rows])
        if keep:
            rest = add_up(rest[:keep], [arrived[rows:]])
    return terms


def add_up(own, terms):
    total = own.astype(jnp.float32)
    for term in terms:
        total = total + term.astype(jnp.float32)
    return total.astype(jnp.bfloat16)


def pack_kernel(tokens, ids, gates, out):
    feature = tokens.shape[1]
    high = gates[...].astype(jnp.bfloat16).astype(jnp.float32)
    low = gates[...] - high
    stacked = jnp.concatenate([ids[...].astype(jnp.float32), high, low], axis=0)
    stacked = stacked.astype(jnp.bfloat16)
    row = lax.broadcasted_iota(jnp.int32, (stacked.shape[0], EXTRA), 0)
    column = lax.broadcasted_iota(jnp.int32, (stacked.shape[0], EXTRA), 1)
    place = jnp.where(row == column, 1.0, 0.0).astype(jnp.bfloat16)
    extra = lax.dot_general(
        stacked, place, (((0,), (0,)), ((), ())), preferred_element_type=jnp.float32
    )
    out[:, :feature] = tokens[...]
    out[:, feature:] = extra.astype(jnp.bfloat16)


def pack(tokens, ids, gates):
    return pl.pallas_call(
        pack_kernel,
        out_shape=jax.ShapeDtypeStruct((tokens.shape[0], tokens.shape[1] + EXTRA), jnp.bfloat16),
        in_specs=[whole] * 3,
        out_specs=whole,
        compiler_params=pltpu.CompilerParams(vmem_limit_bytes=SMALL_BYTES),
        name="pack",
    )(tokens, ids.T, gates.T)


def expert_index():
    return (lax.axis_index("grp") * lax.axis_size("ep") + lax.axis_index("ep")) // 2


def hidden_kernel(picks, own, other, extra_own, extra_other, w_gate, w_up, h_own, h_other, gate_sum, up_sum):
    step = pl.program_id(0)
    rows = jnp.concatenate([own[...], other[...]], axis=0)
    gate_part = jnp.dot(rows, w_gate[0], preferred_element_type=jnp.float32)
    up_part = jnp.dot(rows, w_up[0], preferred_element_type=jnp.float32)

    @pl.when(step == 0)
    def _():
        gate_sum[...] = gate_part
        up_sum[...] = up_part

    @pl.when(step > 0)
    def _():
        gate_sum[...] += gate_part
        up_sum[...] += up_part

    @pl.when(step == pl.num_programs(0) - 1)
    def _():
        count = own.shape[0]
        wanted = expert_index().astype(jnp.float32)
        for extra, out, at in ((extra_own, h_own, 0), (extra_other, h_other, count)):
            columns = extra[...].astype(jnp.float32)
            value = columns[:, picks : 2 * picks] + columns[:, 2 * picks : 3 * picks]
            share = jnp.sum(
                jnp.where(columns[:, :picks] == wanted, value, 0.0), axis=1, keepdims=True
            )
            gate_all = gate_sum[at : at + count, :]
            up_all = up_sum[at : at + count, :]
            hidden = gate_all / (1.0 + jnp.exp(-gate_all)) * up_all
            out[...] = (hidden * share).astype(jnp.bfloat16)


def hidden_of(own, other, w_gate, w_up, picks):
    count, width = own.shape
    _, feature, half = w_gate.shape
    depth = feature // BLOCKS
    rows_spec = pl.BlockSpec((count, depth), lambda k: (0, k))
    extra_spec = pl.BlockSpec((count, EXTRA), lambda k: (0, feature // EXTRA))
    weight_spec = pl.BlockSpec((1, depth, half), lambda k: (0, k, 0))
    out_spec = pl.BlockSpec((count, half), lambda k: (0, 0))
    return pl.pallas_call(
        functools.partial(hidden_kernel, picks),
        grid=(BLOCKS,),
        out_shape=[jax.ShapeDtypeStruct((count, half), jnp.bfloat16)] * 2,
        in_specs=[rows_spec] * 2 + [extra_spec] * 2 + [weight_spec] * 2,
        out_specs=[out_spec] * 2,
        scratch_shapes=[pltpu.VMEM((2 * count, half), jnp.float32)] * 2,
        compiler_params=pltpu.CompilerParams(vmem_limit_bytes=VMEM_BYTES),
        cost_estimate=pl.CostEstimate(
            flops=8 * count * feature * half,
            bytes_accessed=4 * feature * half + 4 * count * width,
            transcendentals=2 * count * half,
        ),
        name="hidden",
    )(own, other, own, other, w_gate, w_up)


def down_kernel(cuts, hidden, w_down, *refs):
    part = jnp.dot(hidden[...], w_down[0], preferred_element_type=jnp.float32)
    if len(refs) > len(cuts):
        part = part + refs[0][...].astype(jnp.float32)
        refs = refs[1:]
    at = 0
    for cut, out in zip(cuts, refs):
        out[...] = part[at : at + cut, :].astype(jnp.bfloat16)
        at += cut


def down_of(hidden, w_down, cuts, arrived=None):
    count, half = hidden.shape
    feature = w_down.shape[2]
    wide = feature // BLOCKS
    operands = [hidden, w_down]
    in_specs = [
        pl.BlockSpec((count, half), lambda n: (0, 0)),
        pl.BlockSpec((1, half, wide), lambda n: (0, 0, n)),
    ]
    if arrived is not None:
        operands.append(arrived)
        in_specs.append(pl.BlockSpec((count, wide), lambda n: (0, n)))
    return pl.pallas_call(
        functools.partial(down_kernel, cuts),
        grid=(BLOCKS,),
        out_shape=[jax.ShapeDtypeStruct((cut, feature), jnp.bfloat16) for cut in cuts],
        in_specs=in_specs,
        out_specs=[pl.BlockSpec((cut, wide), lambda n: (0, n)) for cut in cuts],
        compiler_params=pltpu.CompilerParams(vmem_limit_bytes=VMEM_BYTES),
        cost_estimate=pl.CostEstimate(
            flops=2 * count * feature * half,
            bytes_accessed=2 * feature * half + 4 * count * feature,
            transcendentals=0,
        ),
        name="down",
    )(*operands)


def combine_kernel(count, plans, *refs):
    outs = refs[len(refs) - len(plans) :]
    width = outs[0].shape[1]
    for plan, out in zip(plans, outs):
        at = 0
        for rows, terms in plan:
            if len(terms) == 1:
                index, start = terms[0]
                out[at : at + rows, :] = refs[index][start : start + rows, :]
            else:
                for left in range(0, width, WIDE):
                    span = slice(left, left + WIDE)
                    total = sum(
                        refs[index][start : start + rows, span].astype(jnp.float32)
                        for index, start in terms
                    )
                    out[at : at + rows, span] = total.astype(out.dtype)
            at += rows


def combine(inputs, plans, after=(), flops=0):
    width = inputs[0].shape[1]
    return pl.pallas_call(
        functools.partial(combine_kernel, len(inputs), plans),
        out_shape=[
            jax.ShapeDtypeStruct((sum(rows for rows, _ in plan), width), jnp.bfloat16)
            for plan in plans
        ],
        in_specs=[whole] * len(inputs) + [pl.BlockSpec(memory_space=pl.ANY)] * len(after),
        out_specs=[whole] * len(plans),
        compiler_params=pltpu.CompilerParams(vmem_limit_bytes=SMALL_BYTES),
        cost_estimate=pl.CostEstimate(
            flops=flops, bytes_accessed=4 * width * inputs[0].shape[0], transcendentals=0
        ),
        name="combine",
    )(*inputs, *after)


def expert_kernel(picks, after, own, other, w_gate, w_up, w_down, *refs):
    *outs, rows, hidden = refs[after:]
    expert_body(picks, own, other, w_gate, w_up, w_down, outs, rows, hidden)


def expert_body(
    picks, own, other, w_gate, w_up, w_down, outs, rows, hidden, ready=lambda number: None
):
    h_own, *outs = outs
    count, feature, half = own.shape[0], w_gate.shape[1], w_gate.shape[2]
    wanted = expert_index().astype(jnp.float32)
    shares = []
    for ref, at in ((own, 0), (other, count)):
        rows[at : at + count, :] = ref[:, :feature]
        columns = ref[:, feature:].astype(jnp.float32)
        value = columns[:, picks : 2 * picks] + columns[:, 2 * picks : 3 * picks]
        named = columns[:, :picks] == wanted
        shares.append(jnp.sum(jnp.where(named, value, 0.0), axis=1, keepdims=True))
    share = jnp.concatenate(shares, axis=0)
    for at in range(0, half, TILE):
        ready(at // TILE * 2)
        gate_part = jnp.dot(
            rows[...], w_gate[0, :, at : at + TILE], preferred_element_type=jnp.float32
        )
        ready(at // TILE * 2 + 1)
        up_part = jnp.dot(
            rows[...], w_up[0, :, at : at + TILE], preferred_element_type=jnp.float32
        )
        product = gate_part / (1.0 + jnp.exp(-gate_part)) * up_part * share
        hidden[:, at : at + TILE] = product.astype(jnp.bfloat16)
    h_own[...] = hidden[:count, :]
    wide = feature // BLOCKS
    for at in range(0, feature, wide):
        ready(half // TILE * 2 + at // wide)
        part = jnp.dot(
            hidden[count:, :], w_down[0, :, at : at + wide], preferred_element_type=jnp.float32
        ).astype(jnp.bfloat16)
        top = 0
        for out in outs:
            out[:, at : at + wide] = part[top : top + out.shape[0], :]
            top += out.shape[0]


def first_kernel(picks, own, other, gate_far, up_far, down_far, *refs):
    outs, (w_gate, w_up, w_down, rows, hidden, sems) = refs[:-6], refs[-6:]
    feature, half = w_gate.shape[1], w_gate.shape[2]
    depth = feature // BLOCKS
    groups = []

    def begin(pairs):
        copies = []
        for source, target, index in pairs:
            at = len(copies) + sum(len(group) for group in groups)
            copies.append(pltpu.make_async_copy(source.at[index], target.at[index], sems.at[at]))
        for copy in copies:
            copy.start()
        groups.append(copies)

    for left in range(0, half, TILE):
        for source, target in ((gate_far, w_gate), (up_far, w_up)):
            begin(
                (source, target, (0, pl.ds(top, depth), pl.ds(left, TILE)))
                for top in range(0, feature, depth)
            )
    for left in range(0, feature, feature // BLOCKS):
        begin([(down_far, w_down, (0, slice(None), pl.ds(left, feature // BLOCKS)))])

    def ready(number):
        for copy in groups[number]:
            copy.wait()

    expert_body(picks, own, other, w_gate, w_up, w_down, outs, rows, hidden, ready)


def first_of(own, other, w_gate, w_up, w_down, picks, cuts):
    count = own.shape[0]
    _, feature, half = w_gate.shape
    copies = 2 * (half // TILE) * BLOCKS + BLOCKS
    return pl.pallas_call(
        functools.partial(first_kernel, picks),
        out_shape=[jax.ShapeDtypeStruct((count, half), jnp.bfloat16)]
        + [jax.ShapeDtypeStruct((cut, feature), jnp.bfloat16) for cut in cuts]
        + [jax.ShapeDtypeStruct(w.shape, w.dtype) for w in (w_gate, w_up, w_down)],
        in_specs=[whole] * 2 + [pl.BlockSpec(memory_space=pl.ANY)] * 3,
        out_specs=[whole] * (len(cuts) + 4),
        scratch_shapes=[
            pltpu.VMEM((2 * count, feature), jnp.bfloat16),
            pltpu.VMEM((2 * count, half), jnp.bfloat16),
            pltpu.SemaphoreType.DMA((copies,)),
        ],
        compiler_params=pltpu.CompilerParams(vmem_limit_bytes=FIRST_BYTES),
        cost_estimate=pl.CostEstimate(
            flops=10 * count * feature * half,
            bytes_accessed=6 * feature * half,
            transcendentals=2 * count * half,
        ),
        name="first",
    )(own, other, w_gate, w_up, w_down)


def expert_of(own, other, w_gate, w_up, w_down, picks, cuts, after=()):
    count = own.shape[0]
    _, feature, half = w_gate.shape
    return pl.pallas_call(
        functools.partial(expert_kernel, picks, len(after)),
        out_shape=[jax.ShapeDtypeStruct((count, half), jnp.bfloat16)]
        + [jax.ShapeDtypeStruct((cut, feature), jnp.bfloat16) for cut in cuts],
        in_specs=[whole] * 5 + [pl.BlockSpec(memory_space=pl.ANY)] * len(after),
        out_specs=[whole] * (len(cuts) + 1),
        scratch_shapes=[
            pltpu.VMEM((2 * count, feature), jnp.bfloat16),
            pltpu.VMEM((2 * count, half), jnp.bfloat16),
        ],
        compiler_params=pltpu.CompilerParams(vmem_limit_bytes=LARGE_BYTES),
        cost_estimate=pl.CostEstimate(
            flops=10 * count * feature * half,
            bytes_accessed=2 * count * feature,
            transcendentals=2 * count * half,
        ),
        name="expert",
    )(own, other, w_gate, w_up, w_down, *after)


def sums_kernel(parts, hidden, w_down, *refs):
    arrived, outs = refs[:parts], refs[len(refs) - GROUPS :]
    feature = w_down.shape[2]
    cut = hidden.shape[0] // GROUPS
    places = [
        (term, top) for term in arrived for top in range(0, term.shape[0], cut)
    ]
    for column in range(0, feature, 2 * TILE):
        span = slice(column, column + 2 * TILE)
        part = jnp.dot(hidden[...], w_down[0, :, span], preferred_element_type=jnp.float32)
        for number, ((term, top), out) in enumerate(zip(places, outs)):
            own = part[number * cut : (number + 1) * cut, :]
            other = term[top : top + cut, span].astype(jnp.float32)
            out[:, span] = (own + other).astype(jnp.bfloat16)


def sums_of(hidden, w_down, arrived, after=()):
    count, half = hidden.shape
    feature = w_down.shape[2]
    return pl.pallas_call(
        functools.partial(sums_kernel, len(arrived)),
        out_shape=[jax.ShapeDtypeStruct((count // GROUPS, feature), jnp.bfloat16)] * GROUPS,
        in_specs=[whole] * (2 + len(arrived)) + [pl.BlockSpec(memory_space=pl.ANY)] * len(after),
        out_specs=[whole] * GROUPS,
        compiler_params=pltpu.CompilerParams(vmem_limit_bytes=SMALL_BYTES),
        cost_estimate=pl.CostEstimate(
            flops=2 * count * feature * half,
            bytes_accessed=2 * count * feature,
            transcendentals=0,
        ),
        name="sums",
    )(hidden, w_down, *arrived, *after)


def mix_large(packed, weights, picks, steps):
    w_gate, w_up, w_down = weights
    z_near, z_far, x_steps, y_steps, core = steps
    near = spread(packed, z_near)
    far = spread(swap(packed, z_far), z_near)
    near_x, near_y = others(near, x_steps), others(near, y_steps)
    far_x, far_y = others(far, x_steps), others(far, y_steps)
    near_xy, far_xy = others(near_x, y_steps), others(far_y, x_steps)
    early = [near, near_x, near_y, far, far_x, far_y]
    late = [near_xy, far_xy]
    early_cuts = [group.shape[0] for group in early]
    late_cuts = [group.shape[0] for group in late]
    early_own, late_own = jnp.concatenate(early, axis=0), jnp.concatenate(late, axis=0)
    early_other, late_other = swap(early_own, core), swap(late_own, core)
    early_h, early_h_other = hidden_of(early_own, early_other, w_gate, w_up, picks)
    late_h, late_h_other = hidden_of(late_own, late_other, w_gate, w_up, picks)
    (late_out,) = down_of(late_h_other, w_down, [late_h_other.shape[0]])
    late_in = swap(late_out, core)
    (early_out,) = down_of(early_h_other, w_down, [early_h_other.shape[0]])
    early_in = swap(early_out, core)
    near_xy, far_xy = down_of(late_h, w_down, late_cuts, late_in)
    near, near_x, near_y, far, far_x, far_y = down_of(early_h, w_down, early_cuts, early_in)
    rows, count = near.shape[0], packed.shape[0]
    near_x = add_up(near_x, give_back(near_xy, y_steps, near_x.shape[0]))
    far_y = add_up(far_y, give_back(far_xy, x_steps, far_y.shape[0]))
    far = add_up(far, give_back(far_x, x_steps, rows) + give_back(far_y, y_steps, rows))
    near = add_up(near, give_back(near_y, y_steps, rows) + give_back(near_x, x_steps, rows))
    far = add_up(far[:count], give_back(far[count:], z_near, count))
    return add_up(near[:count], give_back(near[count:], z_near, count) + [swap(far, z_far)])


def mix_small(packed, weights, picks, steps, attention):
    z_near, z_far, x, y, core = steps
    n = packed.shape[0]

    def rows_of(*segments):
        return [(count, [(index, start)]) for index, start, count in segments]

    from_near = swap(packed, z_near)
    from_far = swap(packed, z_far)
    (near,) = combine([packed, from_near], [rows_of((0, 0, n), (1, 0, n))])
    near_x, near_y = swap(near, x), swap(near, y)
    from_both = swap(from_far, z_near)
    first_own, far, way_x, way_y = combine(
        [near, near_x, near_y, from_far, from_both],
        [
            rows_of((0, 0, 2 * n), (1, 0, 2 * n), (2, 0, 2 * n), (3, 0, n), (4, 0, n)),
            rows_of((3, 0, n), (4, 0, n)),
            rows_of((3, 0, n), (4, 0, n), (2, n, n)),
            rows_of((3, 0, n), (4, 0, n), (1, 0, n)),
        ],
    )
    first_other = swap(first_own, core)
    far_x, far_y, far_xy = swap(way_x, x), swap(way_y, y), across(far, x, y)
    first_h, first_out, *weights = first_of(first_own, first_other, *weights, picks, [8 * n])
    w_down = weights[2]
    first_in = swap(first_out, core)
    (second_own,) = combine(
        [far_x, far_y, far_xy],
        [rows_of((0, 0, 2 * n), (1, 0, 2 * n), (2, 0, 2 * n), (1, 2 * n, n), (0, 2 * n, n))],
        [first_out],
    )
    second_other = swap(second_own, core)
    near, near_x, near_y, far = sums_of(first_h, w_down, [first_in])
    to_near = [swap(near_x, x), swap(near_y, y)]
    second_h, *second_out = expert_of(
        second_own, second_other, *weights, picks, [2 * n, 2 * n, 4 * n], [near]
    )
    second_in = [swap(part, core) for part in second_out]

    def all_of(terms, start, count=n):
        return [(count, [(index, start) for index in range(terms)])]

    (near,) = combine([near, *to_near], [all_of(3, 0, 2 * n)], flops=NEAR_FLOPS)
    far_x, far_y, far_xy, near_xy = sums_of(second_h, w_down, second_in, [near])

    to_far = [swap(far_x, x), swap(far_y, y), across(far_xy, x, y)]
    to_near = across(near_xy, x, y)
    context, done = attention([far_x])
    far_sum, both_sum = combine([far, *to_far], [all_of(4, 0), all_of(4, n)], [done])
    own_sum, near_sum = combine([near, to_near], [all_of(2, 0), all_of(2, n)], [far_sum])
    terms = [swap(far_sum, z_far), across(both_sum, z_far, z_near), swap(near_sum, z_near)]
    (mixed,) = combine([own_sum, *terms], [all_of(4, 0)])
    return mixed, context


def per_device(queries, cache, lengths, live_rows, tokens, ids, gates, w_gate, w_up, w_down):
    picks = ids.shape[1]
    grp_bits = bits_of(lax.axis_size("grp"))
    ep_bits = bits_of(lax.axis_size("ep"))
    core = ("grp", 1)
    z_near = [("grp", bit) for bit in reversed(grp_bits[1:-1])]
    z_far = ("grp", grp_bits[-1])
    x_steps = [("ep", bit) for bit in ep_bits[: len(ep_bits) // 2]]
    y_steps = [("ep", bit) for bit in ep_bits[len(ep_bits) // 2 :]]

    packed = pack(tokens, ids, gates)
    weights = (w_gate, w_up, w_down)
    if len(z_near) == len(x_steps) == len(y_steps) == 1:
        steps = (z_near[0], z_far, x_steps[0], y_steps[0], core)
        attention = functools.partial(attend, queries, cache, lengths, live_rows)
        mixed, context = mix_small(packed, weights, picks, steps, attention)
    else:
        steps = (z_near, z_far, x_steps, y_steps, core)
        mixed = mix_large(packed, weights, picks, steps)
        context, _ = attend(queries, cache, lengths, live_rows)
    return (context, mixed)


def solution(mesh):
    rows3 = P(AXES, None, None)
    rows2 = P(AXES, None)
    rows1 = P(AXES)
    return jax.shard_map(
        per_device,
        mesh=mesh,
        in_specs=(rows3, rows3, rows1, rows1, rows2, rows2, rows2, rows3, rows3, rows3),
        out_specs=(rows3, rows2),
        check_vma=False,
    )
```

```python
import functools

import jax
import jax.numpy as jnp
from jax import lax
from jax.experimental import pallas as pl
from jax.experimental.pallas import tpu as pltpu
from jax.sharding import PartitionSpec as P

LAT = 512
AXES = ("grp", "ep")
EXTRA = 128
BLOCKS = 4
TILE = 256
WIDE = 512
NEAR_FLOPS = 4 * 10**9
FAR_FLOPS = 4 * 10**9
VMEM_BYTES = 48 * 1024 * 1024
LARGE_BYTES = 16 * 1024 * 1024
SMALL_BYTES = 8 * 1024 * 1024
FIRST_BYTES = 39 * 1024 * 1024
whole = pl.BlockSpec(memory_space=pltpu.VMEM)

score_scale = 192.0 ** (-0.5)
neg_large = -1e30


def attend_kernel(lengths, live_rows, queries, channels, *refs):
    out, done = refs[-2:]
    count, heads, _ = queries.shape
    positions = lax.broadcasted_iota(jnp.int32, (heads, channels.shape[2]), 1)
    for request in range(count):
        scores = jnp.dot(
            queries[request], channels[request], preferred_element_type=jnp.float32
        )
        inside = positions < lengths[request]
        masked = jnp.where(inside, scores * score_scale, neg_large)
        highest = jnp.max(masked, axis=1, keepdims=True)
        powers = jnp.where(inside, jnp.exp(masked - highest), 0.0)
        totals = jnp.sum(powers, axis=1, keepdims=True)
        weights = (powers / totals).astype(jnp.bfloat16)
        context = lax.dot_general(
            weights,
            channels[request, :LAT, :],
            (((1,), (1,)), ((), ())),
            preferred_element_type=jnp.float32,
        )
        out[request] = jnp.where(request < live_rows[0], context, 0.0).astype(jnp.bfloat16)
    done[...] = jnp.zeros_like(done)


def attend(queries, cache, lengths, live_rows, after=()):
    count, heads, width = queries.shape
    positions = cache.shape[1]
    return pl.pallas_call(
        attend_kernel,
        out_shape=[
            jax.ShapeDtypeStruct((count, heads, LAT), jnp.bfloat16),
            jax.ShapeDtypeStruct((8, 128), jnp.float32),
        ],
        in_specs=[pl.BlockSpec(memory_space=pltpu.SMEM)] * 2
        + [whole] * 2
        + [pl.BlockSpec(memory_space=pl.ANY)] * len(after),
        out_specs=[whole] * 2,
        compiler_params=pltpu.CompilerParams(vmem_limit_bytes=SMALL_BYTES),
        cost_estimate=pl.CostEstimate(
            flops=4 * count * heads * width * positions,
            bytes_accessed=2 * count * positions * width,
            transcendentals=count * heads * positions,
        ),
        name="attend",
    )(lengths, live_rows, queries, jnp.swapaxes(cache, 1, 2), *after)


def bits_of(count):
    return [1 << i for i in range(count.bit_length() - 1)]


def swap(value, step):
    axis, bit = step
    size = lax.axis_size(axis)
    return lax.ppermute(value, axis, [(i, i ^ bit) for i in range(size)])


def across(value, first, second):
    axis = first[0]
    size = lax.axis_size(axis)
    return lax.ppermute(value, axis, [(i, i ^ first[1] ^ second[1]) for i in range(size)])


def spread(value, steps):
    for step in steps:
        value = jnp.concatenate([value, swap(value, step)], axis=0)
    return value


def others(value, steps):
    if len(steps) == 1:
        return swap(value, steps[0])
    return spread(value, steps)[value.shape[0] :]


def give_back(rest, steps, rows):
    terms = []
    for step in reversed(steps):
        keep = (rest.shape[0] + rows) // 2 - rows
        arrived = swap(rest[keep:], step)
        terms.append(arrived[:rows])
        if keep:
            rest = add_up(rest[:keep], [arrived[rows:]])
    return terms


def add_up(own, terms):
    total = own.astype(jnp.float32)
    for term in terms:
        total = total + term.astype(jnp.float32)
    return total.astype(jnp.bfloat16)


def pack_kernel(tokens, chosen, out):
    feature = tokens.shape[1]
    picks = chosen.shape[0] // 2
    gates = chosen[picks:, :]
    high = gates.astype(jnp.bfloat16).astype(jnp.float32)
    stacked = jnp.concatenate([chosen[:picks, :], high, gates - high], axis=0)
    stacked = stacked.astype(jnp.bfloat16)
    row = lax.broadcasted_iota(jnp.int32, (stacked.shape[0], EXTRA), 0)
    column = lax.broadcasted_iota(jnp.int32, (stacked.shape[0], EXTRA), 1)
    place = jnp.where(row == column, 1.0, 0.0).astype(jnp.bfloat16)
    extra = lax.dot_general(
        stacked, place, (((0,), (0,)), ((), ())), preferred_element_type=jnp.float32
    )
    out[:, :feature] = tokens[...]
    out[:, feature:] = extra.astype(jnp.bfloat16)


def pack(tokens, ids, gates):
    return pl.pallas_call(
        pack_kernel,
        out_shape=jax.ShapeDtypeStruct((tokens.shape[0], tokens.shape[1] + EXTRA), jnp.bfloat16),
        in_specs=[whole] * 2,
        out_specs=whole,
        compiler_params=pltpu.CompilerParams(vmem_limit_bytes=SMALL_BYTES),
        name="pack",
    )(tokens, jnp.concatenate([ids.T.astype(jnp.float32), gates.T], axis=0))


def expert_index():
    return (lax.axis_index("grp") * lax.axis_size("ep") + lax.axis_index("ep")) // 2


def hidden_kernel(picks, own, other, extra_own, extra_other, w_gate, w_up, h_own, h_other, gate_sum, up_sum):
    step = pl.program_id(0)
    rows = jnp.concatenate([own[...], other[...]], axis=0)
    gate_part = jnp.dot(rows, w_gate[0], preferred_element_type=jnp.float32)
    up_part = jnp.dot(rows, w_up[0], preferred_element_type=jnp.float32)

    @pl.when(step == 0)
    def _():
        gate_sum[...] = gate_part
        up_sum[...] = up_part

    @pl.when(step > 0)
    def _():
        gate_sum[...] += gate_part
        up_sum[...] += up_part

    @pl.when(step == pl.num_programs(0) - 1)
    def _():
        count = own.shape[0]
        wanted = expert_index().astype(jnp.float32)
        for extra, out, at in ((extra_own, h_own, 0), (extra_other, h_other, count)):
            columns = extra[...].astype(jnp.float32)
            value = columns[:, picks : 2 * picks] + columns[:, 2 * picks : 3 * picks]
            share = jnp.sum(
                jnp.where(columns[:, :picks] == wanted, value, 0.0), axis=1, keepdims=True
            )
            gate_all = gate_sum[at : at + count, :]
            up_all = up_sum[at : at + count, :]
            hidden = gate_all / (1.0 + jnp.exp(-gate_all)) * up_all
            out[...] = (hidden * share).astype(jnp.bfloat16)


def hidden_of(own, other, w_gate, w_up, picks):
    count, width = own.shape
    _, feature, half = w_gate.shape
    depth = feature // BLOCKS
    rows_spec = pl.BlockSpec((count, depth), lambda k: (0, k))
    extra_spec = pl.BlockSpec((count, EXTRA), lambda k: (0, feature // EXTRA))
    weight_spec = pl.BlockSpec((1, depth, half), lambda k: (0, k, 0))
    out_spec = pl.BlockSpec((count, half), lambda k: (0, 0))
    return pl.pallas_call(
        functools.partial(hidden_kernel, picks),
        grid=(BLOCKS,),
        out_shape=[jax.ShapeDtypeStruct((count, half), jnp.bfloat16)] * 2,
        in_specs=[rows_spec] * 2 + [extra_spec] * 2 + [weight_spec] * 2,
        out_specs=[out_spec] * 2,
        scratch_shapes=[pltpu.VMEM((2 * count, half), jnp.float32)] * 2,
        compiler_params=pltpu.CompilerParams(vmem_limit_bytes=VMEM_BYTES),
        cost_estimate=pl.CostEstimate(
            flops=8 * count * feature * half,
            bytes_accessed=4 * feature * half + 4 * count * width,
            transcendentals=2 * count * half,
        ),
        name="hidden",
    )(own, other, own, other, w_gate, w_up)


def down_kernel(cuts, hidden, w_down, *refs):
    part = jnp.dot(hidden[...], w_down[0], preferred_element_type=jnp.float32)
    if len(refs) > len(cuts):
        part = part + refs[0][...].astype(jnp.float32)
        refs = refs[1:]
    at = 0
    for cut, out in zip(cuts, refs):
        out[...] = part[at : at + cut, :].astype(jnp.bfloat16)
        at += cut


def down_of(hidden, w_down, cuts, arrived=None):
    count, half = hidden.shape
    feature = w_down.shape[2]
    wide = feature // BLOCKS
    operands = [hidden, w_down]
    in_specs = [
        pl.BlockSpec((count, half), lambda n: (0, 0)),
        pl.BlockSpec((1, half, wide), lambda n: (0, 0, n)),
    ]
    if arrived is not None:
        operands.append(arrived)
        in_specs.append(pl.BlockSpec((count, wide), lambda n: (0, n)))
    return pl.pallas_call(
        functools.partial(down_kernel, cuts),
        grid=(BLOCKS,),
        out_shape=[jax.ShapeDtypeStruct((cut, feature), jnp.bfloat16) for cut in cuts],
        in_specs=in_specs,
        out_specs=[pl.BlockSpec((cut, wide), lambda n: (0, n)) for cut in cuts],
        compiler_params=pltpu.CompilerParams(vmem_limit_bytes=VMEM_BYTES),
        cost_estimate=pl.CostEstimate(
            flops=2 * count * feature * half,
            bytes_accessed=2 * feature * half + 4 * count * feature,
            transcendentals=0,
        ),
        name="down",
    )(*operands)


def combine_kernel(count, plans, *refs):
    outs = refs[len(refs) - len(plans) :]
    width = outs[0].shape[1]
    for plan, out in zip(plans, outs):
        at = 0
        for rows, terms in plan:
            if len(terms) == 1:
                index, start = terms[0]
                out[at : at + rows, :] = refs[index][start : start + rows, :]
            else:
                for left in range(0, width, WIDE):
                    span = slice(left, left + WIDE)
                    total = sum(
                        refs[index][start : start + rows, span].astype(jnp.float32)
                        for index, start in terms
                    )
                    out[at : at + rows, span] = total.astype(out.dtype)
            at += rows


def combine(inputs, plans, after=(), flops=0):
    width = inputs[0].shape[1]
    return pl.pallas_call(
        functools.partial(combine_kernel, len(inputs), plans),
        out_shape=[
            jax.ShapeDtypeStruct((sum(rows for rows, _ in plan), width), jnp.bfloat16)
            for plan in plans
        ],
        in_specs=[whole] * len(inputs) + [pl.BlockSpec(memory_space=pl.ANY)] * len(after),
        out_specs=[whole] * len(plans),
        compiler_params=pltpu.CompilerParams(vmem_limit_bytes=SMALL_BYTES),
        cost_estimate=pl.CostEstimate(
            flops=flops, bytes_accessed=4 * width * inputs[0].shape[0], transcendentals=0
        ),
        name="combine",
    )(*inputs, *after)


def expert_kernel(picks, after, own, other, w_gate, w_up, w_down, *refs):
    *outs, rows, hidden = refs[after:]
    expert_body(picks, own, other, w_gate, w_up, w_down, outs, rows, hidden)


def expert_body(
    picks, own, other, w_gate, w_up, w_down, outs, rows, hidden, ready=lambda number: None
):
    h_own, *outs = outs
    count, feature, half = own.shape[0], w_gate.shape[1], w_gate.shape[2]
    wanted = expert_index().astype(jnp.float32)
    shares = []
    for ref, at in ((own, 0), (other, count)):
        rows[at : at + count, :] = ref[:, :feature]
        columns = ref[:, feature:].astype(jnp.float32)
        value = columns[:, picks : 2 * picks] + columns[:, 2 * picks : 3 * picks]
        named = columns[:, :picks] == wanted
        shares.append(jnp.sum(jnp.where(named, value, 0.0), axis=1, keepdims=True))
    share = jnp.concatenate(shares, axis=0)
    for at in range(0, half, TILE):
        ready(at // TILE * 2)
        gate_part = jnp.dot(
            rows[...], w_gate[0, :, at : at + TILE], preferred_element_type=jnp.float32
        )
        ready(at // TILE * 2 + 1)
        up_part = jnp.dot(
            rows[...], w_up[0, :, at : at + TILE], preferred_element_type=jnp.float32
        )
        product = gate_part / (1.0 + jnp.exp(-gate_part)) * up_part * share
        hidden[:, at : at + TILE] = product.astype(jnp.bfloat16)
    h_own[...] = hidden[:count, :]
    wide = feature // BLOCKS
    for at in range(0, feature, wide):
        ready(half // TILE * 2 + at // wide)
        part = jnp.dot(
            hidden[count:, :], w_down[0, :, at : at + wide], preferred_element_type=jnp.float32
        ).astype(jnp.bfloat16)
        top = 0
        for out in outs:
            out[:, at : at + wide] = part[top : top + out.shape[0], :]
            top += out.shape[0]


def first_kernel(picks, own, other, gate_far, up_far, down_far, *refs):
    outs, (w_gate, w_up, w_down, rows, hidden, sems) = refs[:-6], refs[-6:]
    feature, half = w_gate.shape[1], w_gate.shape[2]
    depth = feature // BLOCKS
    groups = []

    def begin(pairs):
        copies = []
        for source, target, index in pairs:
            at = len(copies) + sum(len(group) for group in groups)
            copies.append(pltpu.make_async_copy(source.at[index], target.at[index], sems.at[at]))
        for copy in copies:
            copy.start()
        groups.append(copies)

    for left in range(0, half, TILE):
        for source, target in ((gate_far, w_gate), (up_far, w_up)):
            begin(
                (source, target, (0, pl.ds(top, depth), pl.ds(left, TILE)))
                for top in range(0, feature, depth)
            )
    for left in range(0, feature, feature // BLOCKS):
        begin([(down_far, w_down, (0, slice(None), pl.ds(left, feature // BLOCKS)))])

    def ready(number):
        for copy in groups[number]:
            copy.wait()

    expert_body(picks, own, other, w_gate, w_up, w_down, outs, rows, hidden, ready)


def first_of(own, other, w_gate, w_up, w_down, picks, cuts):
    count = own.shape[0]
    _, feature, half = w_gate.shape
    copies = 2 * (half // TILE) * BLOCKS + BLOCKS
    return pl.pallas_call(
        functools.partial(first_kernel, picks),
        out_shape=[jax.ShapeDtypeStruct((count, half), jnp.bfloat16)]
        + [jax.ShapeDtypeStruct((cut, feature), jnp.bfloat16) for cut in cuts]
        + [jax.ShapeDtypeStruct(w.shape, w.dtype) for w in (w_gate, w_up, w_down)],
        in_specs=[whole] * 2 + [pl.BlockSpec(memory_space=pl.ANY)] * 3,
        out_specs=[whole] * (len(cuts) + 4),
        scratch_shapes=[
            pltpu.VMEM((2 * count, feature), jnp.bfloat16),
            pltpu.VMEM((2 * count, half), jnp.bfloat16),
            pltpu.SemaphoreType.DMA((copies,)),
        ],
        compiler_params=pltpu.CompilerParams(vmem_limit_bytes=FIRST_BYTES),
        cost_estimate=pl.CostEstimate(
            flops=10 * count * feature * half,
            bytes_accessed=6 * feature * half,
            transcendentals=2 * count * half,
        ),
        name="first",
    )(own, other, w_gate, w_up, w_down)


def expert_of(own, other, w_gate, w_up, w_down, picks, cuts, after=()):
    count = own.shape[0]
    _, feature, half = w_gate.shape
    return pl.pallas_call(
        functools.partial(expert_kernel, picks, len(after)),
        out_shape=[jax.ShapeDtypeStruct((count, half), jnp.bfloat16)]
        + [jax.ShapeDtypeStruct((cut, feature), jnp.bfloat16) for cut in cuts],
        in_specs=[whole] * 5 + [pl.BlockSpec(memory_space=pl.ANY)] * len(after),
        out_specs=[whole] * (len(cuts) + 1),
        scratch_shapes=[
            pltpu.VMEM((2 * count, feature), jnp.bfloat16),
            pltpu.VMEM((2 * count, half), jnp.bfloat16),
        ],
        compiler_params=pltpu.CompilerParams(vmem_limit_bytes=LARGE_BYTES),
        cost_estimate=pl.CostEstimate(
            flops=10 * count * feature * half,
            bytes_accessed=2 * count * feature,
            transcendentals=2 * count * half,
        ),
        name="expert",
    )(own, other, w_gate, w_up, w_down, *after)


def sums_kernel(parts, groups, hidden, w_down, *refs):
    arrived, outs = refs[:parts], refs[len(refs) - groups :]
    feature = w_down.shape[2]
    cut = hidden.shape[0] // groups
    places = [(term, top) for term in arrived for top in range(0, term.shape[0], cut)]
    for column in range(0, feature, 2 * TILE):
        span = slice(column, column + 2 * TILE)
        part = jnp.dot(hidden[...], w_down[0, :, span], preferred_element_type=jnp.float32)
        for number, ((term, top), out) in enumerate(zip(places, outs)):
            own = part[number * cut : (number + 1) * cut, :]
            other = term[top : top + cut, span].astype(jnp.float32)
            out[:, span] = (own + other).astype(jnp.bfloat16)


def sums_of(hidden, w_down, arrived, cut, after=()):
    count, half = hidden.shape
    feature = w_down.shape[2]
    groups = count // cut
    return pl.pallas_call(
        functools.partial(sums_kernel, len(arrived), groups),
        out_shape=[jax.ShapeDtypeStruct((cut, feature), jnp.bfloat16)] * groups,
        in_specs=[whole] * (2 + len(arrived)) + [pl.BlockSpec(memory_space=pl.ANY)] * len(after),
        out_specs=[whole] * groups,
        compiler_params=pltpu.CompilerParams(vmem_limit_bytes=SMALL_BYTES),
        cost_estimate=pl.CostEstimate(
            flops=2 * count * feature * half,
            bytes_accessed=2 * count * feature,
            transcendentals=0,
        ),
        name="sums",
    )(hidden, w_down, *arrived, *after)


def mix_large(packed, weights, picks, steps):
    w_gate, w_up, w_down = weights
    z_near, z_far, x_steps, y_steps, core = steps
    near = spread(packed, z_near)
    far = spread(swap(packed, z_far), z_near)
    near_x, near_y = others(near, x_steps), others(near, y_steps)
    far_x, far_y = others(far, x_steps), others(far, y_steps)
    near_xy, far_xy = others(near_x, y_steps), others(far_y, x_steps)
    early = [near, near_x, near_y, far, far_x, far_y]
    late = [near_xy, far_xy]
    early_cuts = [group.shape[0] for group in early]
    late_cuts = [group.shape[0] for group in late]
    early_own, late_own = jnp.concatenate(early, axis=0), jnp.concatenate(late, axis=0)
    early_other, late_other = swap(early_own, core), swap(late_own, core)
    early_h, early_h_other = hidden_of(early_own, early_other, w_gate, w_up, picks)
    late_h, late_h_other = hidden_of(late_own, late_other, w_gate, w_up, picks)
    (late_out,) = down_of(late_h_other, w_down, [late_h_other.shape[0]])
    late_in = swap(late_out, core)
    (early_out,) = down_of(early_h_other, w_down, [early_h_other.shape[0]])
    early_in = swap(early_out, core)
    near_xy, far_xy = down_of(late_h, w_down, late_cuts, late_in)
    near, near_x, near_y, far, far_x, far_y = down_of(early_h, w_down, early_cuts, early_in)
    rows, count = near.shape[0], packed.shape[0]
    near_x = add_up(near_x, give_back(near_xy, y_steps, near_x.shape[0]))
    far_y = add_up(far_y, give_back(far_xy, x_steps, far_y.shape[0]))
    far = add_up(far, give_back(far_x, x_steps, rows) + give_back(far_y, y_steps, rows))
    near = add_up(near, give_back(near_y, y_steps, rows) + give_back(near_x, x_steps, rows))
    far = add_up(far[:count], give_back(far[count:], z_near, count))
    return add_up(near[:count], give_back(near[count:], z_near, count) + [swap(far, z_far)])


def mix_small(packed, weights, picks, steps, attention):
    z_near, z_far, x, y, core = steps
    n = packed.shape[0]

    def rows_of(*segments):
        return [(count, [(index, start)]) for index, start, count in segments]

    from_near = swap(packed, z_near)
    from_far = swap(packed, z_far)
    (near,) = combine([packed, from_near], [rows_of((0, 0, n), (1, 0, n))])
    near_x, near_y = swap(near, x), swap(near, y)
    from_both = swap(from_far, z_near)
    first_own, far, way_x, way_y = combine(
        [near, near_x, near_y, from_far, from_both],
        [
            rows_of((0, 0, 2 * n), (1, 0, 2 * n), (2, 0, 2 * n), (3, 0, n), (4, 0, n)),
            rows_of((3, 0, n), (4, 0, n)),
            rows_of((3, 0, n), (4, 0, n), (2, n, n)),
            rows_of((3, 0, n), (4, 0, n), (1, 0, n)),
        ],
    )
    first_other = swap(first_own, core)
    far_xy, far_x, far_y = across(far, x, y), swap(way_x, x), swap(way_y, y)
    first_h, first_out, *weights = first_of(first_own, first_other, *weights, picks, [8 * n])
    w_down = weights[2]
    first_in = swap(first_out, core)
    (second_own,) = combine(
        [far_x, far_y, far_xy],
        [rows_of((0, 0, 2 * n), (1, 0, 2 * n), (2, 0, 2 * n), (1, 2 * n, n), (0, 2 * n, n))],
        [first_out],
    )
    second_other = swap(second_own, core)
    near, near_x, near_y, far = sums_of(first_h, w_down, [first_in], 2 * n)
    to_near = [swap(near_x, x), swap(near_y, y)]
    second_h, *second_out = expert_of(
        second_own, second_other, *weights, picks, [2 * n, 2 * n, 4 * n], [near]
    )
    second_in = [swap(part, core) for part in second_out]

    def all_of(terms, start, count=n):
        return [(count, [(index, start) for index in range(terms)])]

    (near,) = combine([near, *to_near], [all_of(3, 0, 2 * n)], flops=NEAR_FLOPS)
    far_x, far_y, far_xy, near_xy = sums_of(second_h, w_down, second_in, 2 * n, [near])

    to_far = [across(far_xy, x, y), swap(far_x, x), swap(far_y, y)]
    context, done = attention([far_x])
    (near_xy,) = combine([near_xy], [rows_of((0, 0, 2 * n))], [done])
    to_near = across(near_xy, x, y)
    far_sum, both_sum = combine([far, *to_far], [all_of(4, 0), all_of(4, n)], [near_xy])
    own_sum, near_sum = combine([near, to_near], [all_of(2, 0), all_of(2, n)], [far_sum])
    (far_sum,) = combine(
        [swap(far_sum, z_far), across(both_sum, z_far, z_near)], [all_of(2, 0)], flops=FAR_FLOPS
    )
    (mixed,) = combine([own_sum, far_sum, swap(near_sum, z_near)], [all_of(3, 0)])
    return mixed, context


def per_device(queries, cache, lengths, live_rows, tokens, ids, gates, w_gate, w_up, w_down):
    picks = ids.shape[1]
    grp_bits = bits_of(lax.axis_size("grp"))
    ep_bits = bits_of(lax.axis_size("ep"))
    core = ("grp", 1)
    z_near = [("grp", bit) for bit in reversed(grp_bits[1:-1])]
    z_far = ("grp", grp_bits[-1])
    x_steps = [("ep", bit) for bit in ep_bits[: len(ep_bits) // 2]]
    y_steps = [("ep", bit) for bit in ep_bits[len(ep_bits) // 2 :]]

    packed = pack(tokens, ids, gates)
    weights = (w_gate, w_up, w_down)
    if len(z_near) == len(x_steps) == len(y_steps) == 1:
        steps = (z_near[0], z_far, x_steps[0], y_steps[0], core)
        attention = functools.partial(attend, queries, cache, lengths, live_rows)
        mixed, context = mix_small(packed, weights, picks, steps, attention)
    else:
        steps = (z_near, z_far, x_steps, y_steps, core)
        mixed = mix_large(packed, weights, picks, steps)
        context, _ = attend(queries, cache, lengths, live_rows)
    return (context, mixed)


def solution(mesh):
    rows3 = P(AXES, None, None)
    rows2 = P(AXES, None)
    rows1 = P(AXES)
    return jax.shard_map(
        per_device,
        mesh=mesh,
        in_specs=(rows3, rows3, rows1, rows1, rows2, rows2, rows2, rows3, rows3, rows3),
        out_specs=(rows3, rows2),
        check_vma=False,
    )
```

```python
import functools

import jax
import jax.numpy as jnp
from jax import lax
from jax.experimental import pallas as pl
from jax.experimental.pallas import tpu as pltpu
from jax.sharding import PartitionSpec as P

LAT = 512
AXES = ("grp", "ep")
EXTRA = 128
BLOCKS = 4
TILE = 256
WIDE = 512
NEAR_FLOPS = 4 * 10**9
FAR_FLOPS = 4 * 10**9
VMEM_BYTES = 48 * 1024 * 1024
LARGE_BYTES = 16 * 1024 * 1024
SMALL_BYTES = 8 * 1024 * 1024
FIRST_BYTES = 39 * 1024 * 1024
whole = pl.BlockSpec(memory_space=pltpu.VMEM)

score_scale = 192.0 ** (-0.5)
neg_large = -1e30


def attend_kernel(lengths, live_rows, queries, channels, *refs):
    out, done = refs[-2:]
    count, heads, _ = queries.shape
    positions = lax.broadcasted_iota(jnp.int32, (heads, channels.shape[2]), 1)
    for request in range(count):
        scores = jnp.dot(
            queries[request], channels[request], preferred_element_type=jnp.float32
        )
        inside = positions < lengths[request]
        masked = jnp.where(inside, scores * score_scale, neg_large)
        highest = jnp.max(masked, axis=1, keepdims=True)
        powers = jnp.where(inside, jnp.exp(masked - highest), 0.0)
        totals = jnp.sum(powers, axis=1, keepdims=True)
        weights = (powers / totals).astype(jnp.bfloat16)
        context = lax.dot_general(
            weights,
            channels[request, :LAT, :],
            (((1,), (1,)), ((), ())),
            preferred_element_type=jnp.float32,
        )
        out[request] = jnp.where(request < live_rows[0], context, 0.0).astype(jnp.bfloat16)
    done[...] = jnp.zeros_like(done)


def attend(queries, cache, lengths, live_rows, after=()):
    count, heads, width = queries.shape
    positions = cache.shape[1]
    return pl.pallas_call(
        attend_kernel,
        out_shape=[
            jax.ShapeDtypeStruct((count, heads, LAT), jnp.bfloat16),
            jax.ShapeDtypeStruct((8, 128), jnp.float32),
        ],
        in_specs=[pl.BlockSpec(memory_space=pltpu.SMEM)] * 2
        + [whole] * 2
        + [pl.BlockSpec(memory_space=pl.ANY)] * len(after),
        out_specs=[whole] * 2,
        compiler_params=pltpu.CompilerParams(vmem_limit_bytes=SMALL_BYTES),
        cost_estimate=pl.CostEstimate(
            flops=4 * count * heads * width * positions,
            bytes_accessed=2 * count * positions * width,
            transcendentals=count * heads * positions,
        ),
        name="attend",
    )(lengths, live_rows, queries, jnp.swapaxes(cache, 1, 2), *after)


def bits_of(count):
    return [1 << i for i in range(count.bit_length() - 1)]


def swap(value, step):
    axis, bit = step
    size = lax.axis_size(axis)
    return lax.ppermute(value, axis, [(i, i ^ bit) for i in range(size)])


def across(value, first, second):
    axis = first[0]
    size = lax.axis_size(axis)
    return lax.ppermute(value, axis, [(i, i ^ first[1] ^ second[1]) for i in range(size)])


def spread(value, steps):
    for step in steps:
        value = jnp.concatenate([value, swap(value, step)], axis=0)
    return value


def others(value, steps):
    if len(steps) == 1:
        return swap(value, steps[0])
    return spread(value, steps)[value.shape[0] :]


def give_back(rest, steps, rows):
    terms = []
    for step in reversed(steps):
        keep = (rest.shape[0] + rows) // 2 - rows
        arrived = swap(rest[keep:], step)
        terms.append(arrived[:rows])
        if keep:
            rest = add_up(rest[:keep], [arrived[rows:]])
    return terms


def add_up(own, terms):
    total = own.astype(jnp.float32)
    for term in terms:
        total = total + term.astype(jnp.float32)
    return total.astype(jnp.bfloat16)


def pack_kernel(tokens, chosen, out):
    feature = tokens.shape[1]
    picks = chosen.shape[0] // 2
    gates = chosen[picks:, :]
    high = gates.astype(jnp.bfloat16).astype(jnp.float32)
    stacked = jnp.concatenate([chosen[:picks, :], high, gates - high], axis=0)
    stacked = stacked.astype(jnp.bfloat16)
    row = lax.broadcasted_iota(jnp.int32, (stacked.shape[0], EXTRA), 0)
    column = lax.broadcasted_iota(jnp.int32, (stacked.shape[0], EXTRA), 1)
    place = jnp.where(row == column, 1.0, 0.0).astype(jnp.bfloat16)
    extra = lax.dot_general(
        stacked, place, (((0,), (0,)), ((), ())), preferred_element_type=jnp.float32
    )
    out[:, :feature] = tokens[...]
    out[:, feature:] = extra.astype(jnp.bfloat16)


def pack(tokens, ids, gates):
    return pl.pallas_call(
        pack_kernel,
        out_shape=jax.ShapeDtypeStruct((tokens.shape[0], tokens.shape[1] + EXTRA), jnp.bfloat16),
        in_specs=[whole] * 2,
        out_specs=whole,
        compiler_params=pltpu.CompilerParams(vmem_limit_bytes=SMALL_BYTES),
        name="pack",
    )(tokens, jnp.concatenate([ids.T.astype(jnp.float32), gates.T], axis=0))


def expert_index():
    return (lax.axis_index("grp") * lax.axis_size("ep") + lax.axis_index("ep")) // 2


def hidden_kernel(picks, own, other, extra_own, extra_other, w_gate, w_up, h_own, h_other, gate_sum, up_sum):
    step = pl.program_id(0)
    rows = jnp.concatenate([own[...], other[...]], axis=0)
    gate_part = jnp.dot(rows, w_gate[0], preferred_element_type=jnp.float32)
    up_part = jnp.dot(rows, w_up[0], preferred_element_type=jnp.float32)

    @pl.when(step == 0)
    def _():
        gate_sum[...] = gate_part
        up_sum[...] = up_part

    @pl.when(step > 0)
    def _():
        gate_sum[...] += gate_part
        up_sum[...] += up_part

    @pl.when(step == pl.num_programs(0) - 1)
    def _():
        count = own.shape[0]
        wanted = expert_index().astype(jnp.float32)
        for extra, out, at in ((extra_own, h_own, 0), (extra_other, h_other, count)):
            columns = extra[...].astype(jnp.float32)
            value = columns[:, picks : 2 * picks] + columns[:, 2 * picks : 3 * picks]
            share = jnp.sum(
                jnp.where(columns[:, :picks] == wanted, value, 0.0), axis=1, keepdims=True
            )
            gate_all = gate_sum[at : at + count, :]
            up_all = up_sum[at : at + count, :]
            hidden = gate_all / (1.0 + jnp.exp(-gate_all)) * up_all
            out[...] = (hidden * share).astype(jnp.bfloat16)


def hidden_of(own, other, w_gate, w_up, picks):
    count, width = own.shape
    _, feature, half = w_gate.shape
    depth = feature // BLOCKS
    rows_spec = pl.BlockSpec((count, depth), lambda k: (0, k))
    extra_spec = pl.BlockSpec((count, EXTRA), lambda k: (0, feature // EXTRA))
    weight_spec = pl.BlockSpec((1, depth, half), lambda k: (0, k, 0))
    out_spec = pl.BlockSpec((count, half), lambda k: (0, 0))
    return pl.pallas_call(
        functools.partial(hidden_kernel, picks),
        grid=(BLOCKS,),
        out_shape=[jax.ShapeDtypeStruct((count, half), jnp.bfloat16)] * 2,
        in_specs=[rows_spec] * 2 + [extra_spec] * 2 + [weight_spec] * 2,
        out_specs=[out_spec] * 2,
        scratch_shapes=[pltpu.VMEM((2 * count, half), jnp.float32)] * 2,
        compiler_params=pltpu.CompilerParams(vmem_limit_bytes=VMEM_BYTES),
        cost_estimate=pl.CostEstimate(
            flops=8 * count * feature * half,
            bytes_accessed=4 * feature * half + 4 * count * width,
            transcendentals=2 * count * half,
        ),
        name="hidden",
    )(own, other, own, other, w_gate, w_up)


def down_kernel(cuts, hidden, w_down, *refs):
    part = jnp.dot(hidden[...], w_down[0], preferred_element_type=jnp.float32)
    if len(refs) > len(cuts):
        part = part + refs[0][...].astype(jnp.float32)
        refs = refs[1:]
    at = 0
    for cut, out in zip(cuts, refs):
        out[...] = part[at : at + cut, :].astype(jnp.bfloat16)
        at += cut


def down_of(hidden, w_down, cuts, arrived=None):
    count, half = hidden.shape
    feature = w_down.shape[2]
    wide = feature // BLOCKS
    operands = [hidden, w_down]
    in_specs = [
        pl.BlockSpec((count, half), lambda n: (0, 0)),
        pl.BlockSpec((1, half, wide), lambda n: (0, 0, n)),
    ]
    if arrived is not None:
        operands.append(arrived)
        in_specs.append(pl.BlockSpec((count, wide), lambda n: (0, n)))
    return pl.pallas_call(
        functools.partial(down_kernel, cuts),
        grid=(BLOCKS,),
        out_shape=[jax.ShapeDtypeStruct((cut, feature), jnp.bfloat16) for cut in cuts],
        in_specs=in_specs,
        out_specs=[pl.BlockSpec((cut, wide), lambda n: (0, n)) for cut in cuts],
        compiler_params=pltpu.CompilerParams(vmem_limit_bytes=VMEM_BYTES),
        cost_estimate=pl.CostEstimate(
            flops=2 * count * feature * half,
            bytes_accessed=2 * feature * half + 4 * count * feature,
            transcendentals=0,
        ),
        name="down",
    )(*operands)


def combine_kernel(count, plans, *refs):
    outs = refs[len(refs) - len(plans) :]
    width = outs[0].shape[1]
    for plan, out in zip(plans, outs):
        at = 0
        for rows, terms in plan:
            if len(terms) == 1:
                index, start = terms[0]
                out[at : at + rows, :] = refs[index][start : start + rows, :]
            else:
                for left in range(0, width, WIDE):
                    span = slice(left, left + WIDE)
                    total = sum(
                        refs[index][start : start + rows, span].astype(jnp.float32)
                        for index, start in terms
                    )
                    out[at : at + rows, span] = total.astype(out.dtype)
            at += rows


def combine(inputs, plans, after=(), flops=0):
    width = inputs[0].shape[1]
    return pl.pallas_call(
        functools.partial(combine_kernel, len(inputs), plans),
        out_shape=[
            jax.ShapeDtypeStruct((sum(rows for rows, _ in plan), width), jnp.bfloat16)
            for plan in plans
        ],
        in_specs=[whole] * len(inputs) + [pl.BlockSpec(memory_space=pl.ANY)] * len(after),
        out_specs=[whole] * len(plans),
        compiler_params=pltpu.CompilerParams(vmem_limit_bytes=SMALL_BYTES),
        cost_estimate=pl.CostEstimate(
            flops=flops, bytes_accessed=4 * width * inputs[0].shape[0], transcendentals=0
        ),
        name="combine",
    )(*inputs, *after)


def expert_kernel(picks, after, own, other, w_gate, w_up, w_down, *refs):
    *outs, rows, hidden = refs[after:]
    expert_body(picks, own, other, w_gate, w_up, w_down, outs, rows, hidden)


def expert_body(
    picks, own, other, w_gate, w_up, w_down, outs, rows, hidden, ready=lambda number: None
):
    h_own, *outs = outs
    count, feature, half = own.shape[0], w_gate.shape[1], w_gate.shape[2]
    wanted = expert_index().astype(jnp.float32)
    shares = []
    for ref, at in ((own, 0), (other, count)):
        rows[at : at + count, :] = ref[:, :feature]
        columns = ref[:, feature:].astype(jnp.float32)
        value = columns[:, picks : 2 * picks] + columns[:, 2 * picks : 3 * picks]
        named = columns[:, :picks] == wanted
        shares.append(jnp.sum(jnp.where(named, value, 0.0), axis=1, keepdims=True))
    share = jnp.concatenate(shares, axis=0)
    for at in range(0, half, TILE):
        ready(at // TILE * 2)
        gate_part = jnp.dot(
            rows[...], w_gate[0, :, at : at + TILE], preferred_element_type=jnp.float32
        )
        ready(at // TILE * 2 + 1)
        up_part = jnp.dot(
            rows[...], w_up[0, :, at : at + TILE], preferred_element_type=jnp.float32
        )
        product = gate_part / (1.0 + jnp.exp(-gate_part)) * up_part * share
        hidden[:, at : at + TILE] = product.astype(jnp.bfloat16)
    h_own[...] = hidden[:count, :]
    wide = feature // BLOCKS
    for at in range(0, feature, wide):
        ready(half // TILE * 2 + at // wide)
        part = jnp.dot(
            hidden[count:, :], w_down[0, :, at : at + wide], preferred_element_type=jnp.float32
        ).astype(jnp.bfloat16)
        top = 0
        for out in outs:
            out[:, at : at + wide] = part[top : top + out.shape[0], :]
            top += out.shape[0]


def first_kernel(picks, own, other, gate_far, up_far, down_far, *refs):
    outs, (w_gate, w_up, w_down, rows, hidden, sems) = refs[:-6], refs[-6:]
    feature, half = w_gate.shape[1], w_gate.shape[2]
    depth = feature // BLOCKS
    groups = []

    def begin(pairs):
        copies = []
        for source, target, index in pairs:
            at = len(copies) + sum(len(group) for group in groups)
            copies.append(pltpu.make_async_copy(source.at[index], target.at[index], sems.at[at]))
        for copy in copies:
            copy.start()
        groups.append(copies)

    for left in range(0, half, TILE):
        for source, target in ((gate_far, w_gate), (up_far, w_up)):
            begin(
                (source, target, (0, pl.ds(top, depth), pl.ds(left, TILE)))
                for top in range(0, feature, depth)
            )
    for left in range(0, feature, feature // BLOCKS):
        begin([(down_far, w_down, (0, slice(None), pl.ds(left, feature // BLOCKS)))])

    def ready(number):
        for copy in groups[number]:
            copy.wait()

    expert_body(picks, own, other, w_gate, w_up, w_down, outs, rows, hidden, ready)


def first_of(own, other, w_gate, w_up, w_down, picks, cuts):
    count = own.shape[0]
    _, feature, half = w_gate.shape
    copies = 2 * (half // TILE) * BLOCKS + BLOCKS
    return pl.pallas_call(
        functools.partial(first_kernel, picks),
        out_shape=[jax.ShapeDtypeStruct((count, half), jnp.bfloat16)]
        + [jax.ShapeDtypeStruct((cut, feature), jnp.bfloat16) for cut in cuts]
        + [jax.ShapeDtypeStruct(w.shape, w.dtype) for w in (w_gate, w_up, w_down)],
        in_specs=[whole] * 2 + [pl.BlockSpec(memory_space=pl.ANY)] * 3,
        out_specs=[whole] * (len(cuts) + 4),
        scratch_shapes=[
            pltpu.VMEM((2 * count, feature), jnp.bfloat16),
            pltpu.VMEM((2 * count, half), jnp.bfloat16),
            pltpu.SemaphoreType.DMA((copies,)),
        ],
        compiler_params=pltpu.CompilerParams(vmem_limit_bytes=FIRST_BYTES),
        cost_estimate=pl.CostEstimate(
            flops=10 * count * feature * half,
            bytes_accessed=6 * feature * half,
            transcendentals=2 * count * half,
        ),
        name="first",
    )(own, other, w_gate, w_up, w_down)


def expert_of(own, other, w_gate, w_up, w_down, picks, cuts, after=()):
    count = own.shape[0]
    _, feature, half = w_gate.shape
    return pl.pallas_call(
        functools.partial(expert_kernel, picks, len(after)),
        out_shape=[jax.ShapeDtypeStruct((count, half), jnp.bfloat16)]
        + [jax.ShapeDtypeStruct((cut, feature), jnp.bfloat16) for cut in cuts],
        in_specs=[whole] * 5 + [pl.BlockSpec(memory_space=pl.ANY)] * len(after),
        out_specs=[whole] * (len(cuts) + 1),
        scratch_shapes=[
            pltpu.VMEM((2 * count, feature), jnp.bfloat16),
            pltpu.VMEM((2 * count, half), jnp.bfloat16),
        ],
        compiler_params=pltpu.CompilerParams(vmem_limit_bytes=LARGE_BYTES),
        cost_estimate=pl.CostEstimate(
            flops=10 * count * feature * half,
            bytes_accessed=2 * count * feature,
            transcendentals=2 * count * half,
        ),
        name="expert",
    )(own, other, w_gate, w_up, w_down, *after)


def sums_kernel(parts, cuts, hidden, w_down, *refs):
    arrived, outs = refs[:parts], refs[len(refs) - len(cuts) :]
    feature = w_down.shape[2]
    for column in range(0, feature, 2 * TILE):
        span = slice(column, column + 2 * TILE)
        part = jnp.dot(hidden[...], w_down[0, :, span], preferred_element_type=jnp.float32)
        other = jnp.concatenate([term[:, span] for term in arrived], axis=0)
        part = (part + other.astype(jnp.float32)).astype(jnp.bfloat16)
        top = 0
        for cut, out in zip(cuts, outs):
            out[:, span] = part[top : top + cut, :]
            top += cut


def sums_of(hidden, w_down, arrived, cuts, after=()):
    count, half = hidden.shape
    feature = w_down.shape[2]
    return pl.pallas_call(
        functools.partial(sums_kernel, len(arrived), cuts),
        out_shape=[jax.ShapeDtypeStruct((cut, feature), jnp.bfloat16) for cut in cuts],
        in_specs=[whole] * (2 + len(arrived)) + [pl.BlockSpec(memory_space=pl.ANY)] * len(after),
        out_specs=[whole] * len(cuts),
        compiler_params=pltpu.CompilerParams(vmem_limit_bytes=SMALL_BYTES),
        cost_estimate=pl.CostEstimate(
            flops=2 * count * feature * half,
            bytes_accessed=2 * count * feature,
            transcendentals=0,
        ),
        name="sums",
    )(hidden, w_down, *arrived, *after)


def mix_large(packed, weights, picks, steps):
    w_gate, w_up, w_down = weights
    z_near, z_far, x_steps, y_steps, core = steps
    near = spread(packed, z_near)
    far = spread(swap(packed, z_far), z_near)
    near_x, near_y = others(near, x_steps), others(near, y_steps)
    far_x, far_y = others(far, x_steps), others(far, y_steps)
    near_xy, far_xy = others(near_x, y_steps), others(far_y, x_steps)
    early = [near, near_x, near_y, far, far_x, far_y]
    late = [near_xy, far_xy]
    early_cuts = [group.shape[0] for group in early]
    late_cuts = [group.shape[0] for group in late]
    early_own, late_own = jnp.concatenate(early, axis=0), jnp.concatenate(late, axis=0)
    early_other, late_other = swap(early_own, core), swap(late_own, core)
    early_h, early_h_other = hidden_of(early_own, early_other, w_gate, w_up, picks)
    late_h, late_h_other = hidden_of(late_own, late_other, w_gate, w_up, picks)
    (late_out,) = down_of(late_h_other, w_down, [late_h_other.shape[0]])
    late_in = swap(late_out, core)
    (early_out,) = down_of(early_h_other, w_down, [early_h_other.shape[0]])
    early_in = swap(early_out, core)
    near_xy, far_xy = down_of(late_h, w_down, late_cuts, late_in)
    near, near_x, near_y, far, far_x, far_y = down_of(early_h, w_down, early_cuts, early_in)
    rows, count = near.shape[0], packed.shape[0]
    near_x = add_up(near_x, give_back(near_xy, y_steps, near_x.shape[0]))
    far_y = add_up(far_y, give_back(far_xy, x_steps, far_y.shape[0]))
    far = add_up(far, give_back(far_x, x_steps, rows) + give_back(far_y, y_steps, rows))
    near = add_up(near, give_back(near_y, y_steps, rows) + give_back(near_x, x_steps, rows))
    far = add_up(far[:count], give_back(far[count:], z_near, count))
    return add_up(near[:count], give_back(near[count:], z_near, count) + [swap(far, z_far)])


def mix_small(packed, weights, picks, steps, attention):
    z_near, z_far, x, y, core = steps
    n = packed.shape[0]

    def rows_of(*segments):
        return [(count, [(index, start)]) for index, start, count in segments]

    from_near = swap(packed, z_near)
    from_far = swap(packed, z_far)
    (near,) = combine([packed, from_near], [rows_of((0, 0, n), (1, 0, n))])
    near_x, near_y = swap(near, x), swap(near, y)
    from_both = swap(from_far, z_near)
    first_own, far, way_x, way_y = combine(
        [near, near_x, near_y, from_far, from_both],
        [
            rows_of((0, 0, 2 * n), (1, 0, 2 * n), (2, 0, 2 * n), (3, 0, n), (4, 0, n)),
            rows_of((3, 0, n), (4, 0, n)),
            rows_of((3, 0, n), (4, 0, n), (2, n, n)),
            rows_of((3, 0, n), (4, 0, n), (1, 0, n)),
        ],
    )
    first_other = swap(first_own, core)
    far_xy, far_x, far_y = across(far, x, y), swap(way_x, x), swap(way_y, y)
    first_h, first_out, *weights = first_of(first_own, first_other, *weights, picks, [8 * n])
    w_down = weights[2]
    first_in = swap(first_out, core)
    (second_own,) = combine(
        [far_x, far_y, far_xy],
        [rows_of((0, 0, 2 * n), (1, 0, 2 * n), (2, 0, 2 * n), (1, 2 * n, n), (0, 2 * n, n))],
        [first_out],
    )
    second_other = swap(second_own, core)
    near, near_x, near_y, far_sum, both_sum = sums_of(
        first_h, w_down, [first_in], [2 * n] * 3 + [n] * 2
    )
    to_near = [swap(near_x, x), swap(near_y, y)]
    second_h, *second_out = expert_of(
        second_own, second_other, *weights, picks, [2 * n, 2 * n, 4 * n], [near]
    )
    second_in = [swap(part, core) for part in second_out]

    def all_of(terms, start, count=n):
        return [(count, [(index, start) for index in range(terms)])]

    (near,) = combine([near, *to_near], [all_of(3, 0, 2 * n)], flops=NEAR_FLOPS)
    far_x, both_x, far_y, both_y, far_xy, both_xy, near_xy = sums_of(
        second_h, w_down, second_in, [n] * 6 + [2 * n], [near]
    )

    to_both = [across(both_xy, x, y), swap(both_x, x), swap(both_y, y)]
    to_far = [across(far_xy, x, y), swap(far_x, x), swap(far_y, y)]
    context, done = attention([both_x])
    (both_sum,) = combine([both_sum, *to_both], [all_of(4, 0)], [done])
    (near_xy,) = combine([near_xy], [rows_of((0, 0, 2 * n))], [both_sum])
    to_near = across(near_xy, x, y)
    (far_sum,) = combine([far_sum, *to_far], [all_of(4, 0)], [near_xy], flops=FAR_FLOPS)
    from_both = across(both_sum, z_far, z_near)
    own_sum, near_sum = combine(
        [near, to_near, from_both], [all_of(3, 0), all_of(2, n)], [far_sum]
    )
    (mixed,) = combine(
        [own_sum, swap(far_sum, z_far), swap(near_sum, z_near)], [all_of(3, 0)]
    )
    return mixed, context


def per_device(queries, cache, lengths, live_rows, tokens, ids, gates, w_gate, w_up, w_down):
    picks = ids.shape[1]
    grp_bits = bits_of(lax.axis_size("grp"))
    ep_bits = bits_of(lax.axis_size("ep"))
    core = ("grp", 1)
    z_near = [("grp", bit) for bit in reversed(grp_bits[1:-1])]
    z_far = ("grp", grp_bits[-1])
    x_steps = [("ep", bit) for bit in ep_bits[: len(ep_bits) // 2]]
    y_steps = [("ep", bit) for bit in ep_bits[len(ep_bits) // 2 :]]

    packed = pack(tokens, ids, gates)
    weights = (w_gate, w_up, w_down)
    if len(z_near) == len(x_steps) == len(y_steps) == 1:
        steps = (z_near[0], z_far, x_steps[0], y_steps[0], core)
        attention = functools.partial(attend, queries, cache, lengths, live_rows)
        mixed, context = mix_small(packed, weights, picks, steps, attention)
    else:
        steps = (z_near, z_far, x_steps, y_steps, core)
        mixed = mix_large(packed, weights, picks, steps)
        context, _ = attend(queries, cache, lengths, live_rows)
    return (context, mixed)


def solution(mesh):
    rows3 = P(AXES, None, None)
    rows2 = P(AXES, None)
    rows1 = P(AXES)
    return jax.shard_map(
        per_device,
        mesh=mesh,
        in_specs=(rows3, rows3, rows1, rows1, rows2, rows2, rows2, rows3, rows3, rows3),
        out_specs=(rows3, rows2),
        check_vma=False,
    )
```

```python
import functools

import jax
import jax.numpy as jnp
from jax import lax
from jax.experimental import pallas as pl
from jax.experimental.pallas import tpu as pltpu
from jax.sharding import PartitionSpec as P

LAT = 512
AXES = ("grp", "ep")
EXTRA = 128
BLOCKS = 4
TILE = 256
WIDE = 512
NEAR_FLOPS = 4 * 10**9
FAR_FLOPS = 4 * 10**9
VMEM_BYTES = 48 * 1024 * 1024
LARGE_BYTES = 16 * 1024 * 1024
SMALL_BYTES = 8 * 1024 * 1024
FIRST_BYTES = 39 * 1024 * 1024
whole = pl.BlockSpec(memory_space=pltpu.VMEM)

score_scale = 192.0 ** (-0.5)
neg_large = -1e30


def attend_kernel(lengths, live_rows, queries, channels, *refs):
    out, done = refs[-2:]
    count, heads, _ = queries.shape
    positions = lax.broadcasted_iota(jnp.int32, (heads, channels.shape[2]), 1)
    for request in range(count):
        scores = jnp.dot(
            queries[request], channels[request], preferred_element_type=jnp.float32
        )
        inside = positions < lengths[request]
        masked = jnp.where(inside, scores * score_scale, neg_large)
        highest = jnp.max(masked, axis=1, keepdims=True)
        powers = jnp.where(inside, jnp.exp(masked - highest), 0.0)
        totals = jnp.sum(powers, axis=1, keepdims=True)
        weights = (powers / totals).astype(jnp.bfloat16)
        context = lax.dot_general(
            weights,
            channels[request, :LAT, :],
            (((1,), (1,)), ((), ())),
            preferred_element_type=jnp.float32,
        )
        out[request] = jnp.where(request < live_rows[0], context, 0.0).astype(jnp.bfloat16)
    done[...] = jnp.zeros_like(done)


def attend(queries, cache, lengths, live_rows, after=()):
    count, heads, width = queries.shape
    positions = cache.shape[1]
    return pl.pallas_call(
        attend_kernel,
        out_shape=[
            jax.ShapeDtypeStruct((count, heads, LAT), jnp.bfloat16),
            jax.ShapeDtypeStruct((8, 128), jnp.float32),
        ],
        in_specs=[pl.BlockSpec(memory_space=pltpu.SMEM)] * 2
        + [whole] * 2
        + [pl.BlockSpec(memory_space=pl.ANY)] * len(after),
        out_specs=[whole] * 2,
        compiler_params=pltpu.CompilerParams(vmem_limit_bytes=SMALL_BYTES),
        cost_estimate=pl.CostEstimate(
            flops=4 * count * heads * width * positions,
            bytes_accessed=2 * count * positions * width,
            transcendentals=count * heads * positions,
        ),
        name="attend",
    )(lengths, live_rows, queries, jnp.swapaxes(cache, 1, 2), *after)


def bits_of(count):
    return [1 << i for i in range(count.bit_length() - 1)]


def swap(value, step):
    axis, bit = step
    size = lax.axis_size(axis)
    return lax.ppermute(value, axis, [(i, i ^ bit) for i in range(size)])


def across(value, first, second):
    axis = first[0]
    size = lax.axis_size(axis)
    return lax.ppermute(value, axis, [(i, i ^ first[1] ^ second[1]) for i in range(size)])


def spread(value, steps):
    for step in steps:
        value = jnp.concatenate([value, swap(value, step)], axis=0)
    return value


def others(value, steps):
    if len(steps) == 1:
        return swap(value, steps[0])
    return spread(value, steps)[value.shape[0] :]


def give_back(rest, steps, rows):
    terms = []
    for step in reversed(steps):
        keep = (rest.shape[0] + rows) // 2 - rows
        arrived = swap(rest[keep:], step)
        terms.append(arrived[:rows])
        if keep:
            rest = add_up(rest[:keep], [arrived[rows:]])
    return terms


def add_up(own, terms):
    total = own.astype(jnp.float32)
    for term in terms:
        total = total + term.astype(jnp.float32)
    return total.astype(jnp.bfloat16)


def pack_kernel(tokens, chosen, out):
    feature = tokens.shape[1]
    picks = chosen.shape[0] // 2
    gates = chosen[picks:, :]
    high = gates.astype(jnp.bfloat16).astype(jnp.float32)
    stacked = jnp.concatenate([chosen[:picks, :], high, gates - high], axis=0)
    stacked = stacked.astype(jnp.bfloat16)
    row = lax.broadcasted_iota(jnp.int32, (stacked.shape[0], EXTRA), 0)
    column = lax.broadcasted_iota(jnp.int32, (stacked.shape[0], EXTRA), 1)
    place = jnp.where(row == column, 1.0, 0.0).astype(jnp.bfloat16)
    extra = lax.dot_general(
        stacked, place, (((0,), (0,)), ((), ())), preferred_element_type=jnp.float32
    )
    out[:, :feature] = tokens[...]
    out[:, feature:] = extra.astype(jnp.bfloat16)


def pack(tokens, ids, gates):
    return pl.pallas_call(
        pack_kernel,
        out_shape=jax.ShapeDtypeStruct((tokens.shape[0], tokens.shape[1] + EXTRA), jnp.bfloat16),
        in_specs=[whole] * 2,
        out_specs=whole,
        compiler_params=pltpu.CompilerParams(vmem_limit_bytes=SMALL_BYTES),
        name="pack",
    )(tokens, jnp.concatenate([ids.T.astype(jnp.float32), gates.T], axis=0))


def expert_index():
    return (lax.axis_index("grp") * lax.axis_size("ep") + lax.axis_index("ep")) // 2


def hidden_kernel(picks, own, other, extra_own, extra_other, w_gate, w_up, h_own, h_other, gate_sum, up_sum):
    step = pl.program_id(0)
    rows = jnp.concatenate([own[...], other[...]], axis=0)
    gate_part = jnp.dot(rows, w_gate[0], preferred_element_type=jnp.float32)
    up_part = jnp.dot(rows, w_up[0], preferred_element_type=jnp.float32)

    @pl.when(step == 0)
    def _():
        gate_sum[...] = gate_part
        up_sum[...] = up_part

    @pl.when(step > 0)
    def _():
        gate_sum[...] += gate_part
        up_sum[...] += up_part

    @pl.when(step == pl.num_programs(0) - 1)
    def _():
        count = own.shape[0]
        wanted = expert_index().astype(jnp.float32)
        for extra, out, at in ((extra_own, h_own, 0), (extra_other, h_other, count)):
            columns = extra[...].astype(jnp.float32)
            value = columns[:, picks : 2 * picks] + columns[:, 2 * picks : 3 * picks]
            share = jnp.sum(
                jnp.where(columns[:, :picks] == wanted, value, 0.0), axis=1, keepdims=True
            )
            gate_all = gate_sum[at : at + count, :]
            up_all = up_sum[at : at + count, :]
            hidden = gate_all / (1.0 + jnp.exp(-gate_all)) * up_all
            out[...] = (hidden * share).astype(jnp.bfloat16)


def hidden_of(own, other, w_gate, w_up, picks):
    count, width = own.shape
    _, feature, half = w_gate.shape
    depth = feature // BLOCKS
    rows_spec = pl.BlockSpec((count, depth), lambda k: (0, k))
    extra_spec = pl.BlockSpec((count, EXTRA), lambda k: (0, feature // EXTRA))
    weight_spec = pl.BlockSpec((1, depth, half), lambda k: (0, k, 0))
    out_spec = pl.BlockSpec((count, half), lambda k: (0, 0))
    return pl.pallas_call(
        functools.partial(hidden_kernel, picks),
        grid=(BLOCKS,),
        out_shape=[jax.ShapeDtypeStruct((count, half), jnp.bfloat16)] * 2,
        in_specs=[rows_spec] * 2 + [extra_spec] * 2 + [weight_spec] * 2,
        out_specs=[out_spec] * 2,
        scratch_shapes=[pltpu.VMEM((2 * count, half), jnp.float32)] * 2,
        compiler_params=pltpu.CompilerParams(vmem_limit_bytes=VMEM_BYTES),
        cost_estimate=pl.CostEstimate(
            flops=8 * count * feature * half,
            bytes_accessed=4 * feature * half + 4 * count * width,
            transcendentals=2 * count * half,
        ),
        name="hidden",
    )(own, other, own, other, w_gate, w_up)


def down_kernel(cuts, hidden, w_down, *refs):
    part = jnp.dot(hidden[...], w_down[0], preferred_element_type=jnp.float32)
    if len(refs) > len(cuts):
        part = part + refs[0][...].astype(jnp.float32)
        refs = refs[1:]
    at = 0
    for cut, out in zip(cuts, refs):
        out[...] = part[at : at + cut, :].astype(jnp.bfloat16)
        at += cut


def down_of(hidden, w_down, cuts, arrived=None):
    count, half = hidden.shape
    feature = w_down.shape[2]
    wide = feature // BLOCKS
    operands = [hidden, w_down]
    in_specs = [
        pl.BlockSpec((count, half), lambda n: (0, 0)),
        pl.BlockSpec((1, half, wide), lambda n: (0, 0, n)),
    ]
    if arrived is not None:
        operands.append(arrived)
        in_specs.append(pl.BlockSpec((count, wide), lambda n: (0, n)))
    return pl.pallas_call(
        functools.partial(down_kernel, cuts),
        grid=(BLOCKS,),
        out_shape=[jax.ShapeDtypeStruct((cut, feature), jnp.bfloat16) for cut in cuts],
        in_specs=in_specs,
        out_specs=[pl.BlockSpec((cut, wide), lambda n: (0, n)) for cut in cuts],
        compiler_params=pltpu.CompilerParams(vmem_limit_bytes=VMEM_BYTES),
        cost_estimate=pl.CostEstimate(
            flops=2 * count * feature * half,
            bytes_accessed=2 * feature * half + 4 * count * feature,
            transcendentals=0,
        ),
        name="down",
    )(*operands)


def combine_kernel(count, plans, *refs):
    outs = refs[len(refs) - len(plans) :]
    width = outs[0].shape[1]
    for plan, out in zip(plans, outs):
        at = 0
        for rows, terms in plan:
            if len(terms) == 1:
                index, start = terms[0]
                out[at : at + rows, :] = refs[index][start : start + rows, :]
            else:
                for left in range(0, width, WIDE):
                    span = slice(left, left + WIDE)
                    total = sum(
                        refs[index][start : start + rows, span].astype(jnp.float32)
                        for index, start in terms
                    )
                    out[at : at + rows, span] = total.astype(out.dtype)
            at += rows


def combine(inputs, plans, after=(), flops=0):
    width = inputs[0].shape[1]
    return pl.pallas_call(
        functools.partial(combine_kernel, len(inputs), plans),
        out_shape=[
            jax.ShapeDtypeStruct((sum(rows for rows, _ in plan), width), jnp.bfloat16)
            for plan in plans
        ],
        in_specs=[whole] * len(inputs) + [pl.BlockSpec(memory_space=pl.ANY)] * len(after),
        out_specs=[whole] * len(plans),
        compiler_params=pltpu.CompilerParams(vmem_limit_bytes=SMALL_BYTES),
        cost_estimate=pl.CostEstimate(
            flops=flops, bytes_accessed=4 * width * inputs[0].shape[0], transcendentals=0
        ),
        name="combine",
    )(*inputs, *after)


def expert_kernel(picks, after, own, other, w_gate, w_up, w_down, *refs):
    *outs, rows, hidden = refs[after:]
    expert_body(picks, own, other, w_gate, w_up, w_down, outs, rows, hidden)


def expert_body(
    picks, own, other, w_gate, w_up, w_down, outs, rows, hidden, ready=lambda number: None
):
    h_own, *outs = outs
    count, feature, half = own.shape[0], w_gate.shape[1], w_gate.shape[2]
    wanted = expert_index().astype(jnp.float32)
    shares = []
    for ref, at in ((own, 0), (other, count)):
        rows[at : at + count, :] = ref[:, :feature]
        columns = ref[:, feature:].astype(jnp.float32)
        value = columns[:, picks : 2 * picks] + columns[:, 2 * picks : 3 * picks]
        named = columns[:, :picks] == wanted
        shares.append(jnp.sum(jnp.where(named, value, 0.0), axis=1, keepdims=True))
    share = jnp.concatenate(shares, axis=0)
    for at in range(0, half, TILE):
        ready(at // TILE * 2)
        gate_part = jnp.dot(
            rows[...], w_gate[0, :, at : at + TILE], preferred_element_type=jnp.float32
        )
        ready(at // TILE * 2 + 1)
        up_part = jnp.dot(
            rows[...], w_up[0, :, at : at + TILE], preferred_element_type=jnp.float32
        )
        product = gate_part / (1.0 + jnp.exp(-gate_part)) * up_part * share
        hidden[:, at : at + TILE] = product.astype(jnp.bfloat16)
    h_own[...] = hidden[:count, :]
    wide = feature // BLOCKS
    for at in range(0, feature, wide):
        ready(half // TILE * 2 + at // wide)
        part = jnp.dot(
            hidden[count:, :], w_down[0, :, at : at + wide], preferred_element_type=jnp.float32
        ).astype(jnp.bfloat16)
        top = 0
        for out in outs:
            out[:, at : at + wide] = part[top : top + out.shape[0], :]
            top += out.shape[0]


def first_kernel(picks, own, other, gate_far, up_far, down_far, *refs):
    outs, (w_gate, w_up, w_down, rows, hidden, sems) = refs[:-6], refs[-6:]
    feature, half = w_gate.shape[1], w_gate.shape[2]
    depth = feature // BLOCKS
    groups = []

    def begin(pairs):
        copies = []
        for source, target, index in pairs:
            at = len(copies) + sum(len(group) for group in groups)
            copies.append(pltpu.make_async_copy(source.at[index], target.at[index], sems.at[at]))
        for copy in copies:
            copy.start()
        groups.append(copies)

    for left in range(0, half, TILE):
        for source, target in ((gate_far, w_gate), (up_far, w_up)):
            begin(
                (source, target, (0, pl.ds(top, depth), pl.ds(left, TILE)))
                for top in range(0, feature, depth)
            )
    for left in range(0, feature, feature // BLOCKS):
        begin([(down_far, w_down, (0, slice(None), pl.ds(left, feature // BLOCKS)))])

    def ready(number):
        for copy in groups[number]:
            copy.wait()

    expert_body(picks, own, other, w_gate, w_up, w_down, outs, rows, hidden, ready)


def first_of(own, other, w_gate, w_up, w_down, picks, cuts):
    count = own.shape[0]
    _, feature, half = w_gate.shape
    copies = 2 * (half // TILE) * BLOCKS + BLOCKS
    return pl.pallas_call(
        functools.partial(first_kernel, picks),
        out_shape=[jax.ShapeDtypeStruct((count, half), jnp.bfloat16)]
        + [jax.ShapeDtypeStruct((cut, feature), jnp.bfloat16) for cut in cuts]
        + [jax.ShapeDtypeStruct(w.shape, w.dtype) for w in (w_gate, w_up, w_down)],
        in_specs=[whole] * 2 + [pl.BlockSpec(memory_space=pl.ANY)] * 3,
        out_specs=[whole] * (len(cuts) + 4),
        scratch_shapes=[
            pltpu.VMEM((2 * count, feature), jnp.bfloat16),
            pltpu.VMEM((2 * count, half), jnp.bfloat16),
            pltpu.SemaphoreType.DMA((copies,)),
        ],
        compiler_params=pltpu.CompilerParams(vmem_limit_bytes=FIRST_BYTES),
        cost_estimate=pl.CostEstimate(
            flops=10 * count * feature * half,
            bytes_accessed=6 * feature * half,
            transcendentals=2 * count * half,
        ),
        name="first",
    )(own, other, w_gate, w_up, w_down)


def expert_of(own, other, w_gate, w_up, w_down, picks, cuts, after=()):
    count = own.shape[0]
    _, feature, half = w_gate.shape
    return pl.pallas_call(
        functools.partial(expert_kernel, picks, len(after)),
        out_shape=[jax.ShapeDtypeStruct((count, half), jnp.bfloat16)]
        + [jax.ShapeDtypeStruct((cut, feature), jnp.bfloat16) for cut in cuts],
        in_specs=[whole] * 5 + [pl.BlockSpec(memory_space=pl.ANY)] * len(after),
        out_specs=[whole] * (len(cuts) + 1),
        scratch_shapes=[
            pltpu.VMEM((2 * count, feature), jnp.bfloat16),
            pltpu.VMEM((2 * count, half), jnp.bfloat16),
        ],
        compiler_params=pltpu.CompilerParams(vmem_limit_bytes=LARGE_BYTES),
        cost_estimate=pl.CostEstimate(
            flops=10 * count * feature * half,
            bytes_accessed=2 * count * feature,
            transcendentals=2 * count * half,
        ),
        name="expert",
    )(own, other, w_gate, w_up, w_down, *after)


def sums_kernel(parts, cuts, hidden, w_down, *refs):
    arrived, outs = refs[:parts], refs[len(refs) - len(cuts) :]
    feature = w_down.shape[2]
    for column in range(0, feature, 2 * TILE):
        span = slice(column, column + 2 * TILE)
        part = jnp.dot(hidden[...], w_down[0, :, span], preferred_element_type=jnp.float32)
        other = jnp.concatenate([term[:, span] for term in arrived], axis=0)
        part = (part + other.astype(jnp.float32)).astype(jnp.bfloat16)
        top = 0
        for cut, out in zip(cuts, outs):
            out[:, span] = part[top : top + cut, :]
            top += cut


def sums_of(hidden, w_down, arrived, cuts, after=()):
    count, half = hidden.shape
    feature = w_down.shape[2]
    return pl.pallas_call(
        functools.partial(sums_kernel, len(arrived), cuts),
        out_shape=[jax.ShapeDtypeStruct((cut, feature), jnp.bfloat16) for cut in cuts],
        in_specs=[whole] * (2 + len(arrived)) + [pl.BlockSpec(memory_space=pl.ANY)] * len(after),
        out_specs=[whole] * len(cuts),
        compiler_params=pltpu.CompilerParams(vmem_limit_bytes=SMALL_BYTES),
        cost_estimate=pl.CostEstimate(
            flops=2 * count * feature * half,
            bytes_accessed=2 * count * feature,
            transcendentals=0,
        ),
        name="sums",
    )(hidden, w_down, *arrived, *after)


def mix_large(packed, weights, picks, steps):
    w_gate, w_up, w_down = weights
    z_near, z_far, x_steps, y_steps, core = steps
    near = spread(packed, z_near)
    far = spread(swap(packed, z_far), z_near)
    near_x, near_y = others(near, x_steps), others(near, y_steps)
    far_x, far_y = others(far, x_steps), others(far, y_steps)
    near_xy, far_xy = others(near_x, y_steps), others(far_y, x_steps)
    early = [near, near_x, near_y, far, far_x, far_y]
    late = [near_xy, far_xy]
    early_cuts = [group.shape[0] for group in early]
    late_cuts = [group.shape[0] for group in late]
    early_own, late_own = jnp.concatenate(early, axis=0), jnp.concatenate(late, axis=0)
    early_other, late_other = swap(early_own, core), swap(late_own, core)
    early_h, early_h_other = hidden_of(early_own, early_other, w_gate, w_up, picks)
    late_h, late_h_other = hidden_of(late_own, late_other, w_gate, w_up, picks)
    (late_out,) = down_of(late_h_other, w_down, [late_h_other.shape[0]])
    late_in = swap(late_out, core)
    (early_out,) = down_of(early_h_other, w_down, [early_h_other.shape[0]])
    early_in = swap(early_out, core)
    near_xy, far_xy = down_of(late_h, w_down, late_cuts, late_in)
    near, near_x, near_y, far, far_x, far_y = down_of(early_h, w_down, early_cuts, early_in)
    rows, count = near.shape[0], packed.shape[0]
    near_x = add_up(near_x, give_back(near_xy, y_steps, near_x.shape[0]))
    far_y = add_up(far_y, give_back(far_xy, x_steps, far_y.shape[0]))
    far = add_up(far, give_back(far_x, x_steps, rows) + give_back(far_y, y_steps, rows))
    near = add_up(near, give_back(near_y, y_steps, rows) + give_back(near_x, x_steps, rows))
    far = add_up(far[:count], give_back(far[count:], z_near, count))
    return add_up(near[:count], give_back(near[count:], z_near, count) + [swap(far, z_far)])


def mix_small(packed, weights, picks, steps, attention):
    z_near, z_far, x, y, core = steps
    n = packed.shape[0]

    def rows_of(*segments):
        return [(count, [(index, start)]) for index, start, count in segments]

    from_near = swap(packed, z_near)
    from_far = swap(packed, z_far)
    (near,) = combine([packed, from_near], [rows_of((0, 0, n), (1, 0, n))])
    near_x, near_y = swap(near, x), swap(near, y)
    from_both = swap(from_far, z_near)
    first_own, far, way_x, way_y = combine(
        [near, near_x, near_y, from_far, from_both],
        [
            rows_of((0, 0, 2 * n), (1, 0, 2 * n), (2, 0, 2 * n), (3, 0, n), (4, 0, n)),
            rows_of((3, 0, n), (4, 0, n)),
            rows_of((3, 0, n), (4, 0, n), (2, n, n)),
            rows_of((3, 0, n), (4, 0, n), (1, 0, n)),
        ],
    )
    first_other = swap(first_own, core)
    far_xy, far_x, far_y = across(far, x, y), swap(way_x, x), swap(way_y, y)
    first_h, first_out, *weights = first_of(first_own, first_other, *weights, picks, [8 * n])
    w_down = weights[2]
    first_in = swap(first_out, core)
    context, done = attention([first_out])
    (second_own,) = combine(
        [far_x, far_y, far_xy],
        [rows_of((0, 0, 2 * n), (1, 0, 2 * n), (2, 0, 2 * n), (1, 2 * n, n), (0, 2 * n, n))],
        [done],
    )
    second_other = swap(second_own, core)
    near, near_x, near_y, far_sum, both_sum = sums_of(
        first_h, w_down, [first_in], [2 * n] * 3 + [n] * 2
    )
    to_near = [swap(near_x, x), swap(near_y, y)]
    second_h, *second_out = expert_of(
        second_own, second_other, *weights, picks, [2 * n, 2 * n, 4 * n], [near]
    )
    second_in = [swap(part, core) for part in second_out]

    def all_of(terms, start, count=n):
        return [(count, [(index, start) for index in range(terms)])]

    (near,) = combine([near, *to_near], [all_of(3, 0, 2 * n)], flops=NEAR_FLOPS)
    far_x, both_x, far_y, both_y, far_xy, both_xy, near_xy = sums_of(
        second_h, w_down, second_in, [n] * 6 + [2 * n], [near]
    )

    to_both = [across(both_xy, x, y), swap(both_x, x), swap(both_y, y)]
    to_far = [across(far_xy, x, y), swap(far_x, x), swap(far_y, y)]
    (both_sum,) = combine([both_sum, *to_both], [all_of(4, 0)])
    (near_xy,) = combine([near_xy], [rows_of((0, 0, 2 * n))], [both_sum])
    to_near = across(near_xy, x, y)
    (far_sum,) = combine([far_sum, *to_far], [all_of(4, 0)], [near_xy], flops=FAR_FLOPS)
    from_both = across(both_sum, z_far, z_near)
    own_sum, near_sum = combine(
        [near, to_near, from_both], [all_of(3, 0), all_of(2, n)], [far_sum]
    )
    (mixed,) = combine(
        [own_sum, swap(far_sum, z_far), swap(near_sum, z_near)], [all_of(3, 0)]
    )
    return mixed, context


def per_device(queries, cache, lengths, live_rows, tokens, ids, gates, w_gate, w_up, w_down):
    picks = ids.shape[1]
    grp_bits = bits_of(lax.axis_size("grp"))
    ep_bits = bits_of(lax.axis_size("ep"))
    core = ("grp", 1)
    z_near = [("grp", bit) for bit in reversed(grp_bits[1:-1])]
    z_far = ("grp", grp_bits[-1])
    x_steps = [("ep", bit) for bit in ep_bits[: len(ep_bits) // 2]]
    y_steps = [("ep", bit) for bit in ep_bits[len(ep_bits) // 2 :]]

    packed = pack(tokens, ids, gates)
    weights = (w_gate, w_up, w_down)
    if len(z_near) == len(x_steps) == len(y_steps) == 1:
        steps = (z_near[0], z_far, x_steps[0], y_steps[0], core)
        attention = functools.partial(attend, queries, cache, lengths, live_rows)
        mixed, context = mix_small(packed, weights, picks, steps, attention)
    else:
        steps = (z_near, z_far, x_steps, y_steps, core)
        mixed = mix_large(packed, weights, picks, steps)
        context, _ = attend(queries, cache, lengths, live_rows)
    return (context, mixed)


def solution(mesh):
    rows3 = P(AXES, None, None)
    rows2 = P(AXES, None)
    rows1 = P(AXES)
    return jax.shard_map(
        per_device,
        mesh=mesh,
        in_specs=(rows3, rows3, rows1, rows1, rows2, rows2, rows2, rows3, rows3, rows3),
        out_specs=(rows3, rows2),
        check_vma=False,
    )
```

```python
import functools

import jax
import jax.numpy as jnp
from jax import lax
from jax.experimental import pallas as pl
from jax.experimental.pallas import tpu as pltpu
from jax.sharding import PartitionSpec as P

LAT = 512
AXES = ("grp", "ep")
EXTRA = 128
BLOCKS = 4
TILE = 256
WIDE = 512
NEAR_FLOPS = 4 * 10**9
FAR_FLOPS = 4 * 10**9
VMEM_BYTES = 48 * 1024 * 1024
LARGE_BYTES = 16 * 1024 * 1024
SMALL_BYTES = 8 * 1024 * 1024
FIRST_BYTES = 39 * 1024 * 1024
whole = pl.BlockSpec(memory_space=pltpu.VMEM)

score_scale = 192.0 ** (-0.5)
neg_large = -1e30


def attend_kernel(lengths, live_rows, queries, channels, *refs):
    out, done = refs[-2:]
    count, heads, _ = queries.shape
    positions = lax.broadcasted_iota(jnp.int32, (heads, channels.shape[2]), 1)
    for request in range(count):
        scores = jnp.dot(
            queries[request], channels[request], preferred_element_type=jnp.float32
        )
        inside = positions < lengths[request]
        masked = jnp.where(inside, scores * score_scale, neg_large)
        highest = jnp.max(masked, axis=1, keepdims=True)
        powers = jnp.where(inside, jnp.exp(masked - highest), 0.0)
        totals = jnp.sum(powers, axis=1, keepdims=True)
        weights = (powers / totals).astype(jnp.bfloat16)
        context = lax.dot_general(
            weights,
            channels[request, :LAT, :],
            (((1,), (1,)), ((), ())),
            preferred_element_type=jnp.float32,
        )
        out[request] = jnp.where(request < live_rows[0], context, 0.0).astype(jnp.bfloat16)
    done[...] = jnp.zeros_like(done)


def attend(queries, cache, lengths, live_rows, after=()):
    count, heads, width = queries.shape
    positions = cache.shape[1]
    return pl.pallas_call(
        attend_kernel,
        out_shape=[
            jax.ShapeDtypeStruct((count, heads, LAT), jnp.bfloat16),
            jax.ShapeDtypeStruct((8, 128), jnp.float32),
        ],
        in_specs=[pl.BlockSpec(memory_space=pltpu.SMEM)] * 2
        + [whole] * 2
        + [pl.BlockSpec(memory_space=pl.ANY)] * len(after),
        out_specs=[whole] * 2,
        compiler_params=pltpu.CompilerParams(vmem_limit_bytes=SMALL_BYTES),
        cost_estimate=pl.CostEstimate(
            flops=4 * count * heads * width * positions,
            bytes_accessed=2 * count * positions * width,
            transcendentals=count * heads * positions,
        ),
        name="attend",
    )(lengths, live_rows, queries, jnp.swapaxes(cache, 1, 2), *after)


def bits_of(count):
    return [1 << i for i in range(count.bit_length() - 1)]


def swap(value, step):
    axis, bit = step
    size = lax.axis_size(axis)
    return lax.ppermute(value, axis, [(i, i ^ bit) for i in range(size)])


def across(value, first, second):
    axis = first[0]
    size = lax.axis_size(axis)
    return lax.ppermute(value, axis, [(i, i ^ first[1] ^ second[1]) for i in range(size)])


def spread(value, steps):
    for step in steps:
        value = jnp.concatenate([value, swap(value, step)], axis=0)
    return value


def others(value, steps):
    if len(steps) == 1:
        return swap(value, steps[0])
    return spread(value, steps)[value.shape[0] :]


def give_back(rest, steps, rows):
    terms = []
    for step in reversed(steps):
        keep = (rest.shape[0] + rows) // 2 - rows
        arrived = swap(rest[keep:], step)
        terms.append(arrived[:rows])
        if keep:
            rest = add_up(rest[:keep], [arrived[rows:]])
    return terms


def add_up(own, terms):
    total = own.astype(jnp.float32)
    for term in terms:
        total = total + term.astype(jnp.float32)
    return total.astype(jnp.bfloat16)


def pack_kernel(tokens, chosen, out):
    feature = tokens.shape[1]
    picks = chosen.shape[0] // 2
    gates = chosen[picks:, :]
    high = gates.astype(jnp.bfloat16).astype(jnp.float32)
    stacked = jnp.concatenate([chosen[:picks, :], high, gates - high], axis=0)
    stacked = stacked.astype(jnp.bfloat16)
    row = lax.broadcasted_iota(jnp.int32, (stacked.shape[0], EXTRA), 0)
    column = lax.broadcasted_iota(jnp.int32, (stacked.shape[0], EXTRA), 1)
    place = jnp.where(row == column, 1.0, 0.0).astype(jnp.bfloat16)
    extra = lax.dot_general(
        stacked, place, (((0,), (0,)), ((), ())), preferred_element_type=jnp.float32
    )
    out[:, :feature] = tokens[...]
    out[:, feature:] = extra.astype(jnp.bfloat16)


def pack(tokens, ids, gates):
    return pl.pallas_call(
        pack_kernel,
        out_shape=jax.ShapeDtypeStruct((tokens.shape[0], tokens.shape[1] + EXTRA), jnp.bfloat16),
        in_specs=[whole] * 2,
        out_specs=whole,
        compiler_params=pltpu.CompilerParams(vmem_limit_bytes=SMALL_BYTES),
        name="pack",
    )(tokens, jnp.concatenate([ids.T.astype(jnp.float32), gates.T], axis=0))


def expert_index():
    return (lax.axis_index("grp") * lax.axis_size("ep") + lax.axis_index("ep")) // 2


def hidden_kernel(picks, own, other, extra_own, extra_other, w_gate, w_up, h_own, h_other, gate_sum, up_sum):
    step = pl.program_id(0)
    rows = jnp.concatenate([own[...], other[...]], axis=0)
    gate_part = jnp.dot(rows, w_gate[0], preferred_element_type=jnp.float32)
    up_part = jnp.dot(rows, w_up[0], preferred_element_type=jnp.float32)

    @pl.when(step == 0)
    def _():
        gate_sum[...] = gate_part
        up_sum[...] = up_part

    @pl.when(step > 0)
    def _():
        gate_sum[...] += gate_part
        up_sum[...] += up_part

    @pl.when(step == pl.num_programs(0) - 1)
    def _():
        count = own.shape[0]
        wanted = expert_index().astype(jnp.float32)
        for extra, out, at in ((extra_own, h_own, 0), (extra_other, h_other, count)):
            columns = extra[...].astype(jnp.float32)
            value = columns[:, picks : 2 * picks] + columns[:, 2 * picks : 3 * picks]
            share = jnp.sum(
                jnp.where(columns[:, :picks] == wanted, value, 0.0), axis=1, keepdims=True
            )
            gate_all = gate_sum[at : at + count, :]
            up_all = up_sum[at : at + count, :]
            hidden = gate_all / (1.0 + jnp.exp(-gate_all)) * up_all
            out[...] = (hidden * share).astype(jnp.bfloat16)


def hidden_of(own, other, w_gate, w_up, picks):
    count, width = own.shape
    _, feature, half = w_gate.shape
    depth = feature // BLOCKS
    rows_spec = pl.BlockSpec((count, depth), lambda k: (0, k))
    extra_spec = pl.BlockSpec((count, EXTRA), lambda k: (0, feature // EXTRA))
    weight_spec = pl.BlockSpec((1, depth, half), lambda k: (0, k, 0))
    out_spec = pl.BlockSpec((count, half), lambda k: (0, 0))
    return pl.pallas_call(
        functools.partial(hidden_kernel, picks),
        grid=(BLOCKS,),
        out_shape=[jax.ShapeDtypeStruct((count, half), jnp.bfloat16)] * 2,
        in_specs=[rows_spec] * 2 + [extra_spec] * 2 + [weight_spec] * 2,
        out_specs=[out_spec] * 2,
        scratch_shapes=[pltpu.VMEM((2 * count, half), jnp.float32)] * 2,
        compiler_params=pltpu.CompilerParams(vmem_limit_bytes=VMEM_BYTES),
        cost_estimate=pl.CostEstimate(
            flops=8 * count * feature * half,
            bytes_accessed=4 * feature * half + 4 * count * width,
            transcendentals=2 * count * half,
        ),
        name="hidden",
    )(own, other, own, other, w_gate, w_up)


def down_kernel(cuts, hidden, w_down, *refs):
    part = jnp.dot(hidden[...], w_down[0], preferred_element_type=jnp.float32)
    if len(refs) > len(cuts):
        part = part + refs[0][...].astype(jnp.float32)
        refs = refs[1:]
    at = 0
    for cut, out in zip(cuts, refs):
        out[...] = part[at : at + cut, :].astype(jnp.bfloat16)
        at += cut


def down_of(hidden, w_down, cuts, arrived=None):
    count, half = hidden.shape
    feature = w_down.shape[2]
    wide = feature // BLOCKS
    operands = [hidden, w_down]
    in_specs = [
        pl.BlockSpec((count, half), lambda n: (0, 0)),
        pl.BlockSpec((1, half, wide), lambda n: (0, 0, n)),
    ]
    if arrived is not None:
        operands.append(arrived)
        in_specs.append(pl.BlockSpec((count, wide), lambda n: (0, n)))
    return pl.pallas_call(
        functools.partial(down_kernel, cuts),
        grid=(BLOCKS,),
        out_shape=[jax.ShapeDtypeStruct((cut, feature), jnp.bfloat16) for cut in cuts],
        in_specs=in_specs,
        out_specs=[pl.BlockSpec((cut, wide), lambda n: (0, n)) for cut in cuts],
        compiler_params=pltpu.CompilerParams(vmem_limit_bytes=VMEM_BYTES),
        cost_estimate=pl.CostEstimate(
            flops=2 * count * feature * half,
            bytes_accessed=2 * feature * half + 4 * count * feature,
            transcendentals=0,
        ),
        name="down",
    )(*operands)


def combine_kernel(count, plans, *refs):
    outs = refs[len(refs) - len(plans) :]
    width = outs[0].shape[1]
    for plan, out in zip(plans, outs):
        at = 0
        for rows, terms in plan:
            if len(terms) == 1:
                index, start = terms[0]
                out[at : at + rows, :] = refs[index][start : start + rows, :]
            else:
                for left in range(0, width, WIDE):
                    span = slice(left, left + WIDE)
                    total = sum(
                        refs[index][start : start + rows, span].astype(jnp.float32)
                        for index, start in terms
                    )
                    out[at : at + rows, span] = total.astype(out.dtype)
            at += rows


def combine(inputs, plans, after=(), flops=0):
    width = inputs[0].shape[1]
    return pl.pallas_call(
        functools.partial(combine_kernel, len(inputs), plans),
        out_shape=[
            jax.ShapeDtypeStruct((sum(rows for rows, _ in plan), width), jnp.bfloat16)
            for plan in plans
        ],
        in_specs=[whole] * len(inputs) + [pl.BlockSpec(memory_space=pl.ANY)] * len(after),
        out_specs=[whole] * len(plans),
        compiler_params=pltpu.CompilerParams(vmem_limit_bytes=SMALL_BYTES),
        cost_estimate=pl.CostEstimate(
            flops=flops, bytes_accessed=4 * width * inputs[0].shape[0], transcendentals=0
        ),
        name="combine",
    )(*inputs, *after)


def expert_kernel(picks, after, own, other, w_gate, w_up, w_down, *refs):
    *outs, rows, hidden = refs[after:]
    expert_body(picks, own, other, w_gate, w_up, w_down, outs, rows, hidden)


def expert_body(
    picks, own, other, w_gate, w_up, w_down, outs, rows, hidden, ready=lambda number: None
):
    h_own, *outs = outs
    count, feature, half = own.shape[0], w_gate.shape[1], w_gate.shape[2]
    wanted = expert_index().astype(jnp.float32)
    shares = []
    for ref, at in ((own, 0), (other, count)):
        rows[at : at + count, :] = ref[:, :feature]
        columns = ref[:, feature:].astype(jnp.float32)
        value = columns[:, picks : 2 * picks] + columns[:, 2 * picks : 3 * picks]
        named = columns[:, :picks] == wanted
        shares.append(jnp.sum(jnp.where(named, value, 0.0), axis=1, keepdims=True))
    share = jnp.concatenate(shares, axis=0)
    for at in range(0, half, TILE):
        ready(at // TILE * 2)
        gate_part = jnp.dot(
            rows[...], w_gate[0, :, at : at + TILE], preferred_element_type=jnp.float32
        )
        ready(at // TILE * 2 + 1)
        up_part = jnp.dot(
            rows[...], w_up[0, :, at : at + TILE], preferred_element_type=jnp.float32
        )
        product = gate_part / (1.0 + jnp.exp(-gate_part)) * up_part * share
        hidden[:, at : at + TILE] = product.astype(jnp.bfloat16)
    h_own[...] = hidden[:count, :]
    wide = feature // BLOCKS
    for at in range(0, feature, wide):
        ready(half // TILE * 2 + at // wide)
        part = jnp.dot(
            hidden[count:, :], w_down[0, :, at : at + wide], preferred_element_type=jnp.float32
        ).astype(jnp.bfloat16)
        top = 0
        for out in outs:
            out[:, at : at + wide] = part[top : top + out.shape[0], :]
            top += out.shape[0]


def first_kernel(picks, own, other, gate_far, up_far, down_far, *refs):
    outs, (w_gate, w_up, w_down, rows, hidden, sems) = refs[:-6], refs[-6:]
    feature, half = w_gate.shape[1], w_gate.shape[2]
    depth = feature // BLOCKS
    groups = []

    def begin(pairs):
        copies = []
        for source, target, index in pairs:
            at = len(copies) + sum(len(group) for group in groups)
            copies.append(pltpu.make_async_copy(source.at[index], target.at[index], sems.at[at]))
        for copy in copies:
            copy.start()
        groups.append(copies)

    for left in range(0, half, TILE):
        for source, target in ((gate_far, w_gate), (up_far, w_up)):
            begin(
                (source, target, (0, pl.ds(top, depth), pl.ds(left, TILE)))
                for top in range(0, feature, depth)
            )
    for left in range(0, feature, feature // BLOCKS):
        begin([(down_far, w_down, (0, slice(None), pl.ds(left, feature // BLOCKS)))])

    def ready(number):
        for copy in groups[number]:
            copy.wait()

    expert_body(picks, own, other, w_gate, w_up, w_down, outs, rows, hidden, ready)


def first_of(own, other, w_gate, w_up, w_down, picks, cuts):
    count = own.shape[0]
    _, feature, half = w_gate.shape
    copies = 2 * (half // TILE) * BLOCKS + BLOCKS
    return pl.pallas_call(
        functools.partial(first_kernel, picks),
        out_shape=[jax.ShapeDtypeStruct((count, half), jnp.bfloat16)]
        + [jax.ShapeDtypeStruct((cut, feature), jnp.bfloat16) for cut in cuts]
        + [jax.ShapeDtypeStruct(w.shape, w.dtype) for w in (w_gate, w_up, w_down)],
        in_specs=[whole] * 2 + [pl.BlockSpec(memory_space=pl.ANY)] * 3,
        out_specs=[whole] * (len(cuts) + 4),
        scratch_shapes=[
            pltpu.VMEM((2 * count, feature), jnp.bfloat16),
            pltpu.VMEM((2 * count, half), jnp.bfloat16),
            pltpu.SemaphoreType.DMA((copies,)),
        ],
        compiler_params=pltpu.CompilerParams(vmem_limit_bytes=FIRST_BYTES),
        cost_estimate=pl.CostEstimate(
            flops=10 * count * feature * half,
            bytes_accessed=6 * feature * half,
            transcendentals=2 * count * half,
        ),
        name="first",
    )(own, other, w_gate, w_up, w_down)


def expert_of(own, other, w_gate, w_up, w_down, picks, cuts, after=()):
    count = own.shape[0]
    _, feature, half = w_gate.shape
    return pl.pallas_call(
        functools.partial(expert_kernel, picks, len(after)),
        out_shape=[jax.ShapeDtypeStruct((count, half), jnp.bfloat16)]
        + [jax.ShapeDtypeStruct((cut, feature), jnp.bfloat16) for cut in cuts],
        in_specs=[whole] * 5 + [pl.BlockSpec(memory_space=pl.ANY)] * len(after),
        out_specs=[whole] * (len(cuts) + 1),
        scratch_shapes=[
            pltpu.VMEM((2 * count, feature), jnp.bfloat16),
            pltpu.VMEM((2 * count, half), jnp.bfloat16),
        ],
        compiler_params=pltpu.CompilerParams(vmem_limit_bytes=LARGE_BYTES),
        cost_estimate=pl.CostEstimate(
            flops=10 * count * feature * half,
            bytes_accessed=2 * count * feature,
            transcendentals=2 * count * half,
        ),
        name="expert",
    )(own, other, w_gate, w_up, w_down, *after)


def sums_kernel(parts, cuts, hidden, w_down, *refs):
    arrived, outs = refs[:parts], refs[len(refs) - len(cuts) :]
    feature = w_down.shape[2]
    for column in range(0, feature, 2 * TILE):
        span = slice(column, column + 2 * TILE)
        part = jnp.dot(hidden[...], w_down[0, :, span], preferred_element_type=jnp.float32)
        other = jnp.concatenate([term[:, span] for term in arrived], axis=0)
        part = (part + other.astype(jnp.float32)).astype(jnp.bfloat16)
        top = 0
        for cut, out in zip(cuts, outs):
            out[:, span] = part[top : top + cut, :]
            top += cut


def sums_of(hidden, w_down, arrived, cuts, after=()):
    count, half = hidden.shape
    feature = w_down.shape[2]
    return pl.pallas_call(
        functools.partial(sums_kernel, len(arrived), cuts),
        out_shape=[jax.ShapeDtypeStruct((cut, feature), jnp.bfloat16) for cut in cuts],
        in_specs=[whole] * (2 + len(arrived)) + [pl.BlockSpec(memory_space=pl.ANY)] * len(after),
        out_specs=[whole] * len(cuts),
        compiler_params=pltpu.CompilerParams(vmem_limit_bytes=SMALL_BYTES),
        cost_estimate=pl.CostEstimate(
            flops=2 * count * feature * half,
            bytes_accessed=2 * count * feature,
            transcendentals=0,
        ),
        name="sums",
    )(hidden, w_down, *arrived, *after)


def mix_large(packed, weights, picks, steps):
    w_gate, w_up, w_down = weights
    z_near, z_far, x_steps, y_steps, core = steps
    near = spread(packed, z_near)
    far = spread(swap(packed, z_far), z_near)
    near_x, near_y = others(near, x_steps), others(near, y_steps)
    far_x, far_y = others(far, x_steps), others(far, y_steps)
    near_xy, far_xy = others(near_x, y_steps), others(far_y, x_steps)
    early = [near, near_x, near_y, far, far_x, far_y]
    late = [near_xy, far_xy]
    early_cuts = [group.shape[0] for group in early]
    late_cuts = [group.shape[0] for group in late]
    early_own, late_own = jnp.concatenate(early, axis=0), jnp.concatenate(late, axis=0)
    early_other, late_other = swap(early_own, core), swap(late_own, core)
    early_h, early_h_other = hidden_of(early_own, early_other, w_gate, w_up, picks)
    late_h, late_h_other = hidden_of(late_own, late_other, w_gate, w_up, picks)
    (late_out,) = down_of(late_h_other, w_down, [late_h_other.shape[0]])
    late_in = swap(late_out, core)
    (early_out,) = down_of(early_h_other, w_down, [early_h_other.shape[0]])
    early_in = swap(early_out, core)
    near_xy, far_xy = down_of(late_h, w_down, late_cuts, late_in)
    near, near_x, near_y, far, far_x, far_y = down_of(early_h, w_down, early_cuts, early_in)
    rows, count = near.shape[0], packed.shape[0]
    near_x = add_up(near_x, give_back(near_xy, y_steps, near_x.shape[0]))
    far_y = add_up(far_y, give_back(far_xy, x_steps, far_y.shape[0]))
    far = add_up(far, give_back(far_x, x_steps, rows) + give_back(far_y, y_steps, rows))
    near = add_up(near, give_back(near_y, y_steps, rows) + give_back(near_x, x_steps, rows))
    far = add_up(far[:count], give_back(far[count:], z_near, count))
    return add_up(near[:count], give_back(near[count:], z_near, count) + [swap(far, z_far)])


def mix_small(packed, weights, picks, steps, attention):
    z_near, z_far, x, y, core = steps
    n = packed.shape[0]

    def rows_of(*segments):
        return [(count, [(index, start)]) for index, start, count in segments]

    from_near = swap(packed, z_near)
    from_far = swap(packed, z_far)
    (near,) = combine([packed, from_near], [rows_of((0, 0, n), (1, 0, n))])
    near_x, near_y = swap(near, x), swap(near, y)
    from_both = swap(from_far, z_near)
    first_own, far, way_x, way_y = combine(
        [near, near_x, near_y, from_far, from_both],
        [
            rows_of((0, 0, 2 * n), (1, 0, 2 * n), (2, 0, 2 * n), (3, 0, n), (4, 0, n)),
            rows_of((3, 0, n), (4, 0, n)),
            rows_of((3, 0, n), (4, 0, n), (2, n, n)),
            rows_of((3, 0, n), (4, 0, n), (1, 0, n)),
        ],
    )
    first_other = swap(first_own, core)
    far_xy, far_x, far_y = across(far, x, y), swap(way_x, x), swap(way_y, y)
    first_h, first_out, *weights = first_of(first_own, first_other, *weights, picks, [8 * n])
    w_down = weights[2]
    first_in = swap(first_out, core)
    context, done = attention([first_out])
    (second_own,) = combine(
        [far_x, far_y, far_xy],
        [
            rows_of(
                (0, 0, 2 * n), (1, 0, 2 * n), (2, n, n), (2, 0, n), (1, 2 * n, n), (0, 2 * n, n)
            )
        ],
        [done],
    )
    second_other = swap(second_own, core)
    near, near_x, near_y, far_sum, both_sum = sums_of(
        first_h, w_down, [first_in], [2 * n] * 3 + [n] * 2
    )
    to_near = [swap(near_x, x), swap(near_y, y)]
    second_h, *second_out = expert_of(
        second_own, second_other, *weights, picks, [2 * n, 2 * n, 4 * n], [near]
    )
    second_in = [swap(part, core) for part in second_out]

    def all_of(terms, start, count=n):
        return [(count, [(index, start) for index in range(terms)])]

    (near,) = combine([near, *to_near], [all_of(3, 0, 2 * n)], flops=NEAR_FLOPS)
    far_x, both_x, far_y, both_y, both_xy, corner = sums_of(
        second_h, w_down, second_in, [n] * 5 + [3 * n], [near]
    )

    to_both = [across(both_xy, x, y), swap(both_x, x), swap(both_y, y)]
    to_rest = [across(corner, x, y), swap(far_x, x), swap(far_y, y)]
    (both_sum,) = combine([both_sum, *to_both], [all_of(4, 0)])
    far_sum, near_sum = combine(
        [far_sum, *to_rest, near], [all_of(4, 0), [(n, [(1, 2 * n), (4, n)])]], [both_sum]
    )
    from_both = across(both_sum, z_far, z_near)
    (own_sum,) = combine(
        [near, to_rest[0], from_both],
        [[(n, [(0, 0), (1, n), (2, 0)])]],
        [near_sum],
        flops=FAR_FLOPS,
    )
    (mixed,) = combine(
        [own_sum, swap(far_sum, z_far), swap(near_sum, z_near)], [all_of(3, 0)]
    )
    return mixed, context


def per_device(queries, cache, lengths, live_rows, tokens, ids, gates, w_gate, w_up, w_down):
    picks = ids.shape[1]
    grp_bits = bits_of(lax.axis_size("grp"))
    ep_bits = bits_of(lax.axis_size("ep"))
    core = ("grp", 1)
    z_near = [("grp", bit) for bit in reversed(grp_bits[1:-1])]
    z_far = ("grp", grp_bits[-1])
    x_steps = [("ep", bit) for bit in ep_bits[: len(ep_bits) // 2]]
    y_steps = [("ep", bit) for bit in ep_bits[len(ep_bits) // 2 :]]

    packed = pack(tokens, ids, gates)
    weights = (w_gate, w_up, w_down)
    if len(z_near) == len(x_steps) == len(y_steps) == 1:
        steps = (z_near[0], z_far, x_steps[0], y_steps[0], core)
        attention = functools.partial(attend, queries, cache, lengths, live_rows)
        mixed, context = mix_small(packed, weights, picks, steps, attention)
    else:
        steps = (z_near, z_far, x_steps, y_steps, core)
        mixed = mix_large(packed, weights, picks, steps)
        context, _ = attend(queries, cache, lengths, live_rows)
    return (context, mixed)


def solution(mesh):
    rows3 = P(AXES, None, None)
    rows2 = P(AXES, None)
    rows1 = P(AXES)
    return jax.shard_map(
        per_device,
        mesh=mesh,
        in_specs=(rows3, rows3, rows1, rows1, rows2, rows2, rows2, rows3, rows3, rows3),
        out_specs=(rows3, rows2),
        check_vma=False,
    )
```

```python
import functools

import jax
import jax.numpy as jnp
from jax import lax
from jax.experimental import pallas as pl
from jax.experimental.pallas import tpu as pltpu
from jax.sharding import PartitionSpec as P

LAT = 512
AXES = ("grp", "ep")
EXTRA = 128
BLOCKS = 4
TILE = 256
WIDE = 512
NEAR_FLOPS = 4 * 10**9
FAR_FLOPS = 4 * 10**9
VMEM_BYTES = 48 * 1024 * 1024
LARGE_BYTES = 16 * 1024 * 1024
SMALL_BYTES = 8 * 1024 * 1024
FIRST_BYTES = 39 * 1024 * 1024
whole = pl.BlockSpec(memory_space=pltpu.VMEM)

score_scale = 192.0 ** (-0.5)
neg_large = -1e30


def attend_kernel(lengths, live_rows, queries, channels, *refs):
    out, done = refs[-2:]
    count, heads, _ = queries.shape
    positions = lax.broadcasted_iota(jnp.int32, (heads, channels.shape[2]), 1)
    for request in range(count):
        scores = jnp.dot(
            queries[request], channels[request], preferred_element_type=jnp.float32
        )
        inside = positions < lengths[request]
        masked = jnp.where(inside, scores * score_scale, neg_large)
        highest = jnp.max(masked, axis=1, keepdims=True)
        powers = jnp.where(inside, jnp.exp(masked - highest), 0.0)
        totals = jnp.sum(powers, axis=1, keepdims=True)
        weights = (powers / totals).astype(jnp.bfloat16)
        context = lax.dot_general(
            weights,
            channels[request, :LAT, :],
            (((1,), (1,)), ((), ())),
            preferred_element_type=jnp.float32,
        )
        out[request] = jnp.where(request < live_rows[0], context, 0.0).astype(jnp.bfloat16)
    done[...] = jnp.zeros_like(done)


def attend(queries, cache, lengths, live_rows, after=()):
    count, heads, width = queries.shape
    positions = cache.shape[1]
    return pl.pallas_call(
        attend_kernel,
        out_shape=[
            jax.ShapeDtypeStruct((count, heads, LAT), jnp.bfloat16),
            jax.ShapeDtypeStruct((8, 128), jnp.float32),
        ],
        in_specs=[pl.BlockSpec(memory_space=pltpu.SMEM)] * 2
        + [whole] * 2
        + [pl.BlockSpec(memory_space=pl.ANY)] * len(after),
        out_specs=[whole] * 2,
        compiler_params=pltpu.CompilerParams(vmem_limit_bytes=SMALL_BYTES),
        cost_estimate=pl.CostEstimate(
            flops=4 * count * heads * width * positions,
            bytes_accessed=2 * count * positions * width,
            transcendentals=count * heads * positions,
        ),
        name="attend",
    )(lengths, live_rows, queries, jnp.swapaxes(cache, 1, 2), *after)


def bits_of(count):
    return [1 << i for i in range(count.bit_length() - 1)]


def swap(value, step):
    axis, bit = step
    size = lax.axis_size(axis)
    return lax.ppermute(value, axis, [(i, i ^ bit) for i in range(size)])


def across(value, first, second):
    axis = first[0]
    size = lax.axis_size(axis)
    return lax.ppermute(value, axis, [(i, i ^ first[1] ^ second[1]) for i in range(size)])


def spread(value, steps):
    for step in steps:
        value = jnp.concatenate([value, swap(value, step)], axis=0)
    return value


def others(value, steps):
    if len(steps) == 1:
        return swap(value, steps[0])
    return spread(value, steps)[value.shape[0] :]


def give_back(rest, steps, rows):
    terms = []
    for step in reversed(steps):
        keep = (rest.shape[0] + rows) // 2 - rows
        arrived = swap(rest[keep:], step)
        terms.append(arrived[:rows])
        if keep:
            rest = add_up(rest[:keep], [arrived[rows:]])
    return terms


def add_up(own, terms):
    total = own.astype(jnp.float32)
    for term in terms:
        total = total + term.astype(jnp.float32)
    return total.astype(jnp.bfloat16)


def pack_kernel(tokens, chosen, out):
    feature = tokens.shape[1]
    picks = chosen.shape[0] // 2
    gates = chosen[picks:, :]
    high = gates.astype(jnp.bfloat16).astype(jnp.float32)
    stacked = jnp.concatenate([chosen[:picks, :], high, gates - high], axis=0)
    stacked = stacked.astype(jnp.bfloat16)
    row = lax.broadcasted_iota(jnp.int32, (stacked.shape[0], EXTRA), 0)
    column = lax.broadcasted_iota(jnp.int32, (stacked.shape[0], EXTRA), 1)
    place = jnp.where(row == column, 1.0, 0.0).astype(jnp.bfloat16)
    extra = lax.dot_general(
        stacked, place, (((0,), (0,)), ((), ())), preferred_element_type=jnp.float32
    )
    out[:, :feature] = tokens[...]
    out[:, feature:] = extra.astype(jnp.bfloat16)


def pack(tokens, ids, gates):
    picks = ids.shape[1]
    chosen = lax.pad(ids.T, 0, ((0, picks, 0), (0, 0, 0))).astype(jnp.float32)
    chosen = chosen + lax.pad(gates.T, 0.0, ((picks, 0, 0), (0, 0, 0)))
    return pl.pallas_call(
        pack_kernel,
        out_shape=jax.ShapeDtypeStruct((tokens.shape[0], tokens.shape[1] + EXTRA), jnp.bfloat16),
        in_specs=[whole] * 2,
        out_specs=whole,
        compiler_params=pltpu.CompilerParams(vmem_limit_bytes=SMALL_BYTES),
        name="pack",
    )(tokens, chosen)


def expert_index():
    return (lax.axis_index("grp") * lax.axis_size("ep") + lax.axis_index("ep")) // 2


def hidden_kernel(picks, own, other, extra_own, extra_other, w_gate, w_up, h_own, h_other, gate_sum, up_sum):
    step = pl.program_id(0)
    rows = jnp.concatenate([own[...], other[...]], axis=0)
    gate_part = jnp.dot(rows, w_gate[0], preferred_element_type=jnp.float32)
    up_part = jnp.dot(rows, w_up[0], preferred_element_type=jnp.float32)

    @pl.when(step == 0)
    def _():
        gate_sum[...] = gate_part
        up_sum[...] = up_part

    @pl.when(step > 0)
    def _():
        gate_sum[...] += gate_part
        up_sum[...] += up_part

    @pl.when(step == pl.num_programs(0) - 1)
    def _():
        count = own.shape[0]
        wanted = expert_index().astype(jnp.float32)
        for extra, out, at in ((extra_own, h_own, 0), (extra_other, h_other, count)):
            columns = extra[...].astype(jnp.float32)
            value = columns[:, picks : 2 * picks] + columns[:, 2 * picks : 3 * picks]
            share = jnp.sum(
                jnp.where(columns[:, :picks] == wanted, value, 0.0), axis=1, keepdims=True
            )
            gate_all = gate_sum[at : at + count, :]
            up_all = up_sum[at : at + count, :]
            hidden = gate_all / (1.0 + jnp.exp(-gate_all)) * up_all
            out[...] = (hidden * share).astype(jnp.bfloat16)


def hidden_of(own, other, w_gate, w_up, picks):
    count, width = own.shape
    _, feature, half = w_gate.shape
    depth = feature // BLOCKS
    rows_spec = pl.BlockSpec((count, depth), lambda k: (0, k))
    extra_spec = pl.BlockSpec((count, EXTRA), lambda k: (0, feature // EXTRA))
    weight_spec = pl.BlockSpec((1, depth, half), lambda k: (0, k, 0))
    out_spec = pl.BlockSpec((count, half), lambda k: (0, 0))
    return pl.pallas_call(
        functools.partial(hidden_kernel, picks),
        grid=(BLOCKS,),
        out_shape=[jax.ShapeDtypeStruct((count, half), jnp.bfloat16)] * 2,
        in_specs=[rows_spec] * 2 + [extra_spec] * 2 + [weight_spec] * 2,
        out_specs=[out_spec] * 2,
        scratch_shapes=[pltpu.VMEM((2 * count, half), jnp.float32)] * 2,
        compiler_params=pltpu.CompilerParams(vmem_limit_bytes=VMEM_BYTES),
        cost_estimate=pl.CostEstimate(
            flops=8 * count * feature * half,
            bytes_accessed=4 * feature * half + 4 * count * width,
            transcendentals=2 * count * half,
        ),
        name="hidden",
    )(own, other, own, other, w_gate, w_up)


def down_kernel(cuts, hidden, w_down, *refs):
    part = jnp.dot(hidden[...], w_down[0], preferred_element_type=jnp.float32)
    if len(refs) > len(cuts):
        part = part + refs[0][...].astype(jnp.float32)
        refs = refs[1:]
    at = 0
    for cut, out in zip(cuts, refs):
        out[...] = part[at : at + cut, :].astype(jnp.bfloat16)
        at += cut


def down_of(hidden, w_down, cuts, arrived=None):
    count, half = hidden.shape
    feature = w_down.shape[2]
    wide = feature // BLOCKS
    operands = [hidden, w_down]
    in_specs = [
        pl.BlockSpec((count, half), lambda n: (0, 0)),
        pl.BlockSpec((1, half, wide), lambda n: (0, 0, n)),
    ]
    if arrived is not None:
        operands.append(arrived)
        in_specs.append(pl.BlockSpec((count, wide), lambda n: (0, n)))
    return pl.pallas_call(
        functools.partial(down_kernel, cuts),
        grid=(BLOCKS,),
        out_shape=[jax.ShapeDtypeStruct((cut, feature), jnp.bfloat16) for cut in cuts],
        in_specs=in_specs,
        out_specs=[pl.BlockSpec((cut, wide), lambda n: (0, n)) for cut in cuts],
        compiler_params=pltpu.CompilerParams(vmem_limit_bytes=VMEM_BYTES),
        cost_estimate=pl.CostEstimate(
            flops=2 * count * feature * half,
            bytes_accessed=2 * feature * half + 4 * count * feature,
            transcendentals=0,
        ),
        name="down",
    )(*operands)


def combine_kernel(count, plans, *refs):
    outs = refs[len(refs) - len(plans) :]
    width = outs[0].shape[1]
    for plan, out in zip(plans, outs):
        at = 0
        for rows, terms in plan:
            if len(terms) == 1:
                index, start = terms[0]
                out[at : at + rows, :] = refs[index][start : start + rows, :]
            else:
                for left in range(0, width, WIDE):
                    span = slice(left, left + WIDE)
                    total = sum(
                        refs[index][start : start + rows, span].astype(jnp.float32)
                        for index, start in terms
                    )
                    out[at : at + rows, span] = total.astype(out.dtype)
            at += rows


def combine(inputs, plans, after=(), flops=0):
    width = inputs[0].shape[1]
    return pl.pallas_call(
        functools.partial(combine_kernel, len(inputs), plans),
        out_shape=[
            jax.ShapeDtypeStruct((sum(rows for rows, _ in plan), width), jnp.bfloat16)
            for plan in plans
        ],
        in_specs=[whole] * len(inputs) + [pl.BlockSpec(memory_space=pl.ANY)] * len(after),
        out_specs=[whole] * len(plans),
        compiler_params=pltpu.CompilerParams(vmem_limit_bytes=SMALL_BYTES),
        cost_estimate=pl.CostEstimate(
            flops=flops, bytes_accessed=4 * width * inputs[0].shape[0], transcendentals=0
        ),
        name="combine",
    )(*inputs, *after)


def expert_kernel(picks, after, own, other, w_gate, w_up, w_down, *refs):
    *outs, rows, hidden = refs[after:]
    expert_body(picks, own, other, w_gate, w_up, w_down, outs, rows, hidden)


def expert_body(
    picks, own, other, w_gate, w_up, w_down, outs, rows, hidden, ready=lambda number: None
):
    h_own, *outs = outs
    count, feature, half = own.shape[0], w_gate.shape[1], w_gate.shape[2]
    wanted = expert_index().astype(jnp.float32)
    shares = []
    for ref, at in ((own, 0), (other, count)):
        rows[at : at + count, :] = ref[:, :feature]
        columns = ref[:, feature:].astype(jnp.float32)
        value = columns[:, picks : 2 * picks] + columns[:, 2 * picks : 3 * picks]
        named = columns[:, :picks] == wanted
        shares.append(jnp.sum(jnp.where(named, value, 0.0), axis=1, keepdims=True))
    share = jnp.concatenate(shares, axis=0)
    for at in range(0, half, TILE):
        ready(at // TILE * 2)
        gate_part = jnp.dot(
            rows[...], w_gate[0, :, at : at + TILE], preferred_element_type=jnp.float32
        )
        ready(at // TILE * 2 + 1)
        up_part = jnp.dot(
            rows[...], w_up[0, :, at : at + TILE], preferred_element_type=jnp.float32
        )
        product = gate_part / (1.0 + jnp.exp(-gate_part)) * up_part * share
        hidden[:, at : at + TILE] = product.astype(jnp.bfloat16)
    h_own[...] = hidden[:count, :]
    wide = feature // BLOCKS
    for at in range(0, feature, wide):
        ready(half // TILE * 2 + at // wide)
        part = jnp.dot(
            hidden[count:, :], w_down[0, :, at : at + wide], preferred_element_type=jnp.float32
        ).astype(jnp.bfloat16)
        top = 0
        for out in outs:
            out[:, at : at + wide] = part[top : top + out.shape[0], :]
            top += out.shape[0]


def first_kernel(picks, own, other, gate_far, up_far, down_far, *refs):
    outs, (w_gate, w_up, w_down, rows, hidden, sems) = refs[:-6], refs[-6:]
    feature, half = w_gate.shape[1], w_gate.shape[2]
    depth = feature // BLOCKS
    groups = []

    def begin(pairs):
        copies = []
        for source, target, index in pairs:
            at = len(copies) + sum(len(group) for group in groups)
            copies.append(pltpu.make_async_copy(source.at[index], target.at[index], sems.at[at]))
        for copy in copies:
            copy.start()
        groups.append(copies)

    for left in range(0, half, TILE):
        for source, target in ((gate_far, w_gate), (up_far, w_up)):
            begin(
                (source, target, (0, pl.ds(top, depth), pl.ds(left, TILE)))
                for top in range(0, feature, depth)
            )
    for left in range(0, feature, feature // BLOCKS):
        begin([(down_far, w_down, (0, slice(None), pl.ds(left, feature // BLOCKS)))])

    def ready(number):
        for copy in groups[number]:
            copy.wait()

    expert_body(picks, own, other, w_gate, w_up, w_down, outs, rows, hidden, ready)


def first_of(own, other, w_gate, w_up, w_down, picks, cuts):
    count = own.shape[0]
    _, feature, half = w_gate.shape
    copies = 2 * (half // TILE) * BLOCKS + BLOCKS
    return pl.pallas_call(
        functools.partial(first_kernel, picks),
        out_shape=[jax.ShapeDtypeStruct((count, half), jnp.bfloat16)]
        + [jax.ShapeDtypeStruct((cut, feature), jnp.bfloat16) for cut in cuts]
        + [jax.ShapeDtypeStruct(w.shape, w.dtype) for w in (w_gate, w_up, w_down)],
        in_specs=[whole] * 2 + [pl.BlockSpec(memory_space=pl.ANY)] * 3,
        out_specs=[whole] * (len(cuts) + 4),
        scratch_shapes=[
            pltpu.VMEM((2 * count, feature), jnp.bfloat16),
            pltpu.VMEM((2 * count, half), jnp.bfloat16),
            pltpu.SemaphoreType.DMA((copies,)),
        ],
        compiler_params=pltpu.CompilerParams(vmem_limit_bytes=FIRST_BYTES),
        cost_estimate=pl.CostEstimate(
            flops=10 * count * feature * half,
            bytes_accessed=6 * feature * half,
            transcendentals=2 * count * half,
        ),
        name="first",
    )(own, other, w_gate, w_up, w_down)


def expert_of(own, other, w_gate, w_up, w_down, picks, cuts, after=()):
    count = own.shape[0]
    _, feature, half = w_gate.shape
    return pl.pallas_call(
        functools.partial(expert_kernel, picks, len(after)),
        out_shape=[jax.ShapeDtypeStruct((count, half), jnp.bfloat16)]
        + [jax.ShapeDtypeStruct((cut, feature), jnp.bfloat16) for cut in cuts],
        in_specs=[whole] * 5 + [pl.BlockSpec(memory_space=pl.ANY)] * len(after),
        out_specs=[whole] * (len(cuts) + 1),
        scratch_shapes=[
            pltpu.VMEM((2 * count, feature), jnp.bfloat16),
            pltpu.VMEM((2 * count, half), jnp.bfloat16),
        ],
        compiler_params=pltpu.CompilerParams(vmem_limit_bytes=LARGE_BYTES),
        cost_estimate=pl.CostEstimate(
            flops=10 * count * feature * half,
            bytes_accessed=2 * count * feature,
            transcendentals=2 * count * half,
        ),
        name="expert",
    )(own, other, w_gate, w_up, w_down, *after)


def sums_kernel(parts, cuts, hidden, w_down, *refs):
    arrived, outs = refs[:parts], refs[len(refs) - len(cuts) :]
    feature = w_down.shape[2]
    for column in range(0, feature, 2 * TILE):
        span = slice(column, column + 2 * TILE)
        part = jnp.dot(hidden[...], w_down[0, :, span], preferred_element_type=jnp.float32)
        other = jnp.concatenate([term[:, span] for term in arrived], axis=0)
        part = (part + other.astype(jnp.float32)).astype(jnp.bfloat16)
        top = 0
        for cut, out in zip(cuts, outs):
            out[:, span] = part[top : top + cut, :]
            top += cut


def sums_of(hidden, w_down, arrived, cuts, after=()):
    count, half = hidden.shape
    feature = w_down.shape[2]
    return pl.pallas_call(
        functools.partial(sums_kernel, len(arrived), cuts),
        out_shape=[jax.ShapeDtypeStruct((cut, feature), jnp.bfloat16) for cut in cuts],
        in_specs=[whole] * (2 + len(arrived)) + [pl.BlockSpec(memory_space=pl.ANY)] * len(after),
        out_specs=[whole] * len(cuts),
        compiler_params=pltpu.CompilerParams(vmem_limit_bytes=SMALL_BYTES),
        cost_estimate=pl.CostEstimate(
            flops=2 * count * feature * half,
            bytes_accessed=2 * count * feature,
            transcendentals=0,
        ),
        name="sums",
    )(hidden, w_down, *arrived, *after)


def mix_large(packed, weights, picks, steps):
    w_gate, w_up, w_down = weights
    z_near, z_far, x_steps, y_steps, core = steps
    near = spread(packed, z_near)
    far = spread(swap(packed, z_far), z_near)
    near_x, near_y = others(near, x_steps), others(near, y_steps)
    far_x, far_y = others(far, x_steps), others(far, y_steps)
    near_xy, far_xy = others(near_x, y_steps), others(far_y, x_steps)
    early = [near, near_x, near_y, far, far_x, far_y]
    late = [near_xy, far_xy]
    early_cuts = [group.shape[0] for group in early]
    late_cuts = [group.shape[0] for group in late]
    early_own, late_own = jnp.concatenate(early, axis=0), jnp.concatenate(late, axis=0)
    early_other, late_other = swap(early_own, core), swap(late_own, core)
    early_h, early_h_other = hidden_of(early_own, early_other, w_gate, w_up, picks)
    late_h, late_h_other = hidden_of(late_own, late_other, w_gate, w_up, picks)
    (late_out,) = down_of(late_h_other, w_down, [late_h_other.shape[0]])
    late_in = swap(late_out, core)
    (early_out,) = down_of(early_h_other, w_down, [early_h_other.shape[0]])
    early_in = swap(early_out, core)
    near_xy, far_xy = down_of(late_h, w_down, late_cuts, late_in)
    near, near_x, near_y, far, far_x, far_y = down_of(early_h, w_down, early_cuts, early_in)
    rows, count = near.shape[0], packed.shape[0]
    near_x = add_up(near_x, give_back(near_xy, y_steps, near_x.shape[0]))
    far_y = add_up(far_y, give_back(far_xy, x_steps, far_y.shape[0]))
    far = add_up(far, give_back(far_x, x_steps, rows) + give_back(far_y, y_steps, rows))
    near = add_up(near, give_back(near_y, y_steps, rows) + give_back(near_x, x_steps, rows))
    far = add_up(far[:count], give_back(far[count:], z_near, count))
    return add_up(near[:count], give_back(near[count:], z_near, count) + [swap(far, z_far)])


def mix_small(packed, weights, picks, steps, attention):
    z_near, z_far, x, y, core = steps
    n = packed.shape[0]

    def rows_of(*segments):
        return [(count, [(index, start)]) for index, start, count in segments]

    from_near = swap(packed, z_near)
    from_far = swap(packed, z_far)
    (near,) = combine([packed, from_near], [rows_of((0, 0, n), (1, 0, n))])
    near_x, near_y = swap(near, x), swap(near, y)
    from_both = swap(from_far, z_near)
    first_own, far, way_x, way_y = combine(
        [near, near_x, near_y, from_far, from_both],
        [
            rows_of((0, 0, 2 * n), (1, 0, 2 * n), (2, 0, 2 * n), (3, 0, n), (4, 0, n)),
            rows_of((3, 0, n), (4, 0, n)),
            rows_of((3, 0, n), (4, 0, n), (2, n, n)),
            rows_of((3, 0, n), (4, 0, n), (1, 0, n)),
        ],
    )
    first_other = swap(first_own, core)
    far_xy, far_x, far_y = across(far, x, y), swap(way_x, x), swap(way_y, y)
    first_h, first_out, *weights = first_of(first_own, first_other, *weights, picks, [8 * n])
    w_down = weights[2]
    first_in = swap(first_out, core)
    context, done = attention([first_out])
    (second_own,) = combine(
        [far_x, far_y, far_xy],
        [rows_of((0, 0, 2 * n), (1, 0, 2 * n), (2, 0, 2 * n), (1, 2 * n, n), (0, 2 * n, n))],
        [done],
    )
    second_other = swap(second_own, core)
    near, near_x, near_y, far_sum, both_sum = sums_of(
        first_h, w_down, [first_in], [2 * n] * 3 + [n] * 2
    )
    to_near = [swap(near_x, x), swap(near_y, y)]
    second_h, *second_out = expert_of(
        second_own, second_other, *weights, picks, [2 * n, 2 * n, 4 * n], [near]
    )
    second_in = [swap(part, core) for part in second_out]

    def all_of(terms, start, count=n):
        return [(count, [(index, start) for index in range(terms)])]

    (near,) = combine([near, *to_near], [all_of(3, 0, 2 * n)], flops=NEAR_FLOPS)
    far_x, both_x, far_y, both_y, far_xy, both_xy, near_xy = sums_of(
        second_h, w_down, second_in, [n] * 6 + [2 * n], [near]
    )

    to_both = [across(both_xy, x, y), swap(both_x, x), swap(both_y, y)]
    to_far = [across(far_xy, x, y), swap(far_x, x), swap(far_y, y)]
    (both_sum,) = combine([both_sum, *to_both], [all_of(4, 0)])
    to_near = across(near_xy, x, y)
    (far_sum,) = combine([far_sum, *to_far], [all_of(4, 0)], [both_sum], flops=FAR_FLOPS)
    from_both = across(both_sum, z_far, z_near)
    own_sum, near_sum = combine(
        [near, to_near, from_both], [all_of(3, 0), all_of(2, n)], [far_sum]
    )
    (mixed,) = combine(
        [own_sum, swap(far_sum, z_far), swap(near_sum, z_near)], [all_of(3, 0)]
    )
    return mixed, context


def per_device(queries, cache, lengths, live_rows, tokens, ids, gates, w_gate, w_up, w_down):
    picks = ids.shape[1]
    grp_bits = bits_of(lax.axis_size("grp"))
    ep_bits = bits_of(lax.axis_size("ep"))
    core = ("grp", 1)
    z_near = [("grp", bit) for bit in reversed(grp_bits[1:-1])]
    z_far = ("grp", grp_bits[-1])
    x_steps = [("ep", bit) for bit in ep_bits[: len(ep_bits) // 2]]
    y_steps = [("ep", bit) for bit in ep_bits[len(ep_bits) // 2 :]]

    packed = pack(tokens, ids, gates)
    weights = (w_gate, w_up, w_down)
    if len(z_near) == len(x_steps) == len(y_steps) == 1:
        steps = (z_near[0], z_far, x_steps[0], y_steps[0], core)
        attention = functools.partial(attend, queries, cache, lengths, live_rows)
        mixed, context = mix_small(packed, weights, picks, steps, attention)
    else:
        steps = (z_near, z_far, x_steps, y_steps, core)
        mixed = mix_large(packed, weights, picks, steps)
        context, _ = attend(queries, cache, lengths, live_rows)
    return (context, mixed)


def solution(mesh):
    rows3 = P(AXES, None, None)
    rows2 = P(AXES, None)
    rows1 = P(AXES)
    return jax.shard_map(
        per_device,
        mesh=mesh,
        in_specs=(rows3, rows3, rows1, rows1, rows2, rows2, rows2, rows3, rows3, rows3),
        out_specs=(rows3, rows2),
        check_vma=False,
    )
```

```python
import functools

import jax
import jax.numpy as jnp
from jax import lax
from jax.experimental import pallas as pl
from jax.experimental.pallas import tpu as pltpu
from jax.sharding import PartitionSpec as P

LAT = 512
AXES = ("grp", "ep")
EXTRA = 128
BLOCKS = 4
TILE = 256
WIDE = 512
NEAR_FLOPS = 16 * 10**9
FAR_FLOPS = 4 * 10**9
VMEM_BYTES = 48 * 1024 * 1024
LARGE_BYTES = 16 * 1024 * 1024
SMALL_BYTES = 8 * 1024 * 1024
FIRST_BYTES = 39 * 1024 * 1024
whole = pl.BlockSpec(memory_space=pltpu.VMEM)

score_scale = 192.0 ** (-0.5)
neg_large = -1e30


def attend_kernel(lengths, live_rows, queries, channels, *refs):
    out, done = refs[-2:]
    count, heads, _ = queries.shape
    positions = lax.broadcasted_iota(jnp.int32, (heads, channels.shape[2]), 1)
    for request in range(count):
        scores = jnp.dot(
            queries[request], channels[request], preferred_element_type=jnp.float32
        )
        inside = positions < lengths[request]
        masked = jnp.where(inside, scores * score_scale, neg_large)
        highest = jnp.max(masked, axis=1, keepdims=True)
        powers = jnp.where(inside, jnp.exp(masked - highest), 0.0)
        totals = jnp.sum(powers, axis=1, keepdims=True)
        weights = (powers / totals).astype(jnp.bfloat16)
        context = lax.dot_general(
            weights,
            channels[request, :LAT, :],
            (((1,), (1,)), ((), ())),
            preferred_element_type=jnp.float32,
        )
        out[request] = jnp.where(request < live_rows[0], context, 0.0).astype(jnp.bfloat16)
    done[...] = jnp.zeros_like(done)


def attend(queries, cache, lengths, live_rows, after=()):
    count, heads, width = queries.shape
    positions = cache.shape[1]
    return pl.pallas_call(
        attend_kernel,
        out_shape=[
            jax.ShapeDtypeStruct((count, heads, LAT), jnp.bfloat16),
            jax.ShapeDtypeStruct((8, 128), jnp.float32),
        ],
        in_specs=[pl.BlockSpec(memory_space=pltpu.SMEM)] * 2
        + [whole] * 2
        + [pl.BlockSpec(memory_space=pl.ANY)] * len(after),
        out_specs=[whole] * 2,
        compiler_params=pltpu.CompilerParams(vmem_limit_bytes=SMALL_BYTES),
        cost_estimate=pl.CostEstimate(
            flops=4 * count * heads * width * positions,
            bytes_accessed=2 * count * positions * width,
            transcendentals=count * heads * positions,
        ),
        name="attend",
    )(lengths, live_rows, queries, jnp.swapaxes(cache, 1, 2), *after)


def bits_of(count):
    return [1 << i for i in range(count.bit_length() - 1)]


def swap(value, step):
    axis, bit = step
    size = lax.axis_size(axis)
    return lax.ppermute(value, axis, [(i, i ^ bit) for i in range(size)])


def across(value, first, second):
    axis = first[0]
    size = lax.axis_size(axis)
    return lax.ppermute(value, axis, [(i, i ^ first[1] ^ second[1]) for i in range(size)])


def spread(value, steps):
    for step in steps:
        value = jnp.concatenate([value, swap(value, step)], axis=0)
    return value


def others(value, steps):
    if len(steps) == 1:
        return swap(value, steps[0])
    return spread(value, steps)[value.shape[0] :]


def give_back(rest, steps, rows):
    terms = []
    for step in reversed(steps):
        keep = (rest.shape[0] + rows) // 2 - rows
        arrived = swap(rest[keep:], step)
        terms.append(arrived[:rows])
        if keep:
            rest = add_up(rest[:keep], [arrived[rows:]])
    return terms


def add_up(own, terms):
    total = own.astype(jnp.float32)
    for term in terms:
        total = total + term.astype(jnp.float32)
    return total.astype(jnp.bfloat16)


def pack_kernel(tokens, chosen, out):
    feature = tokens.shape[1]
    picks = chosen.shape[0] // 2
    gates = chosen[picks:, :]
    high = gates.astype(jnp.bfloat16).astype(jnp.float32)
    stacked = jnp.concatenate([chosen[:picks, :], high, gates - high], axis=0)
    stacked = stacked.astype(jnp.bfloat16)
    row = lax.broadcasted_iota(jnp.int32, (stacked.shape[0], EXTRA), 0)
    column = lax.broadcasted_iota(jnp.int32, (stacked.shape[0], EXTRA), 1)
    place = jnp.where(row == column, 1.0, 0.0).astype(jnp.bfloat16)
    extra = lax.dot_general(
        stacked, place, (((0,), (0,)), ((), ())), preferred_element_type=jnp.float32
    )
    out[:, :feature] = tokens[...]
    out[:, feature:] = extra.astype(jnp.bfloat16)


def pack(tokens, ids, gates):
    picks = ids.shape[1]
    chosen = lax.pad(ids.T, 0, ((0, picks, 0), (0, 0, 0))).astype(jnp.float32)
    chosen = chosen + lax.pad(gates.T, 0.0, ((picks, 0, 0), (0, 0, 0)))
    return pl.pallas_call(
        pack_kernel,
        out_shape=jax.ShapeDtypeStruct((tokens.shape[0], tokens.shape[1] + EXTRA), jnp.bfloat16),
        in_specs=[whole] * 2,
        out_specs=whole,
        compiler_params=pltpu.CompilerParams(vmem_limit_bytes=SMALL_BYTES),
        name="pack",
    )(tokens, chosen)


def expert_index():
    return (lax.axis_index("grp") * lax.axis_size("ep") + lax.axis_index("ep")) // 2


def hidden_kernel(picks, own, other, extra_own, extra_other, w_gate, w_up, h_own, h_other, gate_sum, up_sum):
    step = pl.program_id(0)
    rows = jnp.concatenate([own[...], other[...]], axis=0)
    gate_part = jnp.dot(rows, w_gate[0], preferred_element_type=jnp.float32)
    up_part = jnp.dot(rows, w_up[0], preferred_element_type=jnp.float32)

    @pl.when(step == 0)
    def _():
        gate_sum[...] = gate_part
        up_sum[...] = up_part

    @pl.when(step > 0)
    def _():
        gate_sum[...] += gate_part
        up_sum[...] += up_part

    @pl.when(step == pl.num_programs(0) - 1)
    def _():
        count = own.shape[0]
        wanted = expert_index().astype(jnp.float32)
        for extra, out, at in ((extra_own, h_own, 0), (extra_other, h_other, count)):
            columns = extra[...].astype(jnp.float32)
            value = columns[:, picks : 2 * picks] + columns[:, 2 * picks : 3 * picks]
            share = jnp.sum(
                jnp.where(columns[:, :picks] == wanted, value, 0.0), axis=1, keepdims=True
            )
            gate_all = gate_sum[at : at + count, :]
            up_all = up_sum[at : at + count, :]
            hidden = gate_all / (1.0 + jnp.exp(-gate_all)) * up_all
            out[...] = (hidden * share).astype(jnp.bfloat16)


def hidden_of(own, other, w_gate, w_up, picks):
    count, width = own.shape
    _, feature, half = w_gate.shape
    depth = feature // BLOCKS
    rows_spec = pl.BlockSpec((count, depth), lambda k: (0, k))
    extra_spec = pl.BlockSpec((count, EXTRA), lambda k: (0, feature // EXTRA))
    weight_spec = pl.BlockSpec((1, depth, half), lambda k: (0, k, 0))
    out_spec = pl.BlockSpec((count, half), lambda k: (0, 0))
    return pl.pallas_call(
        functools.partial(hidden_kernel, picks),
        grid=(BLOCKS,),
        out_shape=[jax.ShapeDtypeStruct((count, half), jnp.bfloat16)] * 2,
        in_specs=[rows_spec] * 2 + [extra_spec] * 2 + [weight_spec] * 2,
        out_specs=[out_spec] * 2,
        scratch_shapes=[pltpu.VMEM((2 * count, half), jnp.float32)] * 2,
        compiler_params=pltpu.CompilerParams(vmem_limit_bytes=VMEM_BYTES),
        cost_estimate=pl.CostEstimate(
            flops=8 * count * feature * half,
            bytes_accessed=4 * feature * half + 4 * count * width,
            transcendentals=2 * count * half,
        ),
        name="hidden",
    )(own, other, own, other, w_gate, w_up)


def down_kernel(cuts, hidden, w_down, *refs):
    part = jnp.dot(hidden[...], w_down[0], preferred_element_type=jnp.float32)
    if len(refs) > len(cuts):
        part = part + refs[0][...].astype(jnp.float32)
        refs = refs[1:]
    at = 0
    for cut, out in zip(cuts, refs):
        out[...] = part[at : at + cut, :].astype(jnp.bfloat16)
        at += cut


def down_of(hidden, w_down, cuts, arrived=None):
    count, half = hidden.shape
    feature = w_down.shape[2]
    wide = feature // BLOCKS
    operands = [hidden, w_down]
    in_specs = [
        pl.BlockSpec((count, half), lambda n: (0, 0)),
        pl.BlockSpec((1, half, wide), lambda n: (0, 0, n)),
    ]
    if arrived is not None:
        operands.append(arrived)
        in_specs.append(pl.BlockSpec((count, wide), lambda n: (0, n)))
    return pl.pallas_call(
        functools.partial(down_kernel, cuts),
        grid=(BLOCKS,),
        out_shape=[jax.ShapeDtypeStruct((cut, feature), jnp.bfloat16) for cut in cuts],
        in_specs=in_specs,
        out_specs=[pl.BlockSpec((cut, wide), lambda n: (0, n)) for cut in cuts],
        compiler_params=pltpu.CompilerParams(vmem_limit_bytes=VMEM_BYTES),
        cost_estimate=pl.CostEstimate(
            flops=2 * count * feature * half,
            bytes_accessed=2 * feature * half + 4 * count * feature,
            transcendentals=0,
        ),
        name="down",
    )(*operands)


def combine_kernel(count, plans, *refs):
    outs = refs[len(refs) - len(plans) :]
    width = outs[0].shape[1]
    for plan, out in zip(plans, outs):
        at = 0
        for rows, terms in plan:
            if len(terms) == 1:
                index, start = terms[0]
                out[at : at + rows, :] = refs[index][start : start + rows, :]
            else:
                for left in range(0, width, WIDE):
                    span = slice(left, left + WIDE)
                    total = sum(
                        refs[index][start : start + rows, span].astype(jnp.float32)
                        for index, start in terms
                    )
                    out[at : at + rows, span] = total.astype(out.dtype)
            at += rows


def combine(inputs, plans, after=(), flops=0):
    width = inputs[0].shape[1]
    return pl.pallas_call(
        functools.partial(combine_kernel, len(inputs), plans),
        out_shape=[
            jax.ShapeDtypeStruct((sum(rows for rows, _ in plan), width), jnp.bfloat16)
            for plan in plans
        ],
        in_specs=[whole] * len(inputs) + [pl.BlockSpec(memory_space=pl.ANY)] * len(after),
        out_specs=[whole] * len(plans),
        compiler_params=pltpu.CompilerParams(vmem_limit_bytes=SMALL_BYTES),
        cost_estimate=pl.CostEstimate(
            flops=flops, bytes_accessed=4 * width * inputs[0].shape[0], transcendentals=0
        ),
        name="combine",
    )(*inputs, *after)


def expert_kernel(picks, after, own, other, w_gate, w_up, w_down, *refs):
    *outs, rows, hidden = refs[after:]
    expert_body(picks, own, other, w_gate, w_up, w_down, outs, rows, hidden)


def expert_body(
    picks, own, other, w_gate, w_up, w_down, outs, rows, hidden, ready=lambda number: None
):
    h_own, *outs = outs
    count, feature, half = own.shape[0], w_gate.shape[1], w_gate.shape[2]
    wanted = expert_index().astype(jnp.float32)
    shares = []
    for ref, at in ((own, 0), (other, count)):
        rows[at : at + count, :] = ref[:, :feature]
        columns = ref[:, feature:].astype(jnp.float32)
        value = columns[:, picks : 2 * picks] + columns[:, 2 * picks : 3 * picks]
        named = columns[:, :picks] == wanted
        shares.append(jnp.sum(jnp.where(named, value, 0.0), axis=1, keepdims=True))
    share = jnp.concatenate(shares, axis=0)
    for at in range(0, half, TILE):
        ready(at // TILE * 2)
        gate_part = jnp.dot(
            rows[...], w_gate[0, :, at : at + TILE], preferred_element_type=jnp.float32
        )
        ready(at // TILE * 2 + 1)
        up_part = jnp.dot(
            rows[...], w_up[0, :, at : at + TILE], preferred_element_type=jnp.float32
        )
        product = gate_part / (1.0 + jnp.exp(-gate_part)) * up_part * share
        hidden[:, at : at + TILE] = product.astype(jnp.bfloat16)
    h_own[...] = hidden[:count, :]
    wide = feature // BLOCKS
    for at in range(0, feature, wide):
        ready(half // TILE * 2 + at // wide)
        part = jnp.dot(
            hidden[count:, :], w_down[0, :, at : at + wide], preferred_element_type=jnp.float32
        ).astype(jnp.bfloat16)
        top = 0
        for out in outs:
            out[:, at : at + wide] = part[top : top + out.shape[0], :]
            top += out.shape[0]


def first_kernel(picks, own, other, gate_far, up_far, down_far, *refs):
    outs, (w_gate, w_up, w_down, rows, hidden, sems) = refs[:-6], refs[-6:]
    feature, half = w_gate.shape[1], w_gate.shape[2]
    depth = feature // BLOCKS
    groups = []

    def begin(pairs):
        copies = []
        for source, target, index in pairs:
            at = len(copies) + sum(len(group) for group in groups)
            copies.append(pltpu.make_async_copy(source.at[index], target.at[index], sems.at[at]))
        for copy in copies:
            copy.start()
        groups.append(copies)

    for left in range(0, half, TILE):
        for source, target in ((gate_far, w_gate), (up_far, w_up)):
            begin(
                (source, target, (0, pl.ds(top, depth), pl.ds(left, TILE)))
                for top in range(0, feature, depth)
            )
    for left in range(0, feature, feature // BLOCKS):
        begin([(down_far, w_down, (0, slice(None), pl.ds(left, feature // BLOCKS)))])

    def ready(number):
        for copy in groups[number]:
            copy.wait()

    expert_body(picks, own, other, w_gate, w_up, w_down, outs, rows, hidden, ready)


def first_of(own, other, w_gate, w_up, w_down, picks, cuts):
    count = own.shape[0]
    _, feature, half = w_gate.shape
    copies = 2 * (half // TILE) * BLOCKS + BLOCKS
    return pl.pallas_call(
        functools.partial(first_kernel, picks),
        out_shape=[jax.ShapeDtypeStruct((count, half), jnp.bfloat16)]
        + [jax.ShapeDtypeStruct((cut, feature), jnp.bfloat16) for cut in cuts]
        + [jax.ShapeDtypeStruct(w.shape, w.dtype) for w in (w_gate, w_up, w_down)],
        in_specs=[whole] * 2 + [pl.BlockSpec(memory_space=pl.ANY)] * 3,
        out_specs=[whole] * (len(cuts) + 4),
        scratch_shapes=[
            pltpu.VMEM((2 * count, feature), jnp.bfloat16),
            pltpu.VMEM((2 * count, half), jnp.bfloat16),
            pltpu.SemaphoreType.DMA((copies,)),
        ],
        compiler_params=pltpu.CompilerParams(vmem_limit_bytes=FIRST_BYTES),
        cost_estimate=pl.CostEstimate(
            flops=10 * count * feature * half,
            bytes_accessed=6 * feature * half,
            transcendentals=2 * count * half,
        ),
        name="first",
    )(own, other, w_gate, w_up, w_down)


def expert_of(own, other, w_gate, w_up, w_down, picks, cuts, after=()):
    count = own.shape[0]
    _, feature, half = w_gate.shape
    return pl.pallas_call(
        functools.partial(expert_kernel, picks, len(after)),
        out_shape=[jax.ShapeDtypeStruct((count, half), jnp.bfloat16)]
        + [jax.ShapeDtypeStruct((cut, feature), jnp.bfloat16) for cut in cuts],
        in_specs=[whole] * 5 + [pl.BlockSpec(memory_space=pl.ANY)] * len(after),
        out_specs=[whole] * (len(cuts) + 1),
        scratch_shapes=[
            pltpu.VMEM((2 * count, feature), jnp.bfloat16),
            pltpu.VMEM((2 * count, half), jnp.bfloat16),
        ],
        compiler_params=pltpu.CompilerParams(vmem_limit_bytes=LARGE_BYTES),
        cost_estimate=pl.CostEstimate(
            flops=10 * count * feature * half,
            bytes_accessed=2 * count * feature,
            transcendentals=2 * count * half,
        ),
        name="expert",
    )(own, other, w_gate, w_up, w_down, *after)


def sums_kernel(parts, cuts, hidden, w_down, *refs):
    arrived, outs = refs[:parts], refs[len(refs) - len(cuts) :]
    feature = w_down.shape[2]
    for column in range(0, feature, 2 * TILE):
        span = slice(column, column + 2 * TILE)
        part = jnp.dot(hidden[...], w_down[0, :, span], preferred_element_type=jnp.float32)
        other = jnp.concatenate([term[:, span] for term in arrived], axis=0)
        part = (part + other.astype(jnp.float32)).astype(jnp.bfloat16)
        top = 0
        for cut, out in zip(cuts, outs):
            out[:, span] = part[top : top + cut, :]
            top += cut


def sums_of(hidden, w_down, arrived, cuts, after=()):
    count, half = hidden.shape
    feature = w_down.shape[2]
    return pl.pallas_call(
        functools.partial(sums_kernel, len(arrived), cuts),
        out_shape=[jax.ShapeDtypeStruct((cut, feature), jnp.bfloat16) for cut in cuts],
        in_specs=[whole] * (2 + len(arrived)) + [pl.BlockSpec(memory_space=pl.ANY)] * len(after),
        out_specs=[whole] * len(cuts),
        compiler_params=pltpu.CompilerParams(vmem_limit_bytes=SMALL_BYTES),
        cost_estimate=pl.CostEstimate(
            flops=2 * count * feature * half,
            bytes_accessed=2 * count * feature,
            transcendentals=0,
        ),
        name="sums",
    )(hidden, w_down, *arrived, *after)


def mix_large(packed, weights, picks, steps):
    w_gate, w_up, w_down = weights
    z_near, z_far, x_steps, y_steps, core = steps
    near = spread(packed, z_near)
    far = spread(swap(packed, z_far), z_near)
    near_x, near_y = others(near, x_steps), others(near, y_steps)
    far_x, far_y = others(far, x_steps), others(far, y_steps)
    near_xy, far_xy = others(near_x, y_steps), others(far_y, x_steps)
    early = [near, near_x, near_y, far, far_x, far_y]
    late = [near_xy, far_xy]
    early_cuts = [group.shape[0] for group in early]
    late_cuts = [group.shape[0] for group in late]
    early_own, late_own = jnp.concatenate(early, axis=0), jnp.concatenate(late, axis=0)
    early_other, late_other = swap(early_own, core), swap(late_own, core)
    early_h, early_h_other = hidden_of(early_own, early_other, w_gate, w_up, picks)
    late_h, late_h_other = hidden_of(late_own, late_other, w_gate, w_up, picks)
    (late_out,) = down_of(late_h_other, w_down, [late_h_other.shape[0]])
    late_in = swap(late_out, core)
    (early_out,) = down_of(early_h_other, w_down, [early_h_other.shape[0]])
    early_in = swap(early_out, core)
    near_xy, far_xy = down_of(late_h, w_down, late_cuts, late_in)
    near, near_x, near_y, far, far_x, far_y = down_of(early_h, w_down, early_cuts, early_in)
    rows, count = near.shape[0], packed.shape[0]
    near_x = add_up(near_x, give_back(near_xy, y_steps, near_x.shape[0]))
    far_y = add_up(far_y, give_back(far_xy, x_steps, far_y.shape[0]))
    far = add_up(far, give_back(far_x, x_steps, rows) + give_back(far_y, y_steps, rows))
    near = add_up(near, give_back(near_y, y_steps, rows) + give_back(near_x, x_steps, rows))
    far = add_up(far[:count], give_back(far[count:], z_near, count))
    return add_up(near[:count], give_back(near[count:], z_near, count) + [swap(far, z_far)])


def mix_small(packed, weights, picks, steps, attention):
    z_near, z_far, x, y, core = steps
    n = packed.shape[0]

    def rows_of(*segments):
        return [(count, [(index, start)]) for index, start, count in segments]

    from_near = swap(packed, z_near)
    from_far = swap(packed, z_far)
    (near,) = combine([packed, from_near], [rows_of((0, 0, n), (1, 0, n))])
    near_x, near_y = swap(near, x), swap(near, y)
    from_both = swap(from_far, z_near)
    first_own, far, way_x, way_y = combine(
        [near, near_x, near_y, from_far, from_both],
        [
            rows_of((0, 0, 2 * n), (1, 0, 2 * n), (2, 0, 2 * n), (3, 0, n), (4, 0, n)),
            rows_of((3, 0, n), (4, 0, n)),
            rows_of((3, 0, n), (4, 0, n), (2, n, n)),
            rows_of((3, 0, n), (4, 0, n), (1, 0, n)),
        ],
    )
    first_other = swap(first_own, core)
    far_xy, far_x, far_y = across(far, x, y), swap(way_x, x), swap(way_y, y)
    first_h, first_out, *weights = first_of(first_own, first_other, *weights, picks, [8 * n])
    w_down = weights[2]
    first_in = swap(first_out, core)
    context, done = attention([first_out])
    (second_own,) = combine(
        [far_x, far_y, far_xy],
        [rows_of((0, 0, 2 * n), (1, 0, 2 * n), (2, 0, 2 * n), (1, 2 * n, n), (0, 2 * n, n))],
        [done],
    )
    second_other = swap(second_own, core)
    near, near_x, near_y, far_sum, both_sum = sums_of(
        first_h, w_down, [first_in], [2 * n] * 3 + [n] * 2
    )
    to_near = [swap(near_x, x), swap(near_y, y)]
    second_h, *second_out = expert_of(
        second_own, second_other, *weights, picks, [8 * n], [near]
    )
    second_in = [swap(part, core) for part in second_out]

    def all_of(terms, start, count=n):
        return [(count, [(index, start) for index in range(terms)])]

    (near,) = combine([near, *to_near], [all_of(3, 0, 2 * n)], flops=NEAR_FLOPS)
    far_x, both_x, far_y, both_y, far_xy, both_xy, near_xy = sums_of(
        second_h, w_down, second_in, [n] * 6 + [2 * n], [near]
    )

    to_both = [across(both_xy, x, y), swap(both_x, x), swap(both_y, y)]
    to_far = [across(far_xy, x, y), swap(far_x, x), swap(far_y, y)]
    (both_sum,) = combine([both_sum, *to_both], [all_of(4, 0)])
    to_near = across(near_xy, x, y)
    (far_sum,) = combine([far_sum, *to_far], [all_of(4, 0)], [both_sum], flops=FAR_FLOPS)
    from_both = across(both_sum, z_far, z_near)
    own_sum, near_sum = combine(
        [near, to_near, from_both], [all_of(3, 0), all_of(2, n)], [far_sum]
    )
    (mixed,) = combine(
        [own_sum, swap(far_sum, z_far), swap(near_sum, z_near)], [all_of(3, 0)]
    )
    return mixed, context


def per_device(queries, cache, lengths, live_rows, tokens, ids, gates, w_gate, w_up, w_down):
    picks = ids.shape[1]
    grp_bits = bits_of(lax.axis_size("grp"))
    ep_bits = bits_of(lax.axis_size("ep"))
    core = ("grp", 1)
    z_near = [("grp", bit) for bit in reversed(grp_bits[1:-1])]
    z_far = ("grp", grp_bits[-1])
    x_steps = [("ep", bit) for bit in ep_bits[: len(ep_bits) // 2]]
    y_steps = [("ep", bit) for bit in ep_bits[len(ep_bits) // 2 :]]

    packed = pack(tokens, ids, gates)
    weights = (w_gate, w_up, w_down)
    if len(z_near) == len(x_steps) == len(y_steps) == 1:
        steps = (z_near[0], z_far, x_steps[0], y_steps[0], core)
        attention = functools.partial(attend, queries, cache, lengths, live_rows)
        mixed, context = mix_small(packed, weights, picks, steps, attention)
    else:
        steps = (z_near, z_far, x_steps, y_steps, core)
        mixed = mix_large(packed, weights, picks, steps)
        context, _ = attend(queries, cache, lengths, live_rows)
    return (context, mixed)


def solution(mesh):
    rows3 = P(AXES, None, None)
    rows2 = P(AXES, None)
    rows1 = P(AXES)
    return jax.shard_map(
        per_device,
        mesh=mesh,
        in_specs=(rows3, rows3, rows1, rows1, rows2, rows2, rows2, rows3, rows3, rows3),
        out_specs=(rows3, rows2),
        check_vma=False,
    )
```

```python
import functools

import jax
import jax.numpy as jnp
from jax import lax
from jax.experimental import pallas as pl
from jax.experimental.pallas import tpu as pltpu
from jax.sharding import PartitionSpec as P

LAT = 512
AXES = ("grp", "ep")
EXTRA = 128
BLOCKS = 4
TILE = 256
WIDE = 512
NEAR_FLOPS = 16 * 10**9
FAR_FLOPS = 4 * 10**9
VMEM_BYTES = 48 * 1024 * 1024
LARGE_BYTES = 16 * 1024 * 1024
SMALL_BYTES = 8 * 1024 * 1024
FIRST_BYTES = 39 * 1024 * 1024
whole = pl.BlockSpec(memory_space=pltpu.VMEM)

score_scale = 192.0 ** (-0.5)
neg_large = -1e30


def attend_kernel(lengths, live_rows, queries, channels, *refs):
    out, done = refs[-2:]
    count, heads, _ = queries.shape
    positions = lax.broadcasted_iota(jnp.int32, (heads, channels.shape[2]), 1)
    for request in range(count):
        scores = jnp.dot(
            queries[request], channels[request], preferred_element_type=jnp.float32
        )
        inside = positions < lengths[request]
        masked = jnp.where(inside, scores * score_scale, neg_large)
        highest = jnp.max(masked, axis=1, keepdims=True)
        powers = jnp.where(inside, jnp.exp(masked - highest), 0.0)
        totals = jnp.sum(powers, axis=1, keepdims=True)
        weights = (powers / totals).astype(jnp.bfloat16)
        context = lax.dot_general(
            weights,
            channels[request, :LAT, :],
            (((1,), (1,)), ((), ())),
            preferred_element_type=jnp.float32,
        )
        out[request] = jnp.where(request < live_rows[0], context, 0.0).astype(jnp.bfloat16)
    done[...] = jnp.zeros_like(done)


def attend(queries, cache, lengths, live_rows, after=()):
    count, heads, width = queries.shape
    positions = cache.shape[1]
    return pl.pallas_call(
        attend_kernel,
        out_shape=[
            jax.ShapeDtypeStruct((count, heads, LAT), jnp.bfloat16),
            jax.ShapeDtypeStruct((8, 128), jnp.float32),
        ],
        in_specs=[pl.BlockSpec(memory_space=pltpu.SMEM)] * 2
        + [whole] * 2
        + [pl.BlockSpec(memory_space=pl.ANY)] * len(after),
        out_specs=[whole] * 2,
        compiler_params=pltpu.CompilerParams(vmem_limit_bytes=SMALL_BYTES),
        cost_estimate=pl.CostEstimate(
            flops=4 * count * heads * width * positions,
            bytes_accessed=2 * count * positions * width,
            transcendentals=count * heads * positions,
        ),
        name="attend",
    )(lengths, live_rows, queries, jnp.swapaxes(cache, 1, 2), *after)


def bits_of(count):
    return [1 << i for i in range(count.bit_length() - 1)]


def swap(value, step):
    axis, bit = step
    size = lax.axis_size(axis)
    return lax.ppermute(value, axis, [(i, i ^ bit) for i in range(size)])


def across(value, first, second):
    axis = first[0]
    size = lax.axis_size(axis)
    return lax.ppermute(value, axis, [(i, i ^ first[1] ^ second[1]) for i in range(size)])


def spread(value, steps):
    for step in steps:
        value = jnp.concatenate([value, swap(value, step)], axis=0)
    return value


def others(value, steps):
    if len(steps) == 1:
        return swap(value, steps[0])
    return spread(value, steps)[value.shape[0] :]


def give_back(rest, steps, rows):
    terms = []
    for step in reversed(steps):
        keep = (rest.shape[0] + rows) // 2 - rows
        arrived = swap(rest[keep:], step)
        terms.append(arrived[:rows])
        if keep:
            rest = add_up(rest[:keep], [arrived[rows:]])
    return terms


def add_up(own, terms):
    total = own.astype(jnp.float32)
    for term in terms:
        total = total + term.astype(jnp.float32)
    return total.astype(jnp.bfloat16)


def pack_kernel(tokens, chosen, out):
    feature = tokens.shape[1]
    picks = chosen.shape[0] // 2
    gates = chosen[picks:, :]
    high = gates.astype(jnp.bfloat16).astype(jnp.float32)
    stacked = jnp.concatenate([chosen[:picks, :], high, gates - high], axis=0)
    stacked = stacked.astype(jnp.bfloat16)
    row = lax.broadcasted_iota(jnp.int32, (stacked.shape[0], EXTRA), 0)
    column = lax.broadcasted_iota(jnp.int32, (stacked.shape[0], EXTRA), 1)
    place = jnp.where(row == column, 1.0, 0.0).astype(jnp.bfloat16)
    extra = lax.dot_general(
        stacked, place, (((0,), (0,)), ((), ())), preferred_element_type=jnp.float32
    )
    out[:, :feature] = tokens[...]
    out[:, feature:] = extra.astype(jnp.bfloat16)


def pack(tokens, ids, gates):
    picks = ids.shape[1]
    chosen = lax.pad(ids.T, 0, ((0, picks, 0), (0, 0, 0))).astype(jnp.float32)
    chosen = chosen + lax.pad(gates.T, 0.0, ((picks, 0, 0), (0, 0, 0)))
    return pl.pallas_call(
        pack_kernel,
        out_shape=jax.ShapeDtypeStruct((tokens.shape[0], tokens.shape[1] + EXTRA), jnp.bfloat16),
        in_specs=[whole] * 2,
        out_specs=whole,
        compiler_params=pltpu.CompilerParams(vmem_limit_bytes=SMALL_BYTES),
        name="pack",
    )(tokens, chosen)


def expert_index():
    return (lax.axis_index("grp") * lax.axis_size("ep") + lax.axis_index("ep")) // 2


def hidden_kernel(picks, own, other, extra_own, extra_other, w_gate, w_up, h_own, h_other, gate_sum, up_sum):
    step = pl.program_id(0)
    rows = jnp.concatenate([own[...], other[...]], axis=0)
    gate_part = jnp.dot(rows, w_gate[0], preferred_element_type=jnp.float32)
    up_part = jnp.dot(rows, w_up[0], preferred_element_type=jnp.float32)

    @pl.when(step == 0)
    def _():
        gate_sum[...] = gate_part
        up_sum[...] = up_part

    @pl.when(step > 0)
    def _():
        gate_sum[...] += gate_part
        up_sum[...] += up_part

    @pl.when(step == pl.num_programs(0) - 1)
    def _():
        count = own.shape[0]
        wanted = expert_index().astype(jnp.float32)
        for extra, out, at in ((extra_own, h_own, 0), (extra_other, h_other, count)):
            columns = extra[...].astype(jnp.float32)
            value = columns[:, picks : 2 * picks] + columns[:, 2 * picks : 3 * picks]
            share = jnp.sum(
                jnp.where(columns[:, :picks] == wanted, value, 0.0), axis=1, keepdims=True
            )
            gate_all = gate_sum[at : at + count, :]
            up_all = up_sum[at : at + count, :]
            hidden = gate_all / (1.0 + jnp.exp(-gate_all)) * up_all
            out[...] = (hidden * share).astype(jnp.bfloat16)


def hidden_of(own, other, w_gate, w_up, picks):
    count, width = own.shape
    _, feature, half = w_gate.shape
    depth = feature // BLOCKS
    rows_spec = pl.BlockSpec((count, depth), lambda k: (0, k))
    extra_spec = pl.BlockSpec((count, EXTRA), lambda k: (0, feature // EXTRA))
    weight_spec = pl.BlockSpec((1, depth, half), lambda k: (0, k, 0))
    out_spec = pl.BlockSpec((count, half), lambda k: (0, 0))
    return pl.pallas_call(
        functools.partial(hidden_kernel, picks),
        grid=(BLOCKS,),
        out_shape=[jax.ShapeDtypeStruct((count, half), jnp.bfloat16)] * 2,
        in_specs=[rows_spec] * 2 + [extra_spec] * 2 + [weight_spec] * 2,
        out_specs=[out_spec] * 2,
        scratch_shapes=[pltpu.VMEM((2 * count, half), jnp.float32)] * 2,
        compiler_params=pltpu.CompilerParams(vmem_limit_bytes=VMEM_BYTES),
        cost_estimate=pl.CostEstimate(
            flops=8 * count * feature * half,
            bytes_accessed=4 * feature * half + 4 * count * width,
            transcendentals=2 * count * half,
        ),
        name="hidden",
    )(own, other, own, other, w_gate, w_up)


def down_kernel(cuts, hidden, w_down, *refs):
    part = jnp.dot(hidden[...], w_down[0], preferred_element_type=jnp.float32)
    if len(refs) > len(cuts):
        part = part + refs[0][...].astype(jnp.float32)
        refs = refs[1:]
    at = 0
    for cut, out in zip(cuts, refs):
        out[...] = part[at : at + cut, :].astype(jnp.bfloat16)
        at += cut


def down_of(hidden, w_down, cuts, arrived=None):
    count, half = hidden.shape
    feature = w_down.shape[2]
    wide = feature // BLOCKS
    operands = [hidden, w_down]
    in_specs = [
        pl.BlockSpec((count, half), lambda n: (0, 0)),
        pl.BlockSpec((1, half, wide), lambda n: (0, 0, n)),
    ]
    if arrived is not None:
        operands.append(arrived)
        in_specs.append(pl.BlockSpec((count, wide), lambda n: (0, n)))
    return pl.pallas_call(
        functools.partial(down_kernel, cuts),
        grid=(BLOCKS,),
        out_shape=[jax.ShapeDtypeStruct((cut, feature), jnp.bfloat16) for cut in cuts],
        in_specs=in_specs,
        out_specs=[pl.BlockSpec((cut, wide), lambda n: (0, n)) for cut in cuts],
        compiler_params=pltpu.CompilerParams(vmem_limit_bytes=VMEM_BYTES),
        cost_estimate=pl.CostEstimate(
            flops=2 * count * feature * half,
            bytes_accessed=2 * feature * half + 4 * count * feature,
            transcendentals=0,
        ),
        name="down",
    )(*operands)


def combine_kernel(count, plans, *refs):
    outs = refs[len(refs) - len(plans) :]
    width = outs[0].shape[1]
    for plan, out in zip(plans, outs):
        at = 0
        for rows, terms in plan:
            if len(terms) == 1:
                index, start = terms[0]
                out[at : at + rows, :] = refs[index][start : start + rows, :]
            else:
                for left in range(0, width, WIDE):
                    span = slice(left, left + WIDE)
                    total = sum(
                        refs[index][start : start + rows, span].astype(jnp.float32)
                        for index, start in terms
                    )
                    out[at : at + rows, span] = total.astype(out.dtype)
            at += rows


def combine(inputs, plans, after=(), flops=0):
    width = inputs[0].shape[1]
    return pl.pallas_call(
        functools.partial(combine_kernel, len(inputs), plans),
        out_shape=[
            jax.ShapeDtypeStruct((sum(rows for rows, _ in plan), width), jnp.bfloat16)
            for plan in plans
        ],
        in_specs=[whole] * len(inputs) + [pl.BlockSpec(memory_space=pl.ANY)] * len(after),
        out_specs=[whole] * len(plans),
        compiler_params=pltpu.CompilerParams(vmem_limit_bytes=SMALL_BYTES),
        cost_estimate=pl.CostEstimate(
            flops=flops, bytes_accessed=4 * width * inputs[0].shape[0], transcendentals=0
        ),
        name="combine",
    )(*inputs, *after)


def expert_kernel(picks, after, own, other, w_gate, w_up, w_down, *refs):
    *outs, rows, hidden = refs[after:]
    expert_body(picks, own, other, w_gate, w_up, w_down, outs, rows, hidden)


def expert_body(
    picks, own, other, w_gate, w_up, w_down, outs, rows, hidden, ready=lambda number: None
):
    h_own, *outs = outs
    count, feature, half = own.shape[0], w_gate.shape[1], w_gate.shape[2]
    wanted = expert_index().astype(jnp.float32)
    shares = []
    for ref, at in ((own, 0), (other, count)):
        rows[at : at + count, :] = ref[:, :feature]
        columns = ref[:, feature:].astype(jnp.float32)
        value = columns[:, picks : 2 * picks] + columns[:, 2 * picks : 3 * picks]
        named = columns[:, :picks] == wanted
        shares.append(jnp.sum(jnp.where(named, value, 0.0), axis=1, keepdims=True))
    share = jnp.concatenate(shares, axis=0)
    for at in range(0, half, TILE):
        ready(at // TILE * 2)
        gate_part = jnp.dot(
            rows[...], w_gate[0, :, at : at + TILE], preferred_element_type=jnp.float32
        )
        ready(at // TILE * 2 + 1)
        up_part = jnp.dot(
            rows[...], w_up[0, :, at : at + TILE], preferred_element_type=jnp.float32
        )
        product = gate_part / (1.0 + jnp.exp(-gate_part)) * up_part * share
        hidden[:, at : at + TILE] = product.astype(jnp.bfloat16)
    h_own[...] = hidden[:count, :]
    wide = feature // BLOCKS
    for at in range(0, feature, wide):
        ready(half // TILE * 2 + at // wide)
        part = jnp.dot(
            hidden[count:, :], w_down[0, :, at : at + wide], preferred_element_type=jnp.float32
        ).astype(jnp.bfloat16)
        top = 0
        for out in outs:
            out[:, at : at + wide] = part[top : top + out.shape[0], :]
            top += out.shape[0]


def first_kernel(picks, own, other, gate_far, up_far, down_far, *refs):
    outs, (w_gate, w_up, w_down, rows, hidden, sems) = refs[:-6], refs[-6:]
    feature, half = w_gate.shape[1], w_gate.shape[2]
    depth = feature // BLOCKS
    groups = []

    def begin(pairs):
        copies = []
        for source, target, index in pairs:
            at = len(copies) + sum(len(group) for group in groups)
            copies.append(pltpu.make_async_copy(source.at[index], target.at[index], sems.at[at]))
        for copy in copies:
            copy.start()
        groups.append(copies)

    for left in range(0, half, TILE):
        for source, target in ((gate_far, w_gate), (up_far, w_up)):
            begin(
                (source, target, (0, pl.ds(top, depth), pl.ds(left, TILE)))
                for top in range(0, feature, depth)
            )
    for left in range(0, feature, feature // BLOCKS):
        begin([(down_far, w_down, (0, slice(None), pl.ds(left, feature // BLOCKS)))])

    def ready(number):
        for copy in groups[number]:
            copy.wait()

    expert_body(picks, own, other, w_gate, w_up, w_down, outs, rows, hidden, ready)


def first_of(own, other, w_gate, w_up, w_down, picks, cuts):
    count = own.shape[0]
    _, feature, half = w_gate.shape
    copies = 2 * (half // TILE) * BLOCKS + BLOCKS
    return pl.pallas_call(
        functools.partial(first_kernel, picks),
        out_shape=[jax.ShapeDtypeStruct((count, half), jnp.bfloat16)]
        + [jax.ShapeDtypeStruct((cut, feature), jnp.bfloat16) for cut in cuts]
        + [jax.ShapeDtypeStruct(w.shape, w.dtype) for w in (w_gate, w_up, w_down)],
        in_specs=[whole] * 2 + [pl.BlockSpec(memory_space=pl.ANY)] * 3,
        out_specs=[whole] * (len(cuts) + 4),
        scratch_shapes=[
            pltpu.VMEM((2 * count, feature), jnp.bfloat16),
            pltpu.VMEM((2 * count, half), jnp.bfloat16),
            pltpu.SemaphoreType.DMA((copies,)),
        ],
        compiler_params=pltpu.CompilerParams(vmem_limit_bytes=FIRST_BYTES),
        cost_estimate=pl.CostEstimate(
            flops=10 * count * feature * half,
            bytes_accessed=6 * feature * half,
            transcendentals=2 * count * half,
        ),
        name="first",
    )(own, other, w_gate, w_up, w_down)


def expert_of(own, other, w_gate, w_up, w_down, picks, cuts, after=()):
    count = own.shape[0]
    _, feature, half = w_gate.shape
    return pl.pallas_call(
        functools.partial(expert_kernel, picks, len(after)),
        out_shape=[jax.ShapeDtypeStruct((count, half), jnp.bfloat16)]
        + [jax.ShapeDtypeStruct((cut, feature), jnp.bfloat16) for cut in cuts],
        in_specs=[whole] * 5 + [pl.BlockSpec(memory_space=pl.ANY)] * len(after),
        out_specs=[whole] * (len(cuts) + 1),
        scratch_shapes=[
            pltpu.VMEM((2 * count, feature), jnp.bfloat16),
            pltpu.VMEM((2 * count, half), jnp.bfloat16),
        ],
        compiler_params=pltpu.CompilerParams(vmem_limit_bytes=LARGE_BYTES),
        cost_estimate=pl.CostEstimate(
            flops=10 * count * feature * half,
            bytes_accessed=2 * count * feature,
            transcendentals=2 * count * half,
        ),
        name="expert",
    )(own, other, w_gate, w_up, w_down, *after)


def sums_kernel(parts, cuts, hidden, w_down, *refs):
    arrived, outs = refs[:parts], refs[len(refs) - len(cuts) :]
    feature = w_down.shape[2]
    for column in range(0, feature, 2 * TILE):
        span = slice(column, column + 2 * TILE)
        part = jnp.dot(hidden[...], w_down[0, :, span], preferred_element_type=jnp.float32)
        other = jnp.concatenate([term[:, span] for term in arrived], axis=0)
        part = (part + other.astype(jnp.float32)).astype(jnp.bfloat16)
        top = 0
        for cut, out in zip(cuts, outs):
            out[:, span] = part[top : top + cut, :]
            top += cut


def sums_of(hidden, w_down, arrived, cuts, after=()):
    count, half = hidden.shape
    feature = w_down.shape[2]
    return pl.pallas_call(
        functools.partial(sums_kernel, len(arrived), cuts),
        out_shape=[jax.ShapeDtypeStruct((cut, feature), jnp.bfloat16) for cut in cuts],
        in_specs=[whole] * (2 + len(arrived)) + [pl.BlockSpec(memory_space=pl.ANY)] * len(after),
        out_specs=[whole] * len(cuts),
        compiler_params=pltpu.CompilerParams(vmem_limit_bytes=SMALL_BYTES),
        cost_estimate=pl.CostEstimate(
            flops=2 * count * feature * half,
            bytes_accessed=2 * count * feature,
            transcendentals=0,
        ),
        name="sums",
    )(hidden, w_down, *arrived, *after)


def mix_large(packed, weights, picks, steps):
    w_gate, w_up, w_down = weights
    z_near, z_far, x_steps, y_steps, core = steps
    near = spread(packed, z_near)
    far = spread(swap(packed, z_far), z_near)
    near_x, near_y = others(near, x_steps), others(near, y_steps)
    far_x, far_y = others(far, x_steps), others(far, y_steps)
    near_xy, far_xy = others(near_x, y_steps), others(far_y, x_steps)
    early = [near, near_x, near_y, far, far_x, far_y]
    late = [near_xy, far_xy]
    early_cuts = [group.shape[0] for group in early]
    late_cuts = [group.shape[0] for group in late]
    early_own, late_own = jnp.concatenate(early, axis=0), jnp.concatenate(late, axis=0)
    early_other, late_other = swap(early_own, core), swap(late_own, core)
    early_h, early_h_other = hidden_of(early_own, early_other, w_gate, w_up, picks)
    late_h, late_h_other = hidden_of(late_own, late_other, w_gate, w_up, picks)
    (late_out,) = down_of(late_h_other, w_down, [late_h_other.shape[0]])
    late_in = swap(late_out, core)
    (early_out,) = down_of(early_h_other, w_down, [early_h_other.shape[0]])
    early_in = swap(early_out, core)
    near_xy, far_xy = down_of(late_h, w_down, late_cuts, late_in)
    near, near_x, near_y, far, far_x, far_y = down_of(early_h, w_down, early_cuts, early_in)
    rows, count = near.shape[0], packed.shape[0]
    near_x = add_up(near_x, give_back(near_xy, y_steps, near_x.shape[0]))
    far_y = add_up(far_y, give_back(far_xy, x_steps, far_y.shape[0]))
    far = add_up(far, give_back(far_x, x_steps, rows) + give_back(far_y, y_steps, rows))
    near = add_up(near, give_back(near_y, y_steps, rows) + give_back(near_x, x_steps, rows))
    far = add_up(far[:count], give_back(far[count:], z_near, count))
    return add_up(near[:count], give_back(near[count:], z_near, count) + [swap(far, z_far)])


def mix_small(packed, weights, picks, steps, attention):
    z_near, z_far, x, y, core = steps
    n = packed.shape[0]

    def rows_of(*segments):
        return [(count, [(index, start)]) for index, start, count in segments]

    from_near = swap(packed, z_near)
    from_far = swap(packed, z_far)
    (near,) = combine([packed, from_near], [rows_of((0, 0, n), (1, 0, n))])
    near_x, near_y = swap(near, x), swap(near, y)
    from_both = swap(from_far, z_near)
    first_own, far, way_x, way_y = combine(
        [near, near_x, near_y, from_far, from_both],
        [
            rows_of((0, 0, 2 * n), (1, 0, 2 * n), (2, 0, 2 * n), (3, 0, n), (4, 0, n)),
            rows_of((3, 0, n), (4, 0, n)),
            rows_of((3, 0, n), (4, 0, n), (2, n, n)),
            rows_of((3, 0, n), (4, 0, n), (1, 0, n)),
        ],
    )
    first_other = swap(first_own, core)
    far_xy, far_x, far_y = across(far, x, y), swap(way_x, x), swap(way_y, y)
    first_h, first_out, *weights = first_of(first_own, first_other, *weights, picks, [8 * n])
    w_down = weights[2]
    first_in = swap(first_out, core)
    context, done = attention([first_out])
    (second_own,) = combine(
        [far_x, far_y, far_xy],
        [rows_of((0, 0, 2 * n), (1, 0, 2 * n), (2, 0, 2 * n), (1, 2 * n, n), (0, 2 * n, n))],
        [done],
    )
    second_other = swap(second_own, core)
    near, near_x, near_y, far_sum, both_sum = sums_of(
        first_h, w_down, [first_in], [2 * n] * 3 + [n] * 2
    )
    to_near = [swap(near_x, x), swap(near_y, y)]
    second_h, *second_out = expert_of(
        second_own, second_other, *weights, picks, [8 * n], [near]
    )
    second_in = [swap(part, core) for part in second_out]

    def all_of(terms, start, count=n):
        return [(count, [(index, start) for index in range(terms)])]

    (near,) = combine([near, *to_near], [all_of(3, 0, 2 * n)], flops=NEAR_FLOPS)
    far_x, both_x, far_y, both_y, far_xy, both_xy, near_xy = sums_of(
        second_h, w_down, second_in, [n] * 6 + [2 * n], [near]
    )

    to_both = [across(both_xy, x, y), swap(both_x, x), swap(both_y, y)]
    to_far = [across(far_xy, x, y), swap(far_x, x), swap(far_y, y)]
    (both_sum,) = combine([both_sum, *to_both], [all_of(4, 0)])
    to_near = across(near_xy, x, y)
    (far_sum,) = combine([far_sum, *to_far], [all_of(4, 0)], [both_sum], flops=FAR_FLOPS)
    from_both = across(both_sum, z_far, z_near)
    own_sum, near_sum = combine(
        [near, to_near], [all_of(2, 0), all_of(2, n)], [far_sum]
    )
    (mixed,) = combine(
        [own_sum, from_both, swap(far_sum, z_far), swap(near_sum, z_near)], [all_of(4, 0)]
    )
    return mixed, context


def per_device(queries, cache, lengths, live_rows, tokens, ids, gates, w_gate, w_up, w_down):
    picks = ids.shape[1]
    grp_bits = bits_of(lax.axis_size("grp"))
    ep_bits = bits_of(lax.axis_size("ep"))
    core = ("grp", 1)
    z_near = [("grp", bit) for bit in reversed(grp_bits[1:-1])]
    z_far = ("grp", grp_bits[-1])
    x_steps = [("ep", bit) for bit in ep_bits[: len(ep_bits) // 2]]
    y_steps = [("ep", bit) for bit in ep_bits[len(ep_bits) // 2 :]]

    packed = pack(tokens, ids, gates)
    weights = (w_gate, w_up, w_down)
    if len(z_near) == len(x_steps) == len(y_steps) == 1:
        steps = (z_near[0], z_far, x_steps[0], y_steps[0], core)
        attention = functools.partial(attend, queries, cache, lengths, live_rows)
        mixed, context = mix_small(packed, weights, picks, steps, attention)
    else:
        steps = (z_near, z_far, x_steps, y_steps, core)
        mixed = mix_large(packed, weights, picks, steps)
        context, _ = attend(queries, cache, lengths, live_rows)
    return (context, mixed)


def solution(mesh):
    rows3 = P(AXES, None, None)
    rows2 = P(AXES, None)
    rows1 = P(AXES)
    return jax.shard_map(
        per_device,
        mesh=mesh,
        in_specs=(rows3, rows3, rows1, rows1, rows2, rows2, rows2, rows3, rows3, rows3),
        out_specs=(rows3, rows2),
        check_vma=False,
    )
```
